32 devices in a mesh: replica: 8 (over z, y), tensor: 4 (over x, core).
Axes of the slice: x: 2, y: 2, z: 4, core: 2. Of those that a mesh axis runs over, the one named last changes fastest.
Arguments:
- grad_q: bfloat16 [16384, 2048], P('replica', 'tensor'), may hold values from -6 to 6
- error_q: bfloat16 [16384, 2048], P('replica', 'tensor'), may hold values from -6 to 6
- qfac_q: bfloat16 [2048, 32], P('tensor'), may hold values from -0.25 to 0.25
- ginv_q: float32 [128, 32], P('tensor'), as said below
- weight_q: float32 [2048, 2048], P('replica', 'tensor'), may hold values from -6 to 6
- momentum_q: float32 [2048, 2048], P('replica', 'tensor'), may hold values from -4 to 4
- grad_o: bfloat16 [16384, 2048], P(('replica', 'tensor')), may hold values from -6 to 6
- error_o: bfloat16 [16384, 2048], P(('replica', 'tensor')), may hold values from -6 to 6
- qfac_o: bfloat16 [8192, 32], P('tensor'), may hold values from -0.125 to 0.125
- ginv_o: float32 [128, 32], P('tensor'), as said below
- weight_o: float32 [2048, 2048], P('tensor', 'replica'), may hold values from -6 to 6
- momentum_o: float32 [2048, 2048], P('tensor', 'replica'), may hold values from -4 to 4
- norm_grads: bfloat16 [8, 4, 4096], P('replica', 'tensor'), may hold values from -24 to 24
Outputs:
- error_q_new: bfloat16 [16384, 2048], P('replica', 'tensor')
- qfac_q_new: bfloat16 [2048, 32], P('tensor')
- momentum_q_new: float32 [2048, 2048], P('replica', 'tensor')
- weight_q_new: float32 [2048, 2048], P('replica', 'tensor')
- error_o_new: bfloat16 [16384, 2048], P(('replica', 'tensor'))
- qfac_o_new: bfloat16 [8192, 32], P('tensor')
- momentum_o_new: float32 [2048, 2048], P('tensor', 'replica')
- weight_o_new: float32 [2048, 2048], P('tensor', 'replica')
- norm_mean: float32 [4096], replicated
The draws below stay inside these ranges and needn't reach their ends.
Inputs may be any that keep to these rules, and one draw needn't show every extreme that they name: `ginv_q`: each block of 32 rows is an upper-triangular matrix with a positive diagonal. `ginv_o`: each block of 32 rows is an upper-triangular matrix with a positive diagonal.
All inputs are finite; a program needn't handle non-finite values.
Results may differ from the reference program's by a relative error of at most 0.0085.
Values may be sent and summed in bfloat16 or wider, within the bound.
No kernel may reach another device: no remote copies, remote signals or barrier semaphores. Data moves between devices by JAX's collectives and lax.ppermute only.
A program may use at most 64 MiB of HBM per device.

```python
import jax
import jax.numpy as jnp
from jax import lax

D = 2048
HD = 2048
RANK = 32
REPLICAS = 8
N_REPLICA = 8
N_TENSOR = 4


def gram_factor(key, row_count):
    key_diag, key_off = jax.random.split(key)
    diagonal = jnp.exp(jax.random.uniform(key_diag, (N_TENSOR, RANK), jnp.float32, jnp.log(0.7), jnp.log(1.4)))
    offdiag = 0.35 * jax.random.truncated_normal(key_off, -3.0, 3.0, (N_TENSOR, RANK, RANK), jnp.float32) / jnp.sqrt(jnp.float32(RANK))
    row_ids = jnp.arange(RANK)[:, None]
    col_ids = jnp.arange(RANK)[None, :]
    upper = (col_ids > row_ids).astype(jnp.float32)
    ident = (col_ids == row_ids).astype(jnp.float32)
    matrix = offdiag * upper[None] + diagonal[:, :, None] * ident[None]
    scale_value = 1.5 / jnp.sqrt(jnp.float32(row_count * REPLICAS))
    return (matrix * scale_value).reshape(N_TENSOR * RANK, RANK)


def draw_ginv_q(key, part):
    return gram_factor(jax.random.fold_in(key, 11), D)


def draw_ginv_o(key, part):
    return gram_factor(jax.random.fold_in(key, 23), HD // N_TENSOR)


def block_scale(stream_key, shape, cuts, smallest, largest):
    loudness = 1.0
    for dim, blocks in cuts:
        steps = jax.random.uniform(jax.random.fold_in(jax.random.fold_in(stream_key, 6), dim), (blocks,), jnp.float32, smallest / len(cuts), largest / len(cuts))
        loudness = loudness * jnp.repeat(jnp.exp(steps), shape[dim] // blocks).reshape((-1,) + (1,) * (len(shape) - 1 - dim))
    return loudness


def gaussian(stream_key, shape, spread, most, cuts=(), dtype=jnp.bfloat16):
    level = block_scale(stream_key, shape, cuts, -0.22, 0.18) if cuts else 1.0
    result = jax.random.normal(stream_key, shape, jnp.float32) * spread * level
    return jnp.minimum(jnp.maximum(result, -most), most).astype(dtype)


def setup_inputs(seed: int = 0) -> dict:
    key_list = jax.random.split(jax.random.key(seed), 14)
    return {
        "grad_q": gaussian(key_list[0], (N_REPLICA * D, HD), 1.0, 6.0, ((0, 8), (1, 4))),
        "error_q": gaussian(key_list[1], (N_REPLICA * D, HD), 0.5, 6.0, ((0, 8), (1, 4))),
        "qfac_q": gaussian(key_list[2], (HD, RANK), (HD // N_TENSOR) ** -0.5, 0.25, ((0, 4),)),
        "ginv_q": draw_ginv_q(jax.random.fold_in(key_list[13], 71), 0),
        "weight_q": gaussian(key_list[4], (D, HD), 1.0, 6.0, ((0, 8), (1, 4)), jnp.float32),
        "momentum_q": gaussian(key_list[5], (D, HD), 0.3, 4.0, ((0, 8), (1, 4)), jnp.float32),
        "grad_o": gaussian(key_list[6], (N_REPLICA * HD, D), 1.0, 6.0, ((0, 32),)),
        "error_o": gaussian(key_list[7], (N_REPLICA * HD, D), 0.5, 6.0, ((0, 32),)),
        "qfac_o": gaussian(key_list[8], (N_TENSOR * D, RANK), D ** -0.5, 0.125, ((0, 4),)),
        "ginv_o": draw_ginv_o(jax.random.fold_in(key_list[13], 71), 0),
        "weight_o": gaussian(key_list[10], (HD, D), 1.0, 6.0, ((0, 4), (1, 8)), jnp.float32),
        "momentum_o": gaussian(key_list[11], (HD, D), 0.3, 4.0, ((0, 4), (1, 8)), jnp.float32),
        "norm_grads": gaussian(key_list[12], (N_REPLICA, N_TENSOR, 2 * D), 4.0, 24.0, ((0, 8), (1, 4))),
    }


momentum_decay = 0.9
step_size = 0.5


def sum_replicas(term, mat_all):
    first = term(mat_all[0])

    def accumulate(running, matrix):
        return running + term(matrix), None

    return lax.scan(accumulate, jnp.zeros_like(first), mat_all)[0]


def compress_shard(grads, errors, qfac, ginv):
    mat_all = (grads.astype(jnp.float32) + errors.astype(jnp.float32)).astype(jnp.bfloat16)
    p_sum = sum_replicas(lambda matrix: jnp.dot(matrix, qfac, preferred_element_type=jnp.float32), mat_all)
    p_hat = jnp.dot(p_sum, ginv, precision=lax.Precision.HIGHEST).astype(jnp.bfloat16)
    q_sum = sum_replicas(lambda matrix: lax.dot_general(matrix, p_hat, (((0,), (0,)), ((), ())), preferred_element_type=jnp.float32), mat_all)
    q_new = (q_sum / N_REPLICA).astype(jnp.bfloat16)
    approx = lax.dot_general(p_hat, q_new, (((1,), (1,)), ((), ())), preferred_element_type=jnp.float32)
    err_new = (mat_all.astype(jnp.float32) - approx[None]).astype(jnp.bfloat16)
    return err_new, q_new, approx


def reference(grad_q, error_q, qfac_q, ginv_q, weight_q, momentum_q, grad_o, error_o, qfac_o, ginv_o, weight_o, momentum_o, norm_grads):
    local_width = HD // N_TENSOR
    grad_q3 = grad_q.reshape(N_REPLICA, D, HD)
    error_q3 = error_q.reshape(N_REPLICA, D, HD)
    grad_o3 = grad_o.reshape(N_REPLICA, HD, D)
    error_o3 = error_o.reshape(N_REPLICA, HD, D)
    errs_q, facs_q, apps_q = [], [], []
    errs_o, facs_o, apps_o = [], [], []
    for shard_index in range(N_TENSOR):
        low = shard_index * local_width
        gram_q = ginv_q[shard_index * RANK:(shard_index + 1) * RANK]
        gram_o = ginv_o[shard_index * RANK:(shard_index + 1) * RANK]
        err_new, q_new, approx = compress_shard(grad_q3[:, :, low:low + local_width], error_q3[:, :, low:low + local_width], qfac_q[low:low + local_width], gram_q)
        errs_q.append(err_new)
        facs_q.append(q_new)
        apps_q.append(approx)
        err_new, q_new, approx = compress_shard(grad_o3[:, low:low + local_width], error_o3[:, low:low + local_width], qfac_o[shard_index * D:(shard_index + 1) * D], gram_o)
        errs_o.append(err_new)
        facs_o.append(q_new)
        apps_o.append(approx)
    error_q_new = jnp.concatenate(errs_q, axis=2).reshape(N_REPLICA * D, HD)
    qfac_q_new = jnp.concatenate(facs_q, axis=0)
    approx_q = jnp.concatenate(apps_q, axis=1)
    error_o_new = jnp.concatenate(errs_o, axis=1).reshape(N_REPLICA * HD, D)
    qfac_o_new = jnp.concatenate(facs_o, axis=0)
    approx_o = jnp.concatenate(apps_o, axis=0)
    momentum_q_new = momentum_decay * momentum_q + approx_q
    weight_q_new = weight_q - step_size * momentum_q_new
    momentum_o_new = momentum_decay * momentum_o + approx_o
    weight_o_new = weight_o - step_size * momentum_o_new
    norm_mean = jnp.sum(norm_grads.astype(jnp.float32), axis=(0, 1)) / (N_REPLICA * N_TENSOR)
    return (error_q_new, qfac_q_new, momentum_q_new, weight_q_new, error_o_new, qfac_o_new, momentum_o_new, weight_o_new, norm_mean)
```

```python
import jax
import jax.numpy as jnp
from jax import lax
from jax.sharding import PartitionSpec as P

momentum_decay = 0.9
step_size = 0.5


def contract(left, right, left_dim, right_dim):
    return lax.dot_general(
        left, right, (((left_dim,), (right_dim,)), ((), ())), preferred_element_type=jnp.float32
    )


def shifts(count, step):
    return [(source, (source + step) % count) for source in range(count)]


def exchange(pieces, axis, count):
    me = lax.axis_index(axis)
    got = [lax.dynamic_index_in_dim(pieces, me, 0, keepdims=False)]
    for step in range(1, count):
        piece = lax.dynamic_index_in_dim(pieces, (me + step) % count, 0, keepdims=False)
        got.append(lax.ppermute(piece, axis, shifts(count, step)))
    return got


def gather(piece, axis, count):
    me = lax.axis_index(axis)
    got = [piece]
    for step in range(1, count):
        got.append(lax.ppermute(piece, axis, shifts(count, step)))
    stacked = jnp.stack(got[::-1])
    return jnp.roll(stacked, me + 1, axis=0)


def cut(factor, count):
    rank, size = factor.shape
    return factor.reshape(rank, count, size // count).transpose(1, 0, 2)


def join(pieces):
    count, rank, size = pieces.shape
    return pieces.transpose(1, 0, 2).reshape(rank, count * size)


def on_device(
    grad_q,
    error_q,
    qfac_q,
    ginv_q,
    weight_q,
    momentum_q,
    grad_o,
    error_o,
    qfac_o,
    ginv_o,
    weight_o,
    momentum_o,
    norm_grads,
):
    replicas = lax.axis_size("replica")
    tensors = lax.axis_size("tensor")
    rank = qfac_q.shape[1]
    mat_q = (grad_q.astype(jnp.float32) + error_q.astype(jnp.float32)).astype(jnp.bfloat16)
    mat_o = (grad_o.astype(jnp.float32) + error_o.astype(jnp.float32)).astype(jnp.bfloat16)
    p_q = contract(qfac_q.T, mat_q, 1, 1)
    p_o = contract(qfac_o.T, mat_o, 1, 1)
    norm = norm_grads.reshape(replicas, rank, -1)
    send = jnp.concatenate(
        [cut(p_q, replicas).astype(jnp.bfloat16), cut(p_o, replicas).astype(jnp.bfloat16), norm], axis=2
    )
    got = exchange(send, "replica", replicas)
    total = sum(part.astype(jnp.float32) for part in got)
    q_size = p_q.shape[1] // replicas
    o_size = p_o.shape[1] // replicas
    sum_q = total[:, :q_size]
    sum_o = total[:, q_size:q_size + o_size]
    sum_norm = total[:, q_size + o_size:]
    hat_q = jnp.dot(ginv_q.T, sum_q, precision=lax.Precision.HIGHEST).astype(jnp.bfloat16)
    hat_o = jnp.dot(ginv_o.T, sum_o, precision=lax.Precision.HIGHEST).astype(jnp.bfloat16)
    hats = gather(jnp.concatenate([hat_q, hat_o], axis=1), "replica", replicas)
    phat_q = join(hats[:, :, :q_size])
    phat_o = join(hats[:, :, q_size:])

    norm_parts = gather(sum_norm, "tensor", tensors)
    norm_piece = jnp.sum(norm_parts, axis=0) / (replicas * tensors)
    norm_mean = gather(norm_piece, "replica", replicas).reshape(-1)

    q_q = contract(phat_q, mat_q, 1, 0)
    q_o = contract(phat_o, mat_o, 1, 0)
    send = jnp.concatenate(
        [cut(q_q, replicas).astype(jnp.bfloat16), cut(q_o, replicas).astype(jnp.bfloat16)], axis=2
    )
    got = lax.all_to_all(send, "replica", 0, 0, tiled=True)
    total = jnp.sum(got.astype(jnp.float32), axis=0)
    piece = (total / replicas).astype(jnp.bfloat16)
    news = lax.all_to_all(
        jnp.broadcast_to(piece[None], (replicas,) + piece.shape), "replica", 0, 0, tiled=True
    )
    q_size = q_q.shape[1] // replicas
    new_q = join(news[:, :, :q_size])
    new_o = join(news[:, :, q_size:])
    approx_q = contract(phat_q, new_q, 0, 0)
    approx_o = contract(phat_o, new_o, 0, 0)
    error_q_new = (mat_q.astype(jnp.float32) - approx_q).astype(jnp.bfloat16)
    error_o_new = (mat_o.astype(jnp.float32) - approx_o).astype(jnp.bfloat16)
    replica_index = lax.axis_index("replica")
    piece_rows = weight_q.shape[0]
    piece_cols = weight_o.shape[1]
    hat_q_mine = lax.dynamic_slice_in_dim(phat_q, replica_index * piece_rows, piece_rows, 1)
    new_o_mine = lax.dynamic_slice_in_dim(new_o, replica_index * piece_cols, piece_cols, 1)
    momentum_q_new = momentum_decay * momentum_q + contract(hat_q_mine, new_q, 0, 0)
    weight_q_new = weight_q - step_size * momentum_q_new
    momentum_o_new = momentum_decay * momentum_o + contract(phat_o, new_o_mine, 0, 0)
    weight_o_new = weight_o - step_size * momentum_o_new
    return (
        error_q_new,
        new_q.T,
        momentum_q_new,
        weight_q_new,
        error_o_new,
        new_o.T,
        momentum_o_new,
        weight_o_new,
        norm_mean,
    )


def solution(mesh):
    in_specs = (
        P("replica", "tensor"),
        P("replica", "tensor"),
        P("tensor", None),
        P("tensor", None),
        P("replica", "tensor"),
        P("replica", "tensor"),
        P(("replica", "tensor"), None),
        P(("replica", "tensor"), None),
        P("tensor", None),
        P("tensor", None),
        P("tensor", "replica"),
        P("tensor", "replica"),
        P("replica", "tensor", None),
    )
    out_specs = (
        P("replica", "tensor"),
        P("tensor", None),
        P("replica", "tensor"),
        P("replica", "tensor"),
        P(("replica", "tensor"), None),
        P("tensor", None),
        P("tensor", "replica"),
        P("tensor", "replica"),
        P(),
    )
    return jax.shard_map(
        on_device, mesh=mesh, in_specs=in_specs, out_specs=out_specs, check_vma=False
    )
```

```python
import functools

import jax
import jax.numpy as jnp
from jax import lax
from jax.experimental import pallas as pl
from jax.experimental.pallas import tpu as pltpu
from jax.sharding import PartitionSpec as P

momentum_decay = 0.9
step_size = 0.5
norm_lanes = 64
low_row = 8
mib = 1024 * 1024

whole = pl.BlockSpec(memory_space=pltpu.VMEM)
in_place = pl.BlockSpec(memory_space=pl.ANY)


def dot(left, right, left_dim, right_dim, precision=None):
    return lax.dot_general(
        left,
        right,
        (((left_dim,), (right_dim,)), ((), ())),
        precision=precision,
        preferred_element_type=jnp.float32,
    )


def padded(width):
    return -(-width // 128) * 128


def project_kernel(
    chunks, fac_q, fac_o, norm, grad_q, error_q, grad_o, error_o, send, mat_q, mat_o,
    grad_q_v, error_q_v, grad_o_v, error_o_v, p_q, p_o, sems
):
    rows_q = grad_q.shape[0] // chunks
    rows_o = grad_o.shape[0] // chunks
    copies = []
    for chunk in range(chunks):
        part_q = pl.ds(chunk * rows_q, rows_q)
        part_o = pl.ds(chunk * rows_o, rows_o)
        quad = (
            (grad_q, grad_q_v, part_q),
            (error_q, error_q_v, part_q),
            (grad_o, grad_o_v, part_o),
            (error_o, error_o_v, part_o),
        )
        group = []
        for slot, (source, target, part) in enumerate(quad):
            copy = pltpu.make_async_copy(source.at[part], target.at[part], sems.at[chunk, slot])
            copy.start()
            group.append(copy)
        copies.append(group)
    for chunk in range(chunks):
        part_q = pl.ds(chunk * rows_q, rows_q)
        part_o = pl.ds(chunk * rows_o, rows_o)
        copies[chunk][0].wait()
        copies[chunk][1].wait()
        block = (
            grad_q_v[part_q].astype(jnp.float32) + error_q_v[part_q].astype(jnp.float32)
        ).astype(jnp.bfloat16)
        mat_q[part_q] = block
        p_q[:, part_q] = dot(fac_q[...], block, 1, 1)
        copies[chunk][2].wait()
        copies[chunk][3].wait()
        block = (
            grad_o_v[part_o].astype(jnp.float32) + error_o_v[part_o].astype(jnp.float32)
        ).astype(jnp.bfloat16)
        mat_o[part_o] = block
        p_o[:, part_o] = dot(fac_o[...], block, 1, 1)
    count = send.shape[0]
    size_q = p_q.shape[1] // count
    size_o = p_o.shape[1] // count
    for slot in range(count):
        send[slot, :, :size_q] = p_q[:, slot * size_q:(slot + 1) * size_q].astype(jnp.bfloat16)
        send[slot, :, size_q:size_q + size_o] = p_o[
            :, slot * size_o:(slot + 1) * size_o
        ].astype(jnp.bfloat16)
        send[slot, :, size_q + size_o:size_q + size_o + norm_lanes] = norm[slot]


def project(grad_q, error_q, grad_o, error_o, fac_q, fac_o, norm):
    rank = fac_q.shape[0]
    count = norm.shape[0]
    width = padded((grad_q.shape[0] + grad_o.shape[0]) // count + norm_lanes)
    chunks = 4
    return pl.pallas_call(
        functools.partial(project_kernel, chunks),
        out_shape=(
            jax.ShapeDtypeStruct((count, rank, width), jnp.bfloat16),
            pltpu.VMEM(grad_q.shape, jnp.bfloat16),
            pltpu.VMEM(grad_o.shape, jnp.bfloat16),
        ),
        in_specs=[whole] * 3 + [in_place] * 4,
        out_specs=(whole, whole, whole),
        scratch_shapes=[
            pltpu.VMEM(grad_q.shape, jnp.bfloat16),
            pltpu.VMEM(grad_q.shape, jnp.bfloat16),
            pltpu.VMEM(grad_o.shape, jnp.bfloat16),
            pltpu.VMEM(grad_o.shape, jnp.bfloat16),
            pltpu.VMEM((rank, grad_q.shape[0]), jnp.float32),
            pltpu.VMEM((rank, grad_o.shape[0]), jnp.float32),
            pltpu.SemaphoreType.DMA((chunks, 4)),
        ],
        compiler_params=pltpu.CompilerParams(vmem_limit_bytes=24 * mib),
        name="project",
    )(fac_q, fac_o, norm, grad_q, error_q, grad_o, error_o)


def total_of(got):
    total = got[0].astype(jnp.float32)
    for slot in range(1, got.shape[0]):
        total = total + got[slot].astype(jnp.float32)
    return total


def hat_kernel(size_q, size_o, got, ginv_q, ginv_o, send):
    total = total_of(got)
    highest = lax.Precision.HIGHEST
    hat_q = dot(ginv_q[...].T, total[:, :size_q], 1, 0, highest)
    hat_o = dot(ginv_o[...].T, total[:, size_q:size_q + size_o], 1, 0, highest)
    part = total[:, size_q + size_o:size_q + size_o + norm_lanes]
    high = part.astype(jnp.bfloat16).astype(jnp.float32)
    low = pltpu.roll(part - high, low_row, 0)
    row = lax.broadcasted_iota(jnp.int32, part.shape, 0)
    norm = jnp.where(row < low_row, high, low).astype(jnp.bfloat16)
    hat_q = hat_q.astype(jnp.bfloat16)
    hat_o = hat_o.astype(jnp.bfloat16)
    for slot in range(send.shape[0]):
        send[slot, :, :size_q] = hat_q
        send[slot, :, size_q:size_q + size_o] = hat_o
        send[slot, :, size_q + size_o:size_q + size_o + norm_lanes] = norm


def hats(got, ginv_q, ginv_o, size_q, size_o):
    return pl.pallas_call(
        functools.partial(hat_kernel, size_q, size_o),
        out_shape=jax.ShapeDtypeStruct(got.shape, jnp.bfloat16),
        in_specs=[whole] * 3,
        out_specs=whole,
        compiler_params=pltpu.CompilerParams(vmem_limit_bytes=16 * mib),
        name="hats",
    )(got, ginv_q, ginv_o)


def right_kernel(got, mat_q, mat_o, hat_q, hat_o, send, norm):
    count = got.shape[0]
    size_q = hat_q.shape[1] // count
    size_o = hat_o.shape[1] // count
    for slot in range(count):
        hat_q[:, slot * size_q:(slot + 1) * size_q] = got[slot, :, :size_q]
        hat_o[:, slot * size_o:(slot + 1) * size_o] = got[slot, :, size_q:size_q + size_o]
        part = got[slot, :, size_q + size_o:size_q + size_o + norm_lanes].astype(jnp.float32)
        norm[slot] = part[:low_row] + part[low_row:2 * low_row]
    q_q = dot(hat_q[...], mat_q[...], 1, 0)
    q_o = dot(hat_o[...], mat_o[...], 1, 0)
    size_q = q_q.shape[1] // count
    size_o = q_o.shape[1] // count
    for slot in range(count):
        send[slot, :, :size_o] = q_o[:, slot * size_o:(slot + 1) * size_o].astype(jnp.bfloat16)
        send[slot, :, size_o:size_o + size_q] = q_q[
            :, slot * size_q:(slot + 1) * size_q
        ].astype(jnp.bfloat16)


def right(got, mat_q, mat_o):
    count, rank, _ = got.shape
    width = padded((mat_q.shape[1] + mat_o.shape[1]) // count)
    return pl.pallas_call(
        right_kernel,
        out_shape=(
            jax.ShapeDtypeStruct((rank, mat_q.shape[0]), jnp.bfloat16),
            jax.ShapeDtypeStruct((rank, mat_o.shape[0]), jnp.bfloat16),
            jax.ShapeDtypeStruct((count, rank, width), jnp.bfloat16),
            jax.ShapeDtypeStruct((count, low_row, norm_lanes), jnp.float32),
        ),
        in_specs=[whole] * 3,
        out_specs=(whole,) * 4,
        compiler_params=pltpu.CompilerParams(vmem_limit_bytes=16 * mib),
        name="right",
    )(got, mat_q, mat_o)


def mean_kernel(got, send):
    mean = (total_of(got) / got.shape[0]).astype(jnp.bfloat16)
    for slot in range(send.shape[0]):
        send[slot] = mean


def means(got):
    return pl.pallas_call(
        mean_kernel,
        out_shape=jax.ShapeDtypeStruct(got.shape, jnp.bfloat16),
        in_specs=[whole],
        out_specs=whole,
        compiler_params=pltpu.CompilerParams(vmem_limit_bytes=16 * mib),
        name="means",
    )(got)


def finish_kernel(
    chunks, got_hat, got_new, hat_q, hat_o, mat_q, mat_o, weight_q, momentum_q, weight_o, momentum_o,
    error_q_new, new_q, momentum_q_new, weight_q_new,
    error_o_new, new_o, momentum_o_new, weight_o_new,
    error_q_v, error_o_v, sems
):
    count = got_new.shape[0]
    me = lax.axis_index("replica")
    size_q = new_q.shape[1] // count
    size_o = new_o.shape[1] // count
    for slot in range(count):
        new_o[:, slot * size_o:(slot + 1) * size_o] = got_new[slot, :, :size_o]
        new_q[:, slot * size_q:(slot + 1) * size_q] = got_new[slot, :, size_o:size_o + size_q]
    copies = []
    rows_q = mat_q.shape[0] // chunks
    rows_o = mat_o.shape[0] // chunks
    for chunk in range(chunks):
        part = pl.ds(chunk * rows_q, rows_q)
        approx = dot(hat_q[:, part], new_q[...], 0, 0)
        error_q_v[part] = (mat_q[part].astype(jnp.float32) - approx).astype(jnp.bfloat16)
        copy = pltpu.make_async_copy(error_q_v.at[part], error_q_new.at[part], sems.at[chunk, 0])
        copy.start()
        copies.append(copy)
        part = pl.ds(chunk * rows_o, rows_o)
        approx = dot(hat_o[:, part], new_o[...], 0, 0)
        error_o_v[part] = (mat_o[part].astype(jnp.float32) - approx).astype(jnp.bfloat16)
        copy = pltpu.make_async_copy(error_o_v.at[part], error_o_new.at[part], sems.at[chunk, 1])
        copy.start()
        copies.append(copy)
    mine = got_hat[me][:, :weight_q.shape[0]]
    moved = momentum_decay * momentum_q[...] + dot(mine, new_q[...], 0, 0)
    momentum_q_new[...] = moved
    weight_q_new[...] = weight_q[...] - step_size * moved
    mine = got_new[me][:, :weight_o.shape[1]]
    moved = momentum_decay * momentum_o[...] + dot(hat_o[...], mine, 0, 0)
    momentum_o_new[...] = moved
    weight_o_new[...] = weight_o[...] - step_size * moved
    for copy in copies:
        copy.wait()


def finish(got_hat, got_new, hat_q, hat_o, mat_q, mat_o, weight_q, momentum_q, weight_o, momentum_o):
    rank = hat_q.shape[0]
    chunks = 4
    f32 = jnp.float32
    bf16 = jnp.bfloat16
    return pl.pallas_call(
        functools.partial(finish_kernel, chunks),
        out_shape=(
            jax.ShapeDtypeStruct(mat_q.shape, bf16),
            jax.ShapeDtypeStruct((rank, mat_q.shape[1]), bf16),
            jax.ShapeDtypeStruct(weight_q.shape, f32),
            jax.ShapeDtypeStruct(weight_q.shape, f32),
            jax.ShapeDtypeStruct(mat_o.shape, bf16),
            jax.ShapeDtypeStruct((rank, mat_o.shape[1]), bf16),
            jax.ShapeDtypeStruct(weight_o.shape, f32),
            jax.ShapeDtypeStruct(weight_o.shape, f32),
        ),
        in_specs=[whole] * 10,
        out_specs=(in_place, whole, whole, whole) * 2,
        scratch_shapes=[
            pltpu.VMEM(mat_q.shape, bf16),
            pltpu.VMEM(mat_o.shape, bf16),
            pltpu.SemaphoreType.DMA((chunks, 2)),
        ],
        compiler_params=pltpu.CompilerParams(vmem_limit_bytes=24 * mib),
        name="finish",
    )(got_hat, got_new, hat_q, hat_o, mat_q, mat_o, weight_q, momentum_q, weight_o, momentum_o)


def spread(send):
    return lax.all_to_all(send, "replica", 0, 0, tiled=True)


def keep(value):
    return pltpu.with_memory_space_constraint(value, pltpu.VMEM)


def on_device(
    grad_q,
    error_q,
    qfac_q,
    ginv_q,
    weight_q,
    momentum_q,
    grad_o,
    error_o,
    qfac_o,
    ginv_o,
    weight_o,
    momentum_o,
    norm_grads,
):
    replicas = lax.axis_size("replica")
    tensors = lax.axis_size("tensor")
    rank = qfac_q.shape[1]
    norm_rows = norm_grads.size // (replicas * norm_lanes)
    norm = norm_grads.reshape(replicas, norm_rows, norm_lanes)
    norm = jnp.pad(norm, ((0, 0), (0, rank - norm_rows), (0, 0)))
    size_q = grad_q.shape[0] // replicas
    size_o = grad_o.shape[0] // replicas
    send, mat_q, mat_o = project(grad_q, error_q, grad_o, error_o, qfac_q.T, qfac_o.T, norm)
    got_hat = spread(hats(spread(send), ginv_q, ginv_o, size_q, size_o))
    hat_q, hat_o, send, norm_part = right(got_hat, keep(mat_q), keep(mat_o))
    got_new = spread(means(spread(send)))
    norm_total = norm_part
    for step in range(1, tensors):
        pairs = [(source, (source + step) % tensors) for source in range(tensors)]
        norm_total = norm_total + lax.ppermute(norm_part, "tensor", pairs)
    norm_mean = (norm_total[:, :norm_rows] / (replicas * tensors)).reshape(-1)
    (
        error_q_new, new_q, momentum_q_new, weight_q_new,
        error_o_new, new_o, momentum_o_new, weight_o_new,
    ) = finish(
        got_hat, got_new, hat_q, hat_o, keep(mat_q), keep(mat_o),
        keep(weight_q), keep(momentum_q), keep(weight_o), keep(momentum_o),
    )
    return (
        error_q_new,
        new_q.T,
        momentum_q_new,
        weight_q_new,
        error_o_new,
        new_o.T,
        momentum_o_new,
        weight_o_new,
        norm_mean,
    )


def solution(mesh):
    in_specs = (
        P("replica", "tensor"),
        P("replica", "tensor"),
        P("tensor", None),
        P("tensor", None),
        P("replica", "tensor"),
        P("replica", "tensor"),
        P(("replica", "tensor"), None),
        P(("replica", "tensor"), None),
        P("tensor", None),
        P("tensor", None),
        P("tensor", "replica"),
        P("tensor", "replica"),
        P("replica", "tensor", None),
    )
    out_specs = (
        P("replica", "tensor"),
        P("tensor", None),
        P("replica", "tensor"),
        P("replica", "tensor"),
        P(("replica", "tensor"), None),
        P("tensor", None),
        P("tensor", "replica"),
        P("tensor", "replica"),
        P(),
    )
    return jax.shard_map(
        on_device, mesh=mesh, in_specs=in_specs, out_specs=out_specs, check_vma=False
    )
```

```python
import functools

import jax
import jax.numpy as jnp
from jax import lax
from jax.experimental import pallas as pl
from jax.experimental.pallas import tpu as pltpu
from jax.sharding import PartitionSpec as P

momentum_decay = 0.9
step_size = 0.5
lanes = 128
mib = 1024 * 1024
bf16 = jnp.bfloat16
f32 = jnp.float32

whole = pl.BlockSpec(memory_space=pltpu.VMEM)
in_place = pl.BlockSpec(memory_space=pl.ANY)


def dot(left, right, left_dim, right_dim, precision=None):
    return lax.dot_general(
        left,
        right,
        (((left_dim,), (right_dim,)), ((), ())),
        precision=precision,
        preferred_element_type=f32,
    )


def params(limit):
    return pltpu.CompilerParams(vmem_limit_bytes=limit * mib)


def cost(flops, moved):
    return pl.CostEstimate(flops=flops, bytes_accessed=moved, transcendentals=0)


def in_hbm(value):
    return pltpu.with_memory_space_constraint(value, pltpu.HBM)


def in_vmem(value):
    return pltpu.with_memory_space_constraint(value, pltpu.VMEM)


def parity():
    return lax.rem(lax.axis_index("replica"), 2)


def half_at(which, size):
    return pl.ds(pl.multiple_of(which * size, size), size)


def load(source, target, sem):
    copy = pltpu.make_async_copy(source, target, sem)
    copy.start()
    return copy


def split_norm(total):
    high = total.astype(bf16)
    low = (total - high.astype(f32)).astype(bf16)
    return jnp.concatenate([high, low], axis=0)


def join_norm(pair):
    rows = pair.shape[0] // 2
    return pair[:rows].astype(f32) + pair[rows:].astype(f32)


def project_half(
    which, fac_q_h, fac_o_h, grad_q, error_q, grad_o, error_o, mat_q, mat_o, store,
    fac_q, fac_o, grad_q_v, error_q_v, grad_o_v, error_o_v, sems,
):
    half_q, half_o = mat_q.shape[0], mat_o.shape[0]
    jobs = []
    fac_copies = [load(fac_q_h, fac_q, sems.at[0]), load(fac_o_h, fac_o, sems.at[1])]
    chunks_q, chunks_o = 4, 2
    rows_q, rows_o = half_q // chunks_q, half_o // chunks_o
    slot = 2
    for chunk in range(chunks_q):
        part = pl.ds(chunk * rows_q, rows_q)
        there = pl.ds(pl.multiple_of(which * half_q + chunk * rows_q, rows_q), rows_q)
        jobs.append((grad_q_v, error_q_v, mat_q, fac_q, part, chunk * rows_q, (
            load(grad_q.at[there], grad_q_v.at[part], sems.at[slot]),
            load(error_q.at[there], error_q_v.at[part], sems.at[slot + 1]),
        )))
        slot += 2
        if chunk % 2 == 0:
            continue
        chunk = chunk // 2
        part = pl.ds(chunk * rows_o, rows_o)
        there = pl.ds(pl.multiple_of(which * half_o + chunk * rows_o, rows_o), rows_o)
        jobs.append((grad_o_v, error_o_v, mat_o, fac_o, part, half_q + chunk * rows_o, (
            load(grad_o.at[there], grad_o_v.at[part], sems.at[slot]),
            load(error_o.at[there], error_o_v.at[part], sems.at[slot + 1]),
        )))
        slot += 2
    for copy in fac_copies:
        copy.wait()
    for grad_v, error_v, mat, fac, part, column, copies in jobs:
        for copy in copies:
            copy.wait()
        block = (grad_v[part].astype(f32) + error_v[part].astype(f32)).astype(bf16)
        mat[part] = block
        store(column, dot(fac[...], block, 1, 1))


def far_kernel(
    fac_q_h, fac_o_h, norm_grads, grad_q, error_q, grad_o, error_o,
    mat_q, mat_o, send, norm_near, norm_rows, *scratch
):
    far = 1 - parity()
    values = norm_grads[0].astype(f32)
    rows = norm_rows.shape[0]
    for row in range(rows):
        norm_rows[row:row + 1, :] = values[:, row * lanes:(row + 1) * lanes]
    half = rows // 2
    norm_near[...] = norm_rows[half_at(1 - far, half), :]
    columns = mat_q.shape[0] + mat_o.shape[0]
    given = norm_rows[half_at(far, half), :]
    send[:, columns:] = jnp.concatenate([given, jnp.zeros_like(given)], axis=0).astype(bf16)

    def store(column, value):
        send[:, column:column + value.shape[1]] = value.astype(bf16)

    project_half(
        far, fac_q_h, fac_o_h, grad_q, error_q, grad_o, error_o, mat_q, mat_o, store, *scratch
    )


def near_kernel(
    fac_q_h, fac_o_h, grad_q, error_q, grad_o, error_o, mat_q, mat_o, part, *scratch
):
    def store(column, value):
        part[:, column:column + value.shape[1]] = value

    project_half(
        parity(), fac_q_h, fac_o_h, grad_q, error_q, grad_o, error_o, mat_q, mat_o, store, *scratch
    )


def project(grad_q, error_q, grad_o, error_o, fac_q, fac_o, norm_grads):
    rank = fac_q.shape[0]
    half_q = (grad_q.shape[0] // 2, grad_q.shape[1])
    half_o = (grad_o.shape[0] // 2, grad_o.shape[1])
    columns = half_q[0] + half_o[0]
    norm_rows = norm_grads.size // lanes
    mats = (pltpu.VMEM(half_q, bf16), pltpu.VMEM(half_o, bf16))
    scratch = [
        pltpu.VMEM(fac_q.shape, bf16),
        pltpu.VMEM(fac_o.shape, bf16),
        pltpu.VMEM(half_q, bf16),
        pltpu.VMEM(half_q, bf16),
        pltpu.VMEM(half_o, bf16),
        pltpu.VMEM(half_o, bf16),
        pltpu.SemaphoreType.DMA((14,)),
    ]
    big = [in_hbm(value) for value in (grad_q, error_q, grad_o, error_o)]
    facs = [in_hbm(fac_q), in_hbm(fac_o)]
    effort = cost(2 * rank * (grad_q.size + grad_o.size) // 2, 4 * grad_q.size)
    mat_q_far, mat_o_far, send, norm_near = pl.pallas_call(
        far_kernel,
        out_shape=mats + (
            jax.ShapeDtypeStruct((rank, columns + lanes), bf16),
            jax.ShapeDtypeStruct((norm_rows // 2, lanes), f32),
        ),
        in_specs=[in_place] * 2 + [whole] + [in_place] * 4,
        out_specs=(whole,) * 4,
        scratch_shapes=[pltpu.VMEM((norm_rows, lanes), f32)] + scratch,
        compiler_params=params(16),
        cost_estimate=effort,
        name="project_far",
    )(*facs, in_hbm(norm_grads), *big)
    mat_q_near, mat_o_near, part = pl.pallas_call(
        near_kernel,
        out_shape=mats + (jax.ShapeDtypeStruct((rank, columns), f32),),
        in_specs=[in_place] * 6,
        out_specs=(whole,) * 3,
        scratch_shapes=scratch,
        compiler_params=params(16),
        cost_estimate=effort,
        name="project_near",
    )(*facs, *big)
    return mat_q_far, mat_o_far, send, norm_near, mat_q_near, mat_o_near, part


def first_sum_kernel(part, norm_near, got, state):
    columns = part.shape[1]
    state[:, :columns] = (part[...] + got[:, :columns].astype(f32)).astype(bf16)
    rows = norm_near.shape[0]
    state[:, columns:] = split_norm(norm_near[...] + got[:rows, columns:].astype(f32))


def first_sum(part, norm_near, got):
    return pl.pallas_call(
        first_sum_kernel,
        out_shape=jax.ShapeDtypeStruct(got.shape, bf16),
        in_specs=[whole] * 3,
        out_specs=whole,
        compiler_params=params(8),
        name="first_sum",
    )(part, norm_near, got)


def norm_sum_kernel(mine, got, state):
    columns = mine.shape[1] - lanes
    state[:, :columns] = (
        mine[:, :columns].astype(f32) + got[:, :columns].astype(f32)
    ).astype(bf16)
    state[:, columns:] = split_norm(join_norm(mine[:, columns:]) + join_norm(got[:, columns:]))


def plain_sum_kernel(mine, got, state):
    state[...] = (mine[...].astype(f32) + got[...].astype(f32)).astype(bf16)


def pair_sum(kernel, mine, got, name):
    return pl.pallas_call(
        kernel,
        out_shape=jax.ShapeDtypeStruct(got.shape, bf16),
        in_specs=[whole] * 2,
        out_specs=whole,
        compiler_params=params(8),
        name=name,
    )(mine, got)


def hat_kernel(size_q, mine, got, ginv_q, ginv_o, state):
    columns = mine.shape[1] - lanes
    total = mine[:, :columns].astype(f32) + got[:, :columns].astype(f32)
    highest = lax.Precision.HIGHEST
    state[:, :size_q] = dot(ginv_q[...].T, total[:, :size_q], 1, 0, highest).astype(bf16)
    state[:, size_q:columns] = dot(ginv_o[...].T, total[:, size_q:], 1, 0, highest).astype(bf16)
    state[:, columns:] = split_norm(join_norm(mine[:, columns:]) + join_norm(got[:, columns:]))


def hats(mine, got, ginv_q, ginv_o, size_q):
    return pl.pallas_call(
        functools.partial(hat_kernel, size_q),
        out_shape=jax.ShapeDtypeStruct(got.shape, bf16),
        in_specs=[whole] * 4,
        out_specs=whole,
        compiler_params=params(8),
        name="hats",
    )(mine, got, ginv_q, ginv_o)


def right_near_kernel(hat, mat_q, mat_o, part_q, part_o):
    size_q, size_o = mat_q.shape[0], mat_o.shape[0]
    part_q[...] = dot(hat[:, :size_q], mat_q[...], 1, 0)
    part_o[...] = dot(hat[:, size_q:size_q + size_o], mat_o[...], 1, 0)


def right_near(hat, mat_q, mat_o):
    rank = hat.shape[0]
    return pl.pallas_call(
        right_near_kernel,
        out_shape=(
            jax.ShapeDtypeStruct((rank, mat_q.shape[1]), f32),
            jax.ShapeDtypeStruct((rank, mat_o.shape[1]), f32),
        ),
        in_specs=[whole] * 3,
        out_specs=(whole,) * 2,
        compiler_params=params(8),
        cost_estimate=cost(2 * rank * (mat_q.size + mat_o.size), 2 * (mat_q.size + mat_o.size)),
        name="right_near",
    )(hat, in_vmem(mat_q), in_vmem(mat_o))


def right_far_kernel(hat, mat_q, mat_o, part_q, part_o, hat_near, send, near, norm, all_q, all_o):
    size_q, size_o = mat_q.shape[0], mat_o.shape[0]
    all_q[...] = part_q[...] + dot(hat[:, :size_q], mat_q[...], 1, 0)
    all_o[...] = part_o[...] + dot(hat[:, size_q:size_q + size_o], mat_o[...], 1, 0)
    mine = parity()
    half_q, half_o = all_q.shape[1] // 2, all_o.shape[1] // 2
    send[:, :half_q] = all_q[:, half_at(1 - mine, half_q)].astype(bf16)
    send[:, half_q:] = all_o[:, half_at(1 - mine, half_o)].astype(bf16)
    near[:, :half_q] = all_q[:, half_at(mine, half_q)]
    near[:, half_q:] = all_o[:, half_at(mine, half_o)]
    columns = size_q + size_o
    half = norm.shape[0] // 2
    norm[half_at(mine, half), :] = join_norm(hat_near[:, columns:])
    norm[half_at(1 - mine, half), :] = join_norm(hat[:, columns:])


def right_far(hat, mat_q, mat_o, part_q, part_o, hat_near, norm_rows):
    rank = hat.shape[0]
    columns = (mat_q.shape[1] + mat_o.shape[1]) // 2
    return pl.pallas_call(
        right_far_kernel,
        out_shape=(
            jax.ShapeDtypeStruct((rank, columns), bf16),
            jax.ShapeDtypeStruct((rank, columns), f32),
            jax.ShapeDtypeStruct((norm_rows, lanes), f32),
        ),
        in_specs=[whole] * 6,
        out_specs=(whole,) * 3,
        scratch_shapes=[pltpu.VMEM(part_q.shape, f32), pltpu.VMEM(part_o.shape, f32)],
        compiler_params=params(8),
        cost_estimate=cost(2 * rank * (mat_q.size + mat_o.size), 2 * (mat_q.size + mat_o.size)),
        name="right_far",
    )(hat, in_vmem(mat_q), in_vmem(mat_o), part_q, part_o, hat_near)


def near_sum_kernel(near, got, norm, state, norm_out):
    state[...] = (near[...] + got[...].astype(f32)).astype(bf16)
    norm_out[...] = norm[...]


def near_sum(near, got, norm):
    return pl.pallas_call(
        near_sum_kernel,
        out_shape=(
            jax.ShapeDtypeStruct(got.shape, bf16),
            jax.ShapeDtypeStruct(norm.shape, f32),
        ),
        in_specs=[whole] * 3,
        out_specs=(whole,) * 2,
        compiler_params=params(8),
        name="near_sum",
    )(near, got, norm)


def mean_kernel(count, mine, got, state):
    state[...] = ((mine[...].astype(f32) + got[...].astype(f32)) / count).astype(bf16)


def error_columns(column, hat, hat_row, half, mat_q, mat_o, new, error_q, error_o, stage_q, stage_o, sems, slot):
    size_q, size_o = mat_q.shape[0], mat_o.shape[0]
    wide_q, wide_o = stage_q.shape[1], stage_o.shape[1]
    copies = []
    chunk_q, chunk_o = size_q // 2, size_o // 2
    cols_q, cols_o = half_at(column, wide_q), half_at(column, wide_o)
    for chunk in range(2):
        part = pl.ds(chunk * chunk_q, chunk_q)
        stage = pl.ds(hat_row * size_q + chunk * chunk_q, chunk_q)
        approx = dot(hat[:, part], new[:, :wide_q], 0, 0)
        stage_q[stage] = (mat_q[part, cols_q].astype(f32) - approx).astype(bf16)
        there = pl.ds(pl.multiple_of(half * size_q + chunk * chunk_q, chunk_q), chunk_q)
        copies.append(load(stage_q.at[stage], error_q.at[there, cols_q], sems.at[slot]))
        part = pl.ds(chunk * chunk_o, chunk_o)
        stage = pl.ds(hat_row * size_o + chunk * chunk_o, chunk_o)
        approx = dot(hat[:, size_q + chunk * chunk_o:size_q + (chunk + 1) * chunk_o], new[:, wide_q:], 0, 0)
        stage_o[stage] = (mat_o[part, cols_o].astype(f32) - approx).astype(bf16)
        there = pl.ds(pl.multiple_of(half * size_o + chunk * chunk_o, chunk_o), chunk_o)
        copies.append(load(stage_o.at[stage], error_o.at[there, cols_o], sems.at[slot + 1]))
        slot += 2
    return copies


def finish_near_kernel(
    hat_near, hat_far, mat_q_near, mat_o_near, mat_q_far, mat_o_far, new,
    error_q, error_o, stage_q, stage_o, sems
):
    mine = parity()
    copies = error_columns(
        mine, hat_near, 0, mine, mat_q_near, mat_o_near, new, error_q, error_o, stage_q, stage_o, sems, 0
    ) + error_columns(
        mine, hat_far, 1, 1 - mine, mat_q_far, mat_o_far, new, error_q, error_o, stage_q, stage_o, sems, 4
    )
    for copy in copies:
        copy.wait()


def piece_of(near, far, index, count, pieces):
    half = count // 2
    size = pieces.shape[2]
    here = index // half == parity()
    chosen = jnp.where(here, near.astype(f32), far.astype(f32))
    for slot in range(half):
        pieces[slot] = chosen[:, slot * size:(slot + 1) * size]
    return pieces[lax.rem(index, half)].astype(bf16)


def finish_far_kernel(
    count, hat_near, hat_far, mat_q_near, mat_o_near, mat_q_far, mat_o_far, new_near, new_far,
    error_q_in, error_o_in, weight_q, momentum_q, weight_o, momentum_o,
    error_q, error_o, new_q, new_o, momentum_q_new, weight_q_new, momentum_o_new, weight_o_new,
    stage_q, stage_o, weight_q_v, momentum_q_v, weight_o_v, momentum_o_v, pieces_q, pieces_o,
    sems, in_sems, out_sems
):
    mine = parity()
    me = lax.axis_index("replica")
    loads = [
        load(source, target, in_sems.at[slot])
        for slot, (source, target) in enumerate((
            (weight_q, weight_q_v), (momentum_q, momentum_q_v),
            (weight_o, weight_o_v), (momentum_o, momentum_o_v),
        ))
    ]
    wide_q, wide_o = stage_q.shape[1], stage_o.shape[1]
    size_q = mat_q_near.shape[0]
    size_o = mat_o_near.shape[0]
    new_q[:, half_at(mine, wide_q)] = new_near[:, :wide_q]
    new_q[:, half_at(1 - mine, wide_q)] = new_far[:, :wide_q]
    new_o[:, half_at(mine, wide_o)] = new_near[:, wide_q:]
    new_o[:, half_at(1 - mine, wide_o)] = new_far[:, wide_q:]
    copies = error_columns(
        1 - mine, hat_near, 0, mine, mat_q_near, mat_o_near, new_far,
        error_q, error_o, stage_q, stage_o, sems, 0
    ) + error_columns(
        1 - mine, hat_far, 1, 1 - mine, mat_q_far, mat_o_far, new_far,
        error_q, error_o, stage_q, stage_o, sems, 4
    )
    hat_piece = piece_of(hat_near[:, :size_q], hat_far[:, :size_q], me, count, pieces_q)
    new_piece = piece_of(new_near[:, wide_q:], new_far[:, wide_q:], me, count, pieces_o)
    for copy in loads:
        copy.wait()
    moved = momentum_decay * momentum_q_v[...] + dot(hat_piece, new_q[...], 0, 0)
    momentum_q_v[...] = moved
    weight_q_v[...] = weight_q_v[...] - step_size * moved
    copies.append(load(momentum_q_v, momentum_q_new, out_sems.at[0]))
    copies.append(load(weight_q_v, weight_q_new, out_sems.at[1]))
    half = mine * size_o
    rows = pl.ds(pl.multiple_of(half, size_o), size_o)
    moved = momentum_decay * momentum_o_v[rows] + dot(
        hat_near[:, size_q:size_q + size_o], new_piece, 0, 0
    )
    momentum_o_v[rows] = moved
    weight_o_v[rows] = weight_o_v[rows] - step_size * moved
    rows = pl.ds(pl.multiple_of((1 - mine) * size_o, size_o), size_o)
    moved = momentum_decay * momentum_o_v[rows] + dot(
        hat_far[:, size_q:size_q + size_o], new_piece, 0, 0
    )
    momentum_o_v[rows] = moved
    weight_o_v[rows] = weight_o_v[rows] - step_size * moved
    copies.append(load(momentum_o_v, momentum_o_new, out_sems.at[2]))
    copies.append(load(weight_o_v, weight_o_new, out_sems.at[3]))
    for copy in copies:
        copy.wait()


def finish(
    count, hat_near, hat_far, mats, new_near, send_far, weight_q, momentum_q, weight_o, momentum_o
):
    mat_q, mat_o = mats[0], mats[1]
    rank = hat_near.shape[0]
    size_q, size_o = mat_q.shape[0], mat_o.shape[0]
    error_q = jax.ShapeDtypeStruct((2 * size_q, mat_q.shape[1]), bf16)
    error_o = jax.ShapeDtypeStruct((2 * size_o, mat_o.shape[1]), bf16)
    stages = [
        pltpu.VMEM((2 * size_q, mat_q.shape[1] // 2), bf16),
        pltpu.VMEM((2 * size_o, mat_o.shape[1] // 2), bf16),
    ]
    moved = 4 * (mat_q.size + mat_o.size)
    mats = [in_vmem(mat) for mat in mats]
    new_far = send_far(new_near)
    error_q_part, error_o_part = pl.pallas_call(
        finish_near_kernel,
        out_shape=(error_q, error_o),
        in_specs=[whole] * 7,
        out_specs=(in_place,) * 2,
        scratch_shapes=stages + [pltpu.SemaphoreType.DMA((8,))],
        compiler_params=params(12),
        cost_estimate=cost(2 * rank * (mat_q.size + mat_o.size), moved),
        name="finish_near",
    )(hat_near, hat_far, *mats, new_near)
    piece_q = weight_q.shape[0]
    piece_o = weight_o.shape[1]
    return pl.pallas_call(
        functools.partial(finish_far_kernel, count),
        out_shape=(
            error_q,
            error_o,
            jax.ShapeDtypeStruct((rank, mat_q.shape[1]), bf16),
            jax.ShapeDtypeStruct((rank, mat_o.shape[1]), bf16),
            jax.ShapeDtypeStruct(weight_q.shape, f32),
            jax.ShapeDtypeStruct(weight_q.shape, f32),
            jax.ShapeDtypeStruct(weight_o.shape, f32),
            jax.ShapeDtypeStruct(weight_o.shape, f32),
        ),
        in_specs=[whole] * 8 + [in_place] * 6,
        out_specs=(in_place, in_place, whole, whole) + (in_place,) * 4,
        scratch_shapes=stages + [
            pltpu.VMEM(weight_q.shape, f32),
            pltpu.VMEM(weight_q.shape, f32),
            pltpu.VMEM(weight_o.shape, f32),
            pltpu.VMEM(weight_o.shape, f32),
            pltpu.VMEM((count // 2, rank, piece_q), f32),
            pltpu.VMEM((count // 2, rank, piece_o), f32),
            pltpu.SemaphoreType.DMA((8,)),
            pltpu.SemaphoreType.DMA((4,)),
            pltpu.SemaphoreType.DMA((4,)),
        ],
        input_output_aliases={8: 0, 9: 1},
        compiler_params=params(16),
        cost_estimate=cost(2 * rank * (mat_q.size + mat_o.size), moved),
        name="finish_far",
    )(
        hat_near, hat_far, *mats, new_near, new_far, error_q_part, error_o_part,
        in_hbm(weight_q), in_hbm(momentum_q), in_hbm(weight_o), in_hbm(momentum_o),
    )


def norm_mean_kernel(count, *refs):
    total = refs[0][...]
    for ref in refs[1:-1]:
        total = total + ref[...]
    refs[-1][...] = total / count


def swap(value, bit):
    count = lax.axis_size("replica")
    return lax.ppermute(value, "replica", [(source, source ^ bit) for source in range(count)])


def on_device(
    grad_q,
    error_q,
    qfac_q,
    ginv_q,
    weight_q,
    momentum_q,
    grad_o,
    error_o,
    qfac_o,
    ginv_o,
    weight_o,
    momentum_o,
    norm_grads,
):
    replicas = lax.axis_size("replica")
    tensors = lax.axis_size("tensor")
    bits = [1 << place for place in range(1, replicas.bit_length() - 1)]
    half_q = grad_q.shape[0] // 2
    norm_rows = norm_grads.size // lanes
    mat_q_far, mat_o_far, send, norm_near, mat_q_near, mat_o_near, part = project(
        grad_q, error_q, grad_o, error_o, qfac_q.T, qfac_o.T, norm_grads
    )
    state = first_sum(part, norm_near, swap(send, 1))
    for bit in bits[:-1]:
        state = pair_sum(norm_sum_kernel, state, swap(state, bit), "norm_sum")
    hat_near = hats(state, swap(state, bits[-1]), ginv_q, ginv_o, half_q)
    hat_far = swap(hat_near, 1)
    part_q, part_o = right_near(hat_near, mat_q_near, mat_o_near)
    send, near, norm = right_far(
        hat_far, mat_q_far, mat_o_far, part_q, part_o, hat_near, norm_rows
    )
    state, norm = near_sum(near, swap(send, 1), norm)
    norms = [norm]
    for step in range(1, tensors):
        pairs = [(source, (source + step) % tensors) for source in range(tensors)]
        norms.append(lax.ppermute(norm, "tensor", pairs))
    for bit in bits[:-1]:
        state = pair_sum(plain_sum_kernel, state, swap(state, bit), "plain_sum")
    new_near = pair_sum(
        functools.partial(mean_kernel, replicas), state, swap(state, bits[-1]), "mean"
    )
    (
        error_q_new, error_o_new, new_q, new_o,
        momentum_q_new, weight_q_new, momentum_o_new, weight_o_new,
    ) = finish(
        replicas, hat_near, hat_far, (mat_q_near, mat_o_near, mat_q_far, mat_o_far),
        new_near, lambda value: swap(value, 1), weight_q, momentum_q, weight_o, momentum_o,
    )
    norm_mean = pl.pallas_call(
        functools.partial(norm_mean_kernel, replicas * tensors),
        out_shape=jax.ShapeDtypeStruct(norm.shape, f32),
        in_specs=[whole] * tensors,
        out_specs=whole,
        compiler_params=params(4),
        name="norm_mean",
    )(*norms)
    return (
        error_q_new,
        new_q.T,
        momentum_q_new,
        weight_q_new,
        error_o_new,
        new_o.T,
        momentum_o_new,
        weight_o_new,
        norm_mean.reshape(-1),
    )


def solution(mesh):
    in_specs = (
        P("replica", "tensor"),
        P("replica", "tensor"),
        P("tensor", None),
        P("tensor", None),
        P("replica", "tensor"),
        P("replica", "tensor"),
        P(("replica", "tensor"), None),
        P(("replica", "tensor"), None),
        P("tensor", None),
        P("tensor", None),
        P("tensor", "replica"),
        P("tensor", "replica"),
        P("replica", "tensor", None),
    )
    out_specs = (
        P("replica", "tensor"),
        P("tensor", None),
        P("replica", "tensor"),
        P("replica", "tensor"),
        P(("replica", "tensor"), None),
        P("tensor", None),
        P("tensor", "replica"),
        P("tensor", "replica"),
        P(),
    )
    return jax.shard_map(
        on_device, mesh=mesh, in_specs=in_specs, out_specs=out_specs, check_vma=False
    )
```

```python
import functools

import jax
import jax.numpy as jnp
from jax import lax
from jax.experimental import pallas as pl
from jax.experimental.pallas import tpu as pltpu
from jax.sharding import PartitionSpec as P

momentum_decay = 0.9
step_size = 0.5
lanes = 128
mib = 1024 * 1024
bf16 = jnp.bfloat16
f32 = jnp.float32

whole = pl.BlockSpec(memory_space=pltpu.VMEM)
in_place = pl.BlockSpec(memory_space=pl.ANY)


def dot(left, right, left_dim, right_dim, precision=None):
    return lax.dot_general(
        left,
        right,
        (((left_dim,), (right_dim,)), ((), ())),
        precision=precision,
        preferred_element_type=f32,
    )


def params(limit):
    return pltpu.CompilerParams(vmem_limit_bytes=limit * mib)


brief = pl.CostEstimate(flops=1, bytes_accessed=1, transcendentals=0)


def in_hbm(value):
    return pltpu.with_memory_space_constraint(value, pltpu.HBM)


def in_vmem(value):
    return pltpu.with_memory_space_constraint(value, pltpu.VMEM)


def launch(kernel, operands, after=(), **options):
    count = len(operands)
    specs = options.pop("in_specs")

    def body(*refs):
        kernel(*refs[:count], *refs[count + len(after):])

    return pl.pallas_call(
        body, in_specs=list(specs) + [in_place] * len(after), cost_estimate=brief, **options
    )(
        *operands, *after
    )


def shaped(shape, dtype):
    return jax.ShapeDtypeStruct(shape, dtype)


def parity():
    return lax.rem(lax.axis_index("replica"), 2)


def half_at(which, size):
    return pl.ds(pl.multiple_of(which * size, size), size)


def load(source, target, sem):
    copy = pltpu.make_async_copy(source, target, sem)
    copy.start()
    return copy


def split_norm(total):
    high = total.astype(bf16)
    low = (total - high.astype(f32)).astype(bf16)
    return jnp.concatenate([high, low], axis=0)


def join_norm(pair):
    rows = pair.shape[0] // 2
    return pair[:rows].astype(f32) + pair[rows:].astype(f32)


def project_half(which, chunks, fac_h, grad, error, mat, store, fac, grad_v, error_v, sems):
    half = mat.shape[0]
    rows = half // chunks
    fac_copy = load(fac_h, fac, sems.at[0])
    jobs = []
    for chunk in range(chunks):
        part = pl.ds(chunk * rows, rows)
        there = pl.ds(pl.multiple_of(which * half + chunk * rows, rows), rows)
        jobs.append((part, chunk * rows, (
            load(grad.at[there], grad_v.at[part], sems.at[1 + 2 * chunk]),
            load(error.at[there], error_v.at[part], sems.at[2 + 2 * chunk]),
        )))
    fac_copy.wait()
    for part, column, copies in jobs:
        for copy in copies:
            copy.wait()
        block = (grad_v[part].astype(f32) + error_v[part].astype(f32)).astype(bf16)
        mat[part] = block
        store(column, dot(fac[...], block, 1, 1))


def far_kernel(chunks, fac_h, grad, error, mat, send, *scratch):
    def store(column, value):
        send[:, column:column + value.shape[1]] = value.astype(bf16)

    project_half(1 - parity(), chunks, fac_h, grad, error, mat, store, *scratch)


def far_norm_kernel(
    chunks, fac_h, grad, error, norm_grads, mat, send, norm_near, norm_rows, *scratch
):
    far = 1 - parity()
    values = norm_grads[0].astype(f32)
    rows = norm_rows.shape[0]
    for row in range(rows):
        norm_rows[row:row + 1, :] = values[:, row * lanes:(row + 1) * lanes]
    half = rows // 2
    norm_near[...] = norm_rows[half_at(1 - far, half), :]
    given = norm_rows[half_at(far, half), :]
    send[:, mat.shape[0]:] = jnp.concatenate([given, jnp.zeros_like(given)], axis=0).astype(bf16)
    far_kernel(chunks, fac_h, grad, error, mat, send, *scratch)


def near_kernel(chunks, fac_h, grad, error, mat, part, *scratch):
    def store(column, value):
        part[:, column:column + value.shape[1]] = value

    project_half(parity(), chunks, fac_h, grad, error, mat, store, *scratch)


def project(kernel, chunks, name, grad, error, fac, outs, norm=(), after=()):
    half = (grad.shape[0] // 2, grad.shape[1])
    rank = fac.shape[0]
    scratch = [
        pltpu.VMEM(fac.shape, bf16),
        pltpu.VMEM(half, bf16),
        pltpu.VMEM(half, bf16),
        pltpu.SemaphoreType.DMA((1 + 2 * chunks,)),
    ]
    if norm:
        scratch = [pltpu.VMEM((norm[0].size // lanes, lanes), f32)] + scratch
    return launch(
        functools.partial(kernel, chunks),
        (in_hbm(fac), in_hbm(grad), in_hbm(error), *norm),
        after,
        out_shape=(pltpu.VMEM(half, bf16),) + outs,
        in_specs=[in_place] * 3 + [whole] * len(norm),
        out_specs=(whole,) * (1 + len(outs)),
        scratch_shapes=scratch,
        compiler_params=params(12),
        name=name,
    )


def small(kernel, name, outs, *operands, after=()):
    return launch(
        kernel,
        operands,
        after,
        out_shape=outs,
        in_specs=[whole] * len(operands),
        out_specs=(whole,) * len(outs) if isinstance(outs, tuple) else whole,
        compiler_params=params(8),
        name=name,
    )


def first_sum_kernel(part, got, state):
    state[...] = (part[...] + got[...].astype(f32)).astype(bf16)


def first_norm_sum_kernel(part, norm_near, got, state):
    columns = part.shape[1]
    state[:, :columns] = (part[...] + got[:, :columns].astype(f32)).astype(bf16)
    rows = norm_near.shape[0]
    state[:, columns:] = split_norm(norm_near[...] + got[:rows, columns:].astype(f32))


def sum_kernel(mine, got, state):
    state[...] = (mine[...].astype(f32) + got[...].astype(f32)).astype(bf16)


def norm_sum_kernel(mine, got, state):
    columns = mine.shape[1] - lanes
    state[:, :columns] = (
        mine[:, :columns].astype(f32) + got[:, :columns].astype(f32)
    ).astype(bf16)
    state[:, columns:] = split_norm(join_norm(mine[:, columns:]) + join_norm(got[:, columns:]))


def hat_kernel(columns, mine, got, ginv, state):
    total = mine[:, :columns].astype(f32) + got[:, :columns].astype(f32)
    state[:, :columns] = dot(
        ginv[...].T, total, 1, 0, lax.Precision.HIGHEST
    ).astype(bf16)
    if columns < mine.shape[1]:
        state[:, columns:] = split_norm(join_norm(mine[:, columns:]) + join_norm(got[:, columns:]))


def mean_kernel(count, mine, got, state):
    state[...] = ((mine[...].astype(f32) + got[...].astype(f32)) / count).astype(bf16)


def right_near_kernel(hat, mat, part):
    part[...] = dot(hat[:, :mat.shape[0]], mat[...], 1, 0)


def right_near(name, hat, mat, after=()):
    rank = hat.shape[0]
    return launch(
        right_near_kernel,
        (hat, in_vmem(mat)),
        after,
        out_shape=shaped((rank, mat.shape[1]), f32),
        in_specs=[whole] * 2,
        out_specs=whole,
        compiler_params=params(8),
        name=name,
    )


def right_far_kernel(hat, mat, part, send, near, full):
    full[...] = part[...] + dot(hat[:, :mat.shape[0]], mat[...], 1, 0)
    mine = parity()
    half = full.shape[1] // 2
    send[...] = full[:, half_at(1 - mine, half)].astype(bf16)
    near[...] = full[:, half_at(mine, half)]


def right_far(name, hat, mat, part, after=()):
    rank = hat.shape[0]
    half = mat.shape[1] // 2
    return launch(
        right_far_kernel,
        (hat, in_vmem(mat), part),
        after,
        out_shape=(shaped((rank, half), bf16), shaped((rank, half), f32)),
        in_specs=[whole] * 3,
        out_specs=(whole,) * 2,
        scratch_shapes=[pltpu.VMEM(part.shape, f32)],
        compiler_params=params(8),
        name=name,
    )


def norm_join_kernel(columns, hat_near, hat_far, norm):
    half = norm.shape[0] // 2
    mine = parity()
    norm[half_at(mine, half), :] = join_norm(hat_near[:, columns:])
    norm[half_at(1 - mine, half), :] = join_norm(hat_far[:, columns:])


def norm_add_kernel(count, mine, got, total):
    total[...] = (mine[...] + got[...]) / count


def error_columns(chunks, column, hat, hat_row, half, mat, new, error, stage, sems, slot):
    size = mat.shape[0]
    rows = size // chunks
    columns = half_at(column, stage.shape[1])
    copies = []
    for chunk in range(chunks):
        part = pl.ds(chunk * rows, rows)
        staged = pl.ds(hat_row * size + chunk * rows, rows)
        approx = dot(hat[:, part], new[...], 0, 0)
        stage[staged] = (mat[part, columns].astype(f32) - approx).astype(bf16)
        there = pl.ds(pl.multiple_of(half * size + chunk * rows, rows), rows)
        copies.append(load(stage.at[staged], error.at[there, columns], sems.at[slot + chunk]))
    return copies


def finish_near_kernel(chunks, hat_near, hat_far, mat_near, mat_far, new, error, stage, sems):
    mine = parity()
    copies = error_columns(
        chunks, mine, hat_near, 0, mine, mat_near, new, error, stage, sems, 0
    ) + error_columns(
        chunks, mine, hat_far, 1, 1 - mine, mat_far, new, error, stage, sems, chunks
    )
    for copy in copies:
        copy.wait()


def piece_of(near, far, width, size, index, count, pieces):
    half = count // 2
    here = index // half == parity()
    slot = lax.rem(index, half)
    if size % lanes == 0:
        part = half_at(slot, size)
        return jnp.where(here, near[:, part].astype(f32), far[:, part].astype(f32)).astype(bf16)
    chosen = jnp.where(here, near[:, :width].astype(f32), far[:, :width].astype(f32))
    for place in range(half):
        pieces[place] = chosen[:, place * size:(place + 1) * size]
    return pieces[slot].astype(bf16)


def finish_far_kernel(
    chunks, count, by_rows, hat_near, hat_far, mat_near, mat_far, new_near, new_far, error_in,
    weight_v, momentum_v, error, new, momentum_new, weight_new,
    stage, moved_v, stepped_v, pieces, sems, out_sems
):
    mine = parity()
    me = lax.axis_index("replica")
    wide = stage.shape[1]
    size = mat_near.shape[0]
    new[:, half_at(mine, wide)] = new_near[...]
    new[:, half_at(1 - mine, wide)] = new_far[...]
    if by_rows:
        piece = piece_of(hat_near, hat_far, size, weight_v.shape[0], me, count, pieces)
        moved = momentum_decay * momentum_v[...] + dot(piece, new[...], 0, 0)
        moved_v[...] = moved
        stepped_v[...] = weight_v[...] - step_size * moved
    else:
        piece = piece_of(new_near, new_far, wide, weight_v.shape[1], me, count, pieces)
        for which, hat in ((mine, hat_near), (1 - mine, hat_far)):
            rows = half_at(which, size)
            moved = momentum_decay * momentum_v[rows] + dot(hat[:, :size], piece, 0, 0)
            moved_v[rows] = moved
            stepped_v[rows] = weight_v[rows] - step_size * moved
    copies = [
        load(moved_v, momentum_new, out_sems.at[0]),
        load(stepped_v, weight_new, out_sems.at[1]),
    ]
    copies += error_columns(
        chunks, 1 - mine, hat_near, 0, mine, mat_near, new_far, error, stage, sems, 0
    ) + error_columns(
        chunks, 1 - mine, hat_far, 1, 1 - mine, mat_far, new_far, error, stage, sems, chunks
    )
    for copy in copies:
        copy.wait()


def finish_near(name, chunks, hat_near, hat_far, mat_near, mat_far, new_near, after=()):
    size, width = mat_near.shape
    return launch(
        functools.partial(finish_near_kernel, chunks),
        (hat_near, hat_far, in_vmem(mat_near), in_vmem(mat_far), new_near),
        after,
        out_shape=shaped((2 * size, width), bf16),
        in_specs=[whole] * 5,
        out_specs=in_place,
        scratch_shapes=[
            pltpu.VMEM((2 * size, width // 2), bf16),
            pltpu.SemaphoreType.DMA((2 * chunks,)),
        ],
        compiler_params=params(12),
        name=name,
    )


def finish_far(
    name, chunks, count, by_rows,
    hat_near, hat_far, mat_near, mat_far, new_near, new_far, error, weight_v, momentum_v, after=()
):
    size, width = mat_near.shape
    rank = hat_near.shape[0]
    weight = weight_v.shape
    piece = weight[0] if by_rows else weight[1]
    return launch(
        functools.partial(finish_far_kernel, chunks, count, by_rows),
        (
            hat_near, hat_far, in_vmem(mat_near), in_vmem(mat_far), new_near, new_far, error,
            in_vmem(weight_v), in_vmem(momentum_v),
        ),
        after,
        out_shape=(
            shaped((2 * size, width), bf16),
            shaped((rank, width), bf16),
            shaped(weight, f32),
            shaped(weight, f32),
        ),
        in_specs=[whole] * 6 + [in_place] + [whole] * 2,
        out_specs=(in_place, whole, in_place, in_place),
        scratch_shapes=[
            pltpu.VMEM((2 * size, width // 2), bf16),
            pltpu.VMEM(weight, f32),
            pltpu.VMEM(weight, f32),
            pltpu.VMEM((count // 2, rank, piece), f32),
            pltpu.SemaphoreType.DMA((2 * chunks,)),
            pltpu.SemaphoreType.DMA((2,)),
        ],
        input_output_aliases={6: 0},
        compiler_params=params(16),
        name=name,
    )


def swap(value, bit, axis="replica"):
    count = lax.axis_size(axis)
    return lax.ppermute(value, axis, [(source, source ^ bit) for source in range(count)])


def bits_of(count):
    return [1 << place for place in range(1, count.bit_length() - 1)]


def on_device(
    grad_q,
    error_q,
    qfac_q,
    ginv_q,
    weight_q,
    momentum_q,
    grad_o,
    error_o,
    qfac_o,
    ginv_o,
    weight_o,
    momentum_o,
    norm_grads,
):
    replicas = lax.axis_size("replica")
    tensors = lax.axis_size("tensor")
    rank = qfac_q.shape[1]
    half_q = grad_q.shape[0] // 2
    half_o = grad_o.shape[0] // 2
    norm_rows = norm_grads.size // lanes
    fac_q, fac_o = qfac_q.T, qfac_o.T
    wide_q = (rank, half_q)
    wide_o = (rank, half_o + lanes)
    mat_q_far, send_q = project(
        far_kernel, 4, "project_far_q", grad_q, error_q, fac_q, (shaped(wide_q, bf16),)
    )
    got_q = swap(send_q, 1)
    mat_o_far, send_o, norm_near = project(
        far_norm_kernel, 2, "project_far_o", grad_o, error_o, fac_o,
        (shaped(wide_o, bf16), shaped((norm_rows // 2, lanes), f32)), (in_hbm(norm_grads),),
    )
    got_o = swap(send_o, 1)
    mat_q_near, part_q = project(
        near_kernel, 4, "project_near_q", grad_q, error_q, fac_q, (shaped(wide_q, f32),),
    )
    state_q = small(first_sum_kernel, "first_sum_q", shaped(wide_q, bf16), part_q, got_q)
    mat_o_near, part_o = project(
        near_kernel, 2, "project_near_o", grad_o, error_o, fac_o, (shaped((rank, half_o), f32),),
    )
    state_o = small(
        first_norm_sum_kernel, "first_sum_o", shaped(wide_o, bf16), part_o, norm_near, got_o
    )
    bits = bits_of(replicas)
    for bit in bits[:-1]:
        got_q = swap(state_q, bit)
        got_o = swap(state_o, bit)
        state_q = small(
            sum_kernel, "sum_q", shaped(wide_q, bf16), state_q, got_q
        )
        state_o = small(
            norm_sum_kernel, "sum_o", shaped(wide_o, bf16), state_o, got_o
        )
    got_q = swap(state_q, bits[-1])
    got_o = swap(state_o, bits[-1])
    hat_q = small(
        functools.partial(hat_kernel, half_q), "hat_q", shaped(wide_q, bf16),
        state_q, got_q, ginv_q,
    )
    hat_q_far = swap(hat_q, 1)
    part_q = right_near("right_near_q", hat_q, mat_q_near)
    hat_o = small(
        functools.partial(hat_kernel, half_o), "hat_o", shaped(wide_o, bf16),
        state_o, got_o, ginv_o,
    )
    hat_o_far = swap(hat_o, 1)
    part_o = right_near("right_near_o", hat_o, mat_o_near)
    send_q, near_q = right_far("right_far_q", hat_q_far, mat_q_far, part_q)
    got_q = swap(send_q, 1)
    send_o, near_o = right_far("right_far_o", hat_o_far, mat_o_far, part_o)
    got_o = swap(send_o, 1)
    state_q = small(
        first_sum_kernel, "first_sum_q", shaped(got_q.shape, bf16), near_q, got_q
    )
    state_o = small(
        first_sum_kernel, "first_sum_o", shaped(got_o.shape, bf16), near_o, got_o
    )
    norm = small(
        functools.partial(norm_join_kernel, half_o), "norm_join", shaped((norm_rows, lanes), f32),
        hat_o, hat_o_far, after=(state_o,),
    )
    for bit in bits[:-1]:
        got_q = swap(state_q, bit)
        got_o = swap(state_o, bit)
        state_q = small(
            sum_kernel, "sum_q", shaped(got_q.shape, bf16), state_q, got_q
        )
        state_o = small(
            sum_kernel, "sum_o", shaped(got_o.shape, bf16), state_o, got_o
        )
    got_q = swap(state_q, bits[-1])
    got_o = swap(state_o, bits[-1])
    mean = functools.partial(mean_kernel, replicas)
    new_q = small(mean, "mean_q", shaped(got_q.shape, bf16), state_q, got_q)
    new_q_far = swap(new_q, 1)
    chain_q = (hat_q, hat_q_far, mat_q_near, mat_q_far, new_q)
    error_q_part = finish_near("finish_near_q", 2, *chain_q)
    new_o = small(mean, "mean_o", shaped(got_o.shape, bf16), state_o, got_o)
    new_o_far = swap(new_o, 1)
    chain_o = (hat_o, hat_o_far, mat_o_near, mat_o_far, new_o)
    waits = [(state_o,), (new_o,)]
    bit = 1
    while bit < tensors:
        last = 2 * bit >= tensors
        norm = small(
            functools.partial(norm_add_kernel, replicas * tensors if last else 1), "norm_add",
            shaped(norm.shape, f32), norm, swap(norm, bit, "tensor"), after=waits[last],
        )
        bit *= 2
    error_q_new, qfac_q_new, momentum_q_new, weight_q_new = finish_far(
        "finish_far_q", 2, replicas, True, *chain_q, new_q_far, error_q_part,
        weight_q, momentum_q,
    )
    error_o_part = finish_near("finish_near_o", 2, *chain_o)
    error_o_new, qfac_o_new, momentum_o_new, weight_o_new = finish_far(
        "finish_far_o", 2, replicas, False, *chain_o, new_o_far, error_o_part,
        weight_o, momentum_o,
    )
    return (
        error_q_new,
        qfac_q_new.T,
        momentum_q_new,
        weight_q_new,
        error_o_new,
        qfac_o_new.T,
        momentum_o_new,
        weight_o_new,
        norm.reshape(-1),
    )


def solution(mesh):
    in_specs = (
        P("replica", "tensor"),
        P("replica", "tensor"),
        P("tensor", None),
        P("tensor", None),
        P("replica", "tensor"),
        P("replica", "tensor"),
        P(("replica", "tensor"), None),
        P(("replica", "tensor"), None),
        P("tensor", None),
        P("tensor", None),
        P("tensor", "replica"),
        P("tensor", "replica"),
        P("replica", "tensor", None),
    )
    out_specs = (
        P("replica", "tensor"),
        P("tensor", None),
        P("replica", "tensor"),
        P("replica", "tensor"),
        P(("replica", "tensor"), None),
        P("tensor", None),
        P("tensor", "replica"),
        P("tensor", "replica"),
        P(),
    )
    return jax.shard_map(
        on_device, mesh=mesh, in_specs=in_specs, out_specs=out_specs, check_vma=False
    )
```

```python
import functools

import jax
import jax.numpy as jnp
from jax import lax
from jax.experimental import pallas as pl
from jax.experimental.pallas import tpu as pltpu
from jax.sharding import PartitionSpec as P

momentum_decay = 0.9
step_size = 0.5
lanes = 128
mib = 1024 * 1024
bf16 = jnp.bfloat16
f32 = jnp.float32

whole = pl.BlockSpec(memory_space=pltpu.VMEM)
in_place = pl.BlockSpec(memory_space=pl.ANY)


def dot(left, right, left_dim, right_dim, precision=None):
    return lax.dot_general(
        left,
        right,
        (((left_dim,), (right_dim,)), ((), ())),
        precision=precision,
        preferred_element_type=f32,
    )


def params(limit):
    return pltpu.CompilerParams(vmem_limit_bytes=limit * mib)


def cost(flops, moved):
    return pl.CostEstimate(flops=flops, bytes_accessed=moved, transcendentals=0)


def in_hbm(value):
    return pltpu.with_memory_space_constraint(value, pltpu.HBM)


def in_vmem(value):
    return pltpu.with_memory_space_constraint(value, pltpu.VMEM)


def shaped(shape, dtype):
    return jax.ShapeDtypeStruct(shape, dtype)


def parity():
    return lax.rem(lax.axis_index("replica"), 2)


def half_at(which, size):
    return pl.ds(pl.multiple_of(which * size, size), size)


def load(source, target, sem):
    copy = pltpu.make_async_copy(source, target, sem)
    copy.start()
    return copy


def project_half(
    which, fac_q_h, fac_o_h, grad_q, error_q, grad_o, error_o, mat_q, mat_o, store,
    fac_q, fac_o, grad_q_v, error_q_v, grad_o_v, error_o_v, sems,
):
    half_q, half_o = mat_q.shape[0], mat_o.shape[0]
    jobs = []
    fac_copies = [load(fac_q_h, fac_q, sems.at[0]), load(fac_o_h, fac_o, sems.at[1])]
    chunks_q, chunks_o = 4, 2
    rows_q, rows_o = half_q // chunks_q, half_o // chunks_o
    slot = 2
    for chunk in range(chunks_q):
        part = pl.ds(chunk * rows_q, rows_q)
        there = pl.ds(pl.multiple_of(which * half_q + chunk * rows_q, rows_q), rows_q)
        jobs.append((grad_q_v, error_q_v, mat_q, fac_q, part, chunk * rows_q, (
            load(grad_q.at[there], grad_q_v.at[part], sems.at[slot]),
            load(error_q.at[there], error_q_v.at[part], sems.at[slot + 1]),
        )))
        slot += 2
        if chunk % 2 == 0:
            continue
        chunk = chunk // 2
        part = pl.ds(chunk * rows_o, rows_o)
        there = pl.ds(pl.multiple_of(which * half_o + chunk * rows_o, rows_o), rows_o)
        jobs.append((grad_o_v, error_o_v, mat_o, fac_o, part, half_q + chunk * rows_o, (
            load(grad_o.at[there], grad_o_v.at[part], sems.at[slot]),
            load(error_o.at[there], error_o_v.at[part], sems.at[slot + 1]),
        )))
        slot += 2
    for copy in fac_copies:
        copy.wait()
    for grad_v, error_v, mat, fac, part, column, copies in jobs:
        for copy in copies:
            copy.wait()
        block = (grad_v[part].astype(f32) + error_v[part].astype(f32)).astype(bf16)
        mat[part] = block
        store(column, dot(fac[...], block, 1, 1))


def far_kernel(
    fac_q_h, fac_o_h, grad_q, error_q, grad_o, error_o, mat_q, mat_o, send, *scratch
):
    def store(column, value):
        send[:, column:column + value.shape[1]] = value.astype(bf16)

    project_half(
        1 - parity(), fac_q_h, fac_o_h, grad_q, error_q, grad_o, error_o,
        mat_q, mat_o, store, *scratch
    )


def near_kernel(
    fac_q_h, fac_o_h, grad_q, error_q, grad_o, error_o, norm_grads,
    mat_q, mat_o, part, norm, *scratch
):
    def store(column, value):
        part[:, column:column + value.shape[1]] = value

    project_half(
        parity(), fac_q_h, fac_o_h, grad_q, error_q, grad_o, error_o,
        mat_q, mat_o, store, *scratch
    )
    values = norm_grads[0].astype(f32)
    for row in range(norm.shape[0]):
        norm[row:row + 1, :] = values[:, row * lanes:(row + 1) * lanes]


def project(grad_q, error_q, grad_o, error_o, fac_q, fac_o, norm_grads):
    rank = fac_q.shape[0]
    half_q = (grad_q.shape[0] // 2, grad_q.shape[1])
    half_o = (grad_o.shape[0] // 2, grad_o.shape[1])
    columns = half_q[0] + half_o[0]
    norm_rows = norm_grads.size // lanes
    mats = (pltpu.VMEM(half_q, bf16), pltpu.VMEM(half_o, bf16))
    scratch = [
        pltpu.VMEM(fac_q.shape, bf16),
        pltpu.VMEM(fac_o.shape, bf16),
        pltpu.VMEM(half_q, bf16),
        pltpu.VMEM(half_q, bf16),
        pltpu.VMEM(half_o, bf16),
        pltpu.VMEM(half_o, bf16),
        pltpu.SemaphoreType.DMA((14,)),
    ]
    operands = [
        in_hbm(value) for value in (fac_q, fac_o, grad_q, error_q, grad_o, error_o)
    ]
    effort = cost(2 * rank * (grad_q.size + grad_o.size) // 2, 4 * grad_q.size)
    mat_q_far, mat_o_far, send = pl.pallas_call(
        far_kernel,
        out_shape=mats + (shaped((rank, columns), bf16),),
        in_specs=[in_place] * 6,
        out_specs=(whole,) * 3,
        scratch_shapes=scratch,
        compiler_params=params(16),
        cost_estimate=effort,
        name="project_far",
    )(*operands)
    mat_q_near, mat_o_near, part, norm = pl.pallas_call(
        near_kernel,
        out_shape=mats + (shaped((rank, columns), f32), shaped((norm_rows, lanes), f32)),
        in_specs=[in_place] * 6 + [whole],
        out_specs=(whole,) * 4,
        scratch_shapes=scratch,
        compiler_params=params(16),
        cost_estimate=effort,
        name="project_near",
    )(*operands, norm_grads)
    return mat_q_far, mat_o_far, send, mat_q_near, mat_o_near, part, norm


def small(kernel, name, outs, *operands):
    return pl.pallas_call(
        kernel,
        out_shape=outs,
        in_specs=[whole] * len(operands),
        out_specs=(whole,) * len(outs) if isinstance(outs, tuple) else whole,
        compiler_params=params(8),
        name=name,
    )(*operands)


def tree(parts):
    while len(parts) > 1:
        parts = [parts[place] + parts[place + 1] for place in range(0, len(parts), 2)]
    return parts[0]


def total_of(states, columns):
    return tree([state[:, :columns].astype(f32) for state in states])


def norm_of(states, columns):
    parts = []
    for state in states:
        part = state[:, columns:columns + lanes].astype(f32)
        if state.shape[1] > columns + lanes:
            part = part + state[:, columns + lanes:columns + 2 * lanes].astype(f32)
        parts.append(part)
    return tree(parts)


def store_norm(state, columns, total):
    high = total.astype(bf16)
    state[:, columns:columns + lanes] = high
    state[:, columns + lanes:columns + 2 * lanes] = (total - high.astype(f32)).astype(bf16)


def first_sum_kernel(part, norm, got, state):
    columns = part.shape[1]
    state[:, :columns] = (part[...] + got[...].astype(f32)).astype(bf16)
    state[:, columns:] = norm[...].astype(bf16)


def norm_sum_kernel(columns, *refs):
    *states, out = refs
    out[:, :columns] = total_of(states, columns).astype(bf16)
    store_norm(out, columns, norm_of(states, columns))


def plain_sum_kernel(*refs):
    *states, out = refs
    out[...] = total_of(states, out.shape[1]).astype(bf16)


def hat_kernel(size_q, columns, ginv_q, ginv_o, *refs):
    *states, out = refs
    total = total_of(states, columns)
    highest = lax.Precision.HIGHEST
    out[:, :size_q] = dot(ginv_q[...].T, total[:, :size_q], 1, 0, highest).astype(bf16)
    out[:, size_q:columns] = dot(ginv_o[...].T, total[:, size_q:], 1, 0, highest).astype(bf16)
    store_norm(out, columns, norm_of(states, columns))


def mean_kernel(count, norm, norm_got, *refs):
    *states, new, norm_sum = refs
    new[...] = (total_of(states, new.shape[1]) / count).astype(bf16)
    norm_sum[...] = norm[...] + norm_got[...]


def right_near_kernel(hat, mat_q, mat_o, part_q, part_o):
    size_q, size_o = mat_q.shape[0], mat_o.shape[0]
    part_q[...] = dot(hat[:, :size_q], mat_q[...], 1, 0)
    part_o[...] = dot(hat[:, size_q:size_q + size_o], mat_o[...], 1, 0)


def right_near(hat, mat_q, mat_o):
    rank = hat.shape[0]
    return pl.pallas_call(
        right_near_kernel,
        out_shape=(shaped((rank, mat_q.shape[1]), f32), shaped((rank, mat_o.shape[1]), f32)),
        in_specs=[whole] * 3,
        out_specs=(whole,) * 2,
        compiler_params=params(8),
        cost_estimate=cost(2 * rank * (mat_q.size + mat_o.size), 2 * (mat_q.size + mat_o.size)),
        name="right_near",
    )(hat, in_vmem(mat_q), in_vmem(mat_o))


def right_far_kernel(hat, mat_q, mat_o, part_q, part_o, hat_near, send, near, norm, all_q, all_o):
    size_q, size_o = mat_q.shape[0], mat_o.shape[0]
    all_q[...] = part_q[...] + dot(hat[:, :size_q], mat_q[...], 1, 0)
    all_o[...] = part_o[...] + dot(hat[:, size_q:size_q + size_o], mat_o[...], 1, 0)
    mine = parity()
    half_q, half_o = all_q.shape[1] // 2, all_o.shape[1] // 2
    send[:, :half_q] = all_q[:, half_at(1 - mine, half_q)].astype(bf16)
    send[:, half_q:] = all_o[:, half_at(1 - mine, half_o)].astype(bf16)
    near[:, :half_q] = all_q[:, half_at(mine, half_q)]
    near[:, half_q:] = all_o[:, half_at(mine, half_o)]
    norm[...] = norm_of([hat_near, hat], size_q + size_o)


def right_far(hat, mat_q, mat_o, part_q, part_o, hat_near, norm_rows):
    rank = hat.shape[0]
    columns = (mat_q.shape[1] + mat_o.shape[1]) // 2
    return pl.pallas_call(
        right_far_kernel,
        out_shape=(
            shaped((rank, columns), bf16),
            shaped((rank, columns), f32),
            shaped((norm_rows, lanes), f32),
        ),
        in_specs=[whole] * 6,
        out_specs=(whole,) * 3,
        scratch_shapes=[pltpu.VMEM(part_q.shape, f32), pltpu.VMEM(part_o.shape, f32)],
        compiler_params=params(8),
        cost_estimate=cost(2 * rank * (mat_q.size + mat_o.size), 2 * (mat_q.size + mat_o.size)),
        name="right_far",
    )(hat, in_vmem(mat_q), in_vmem(mat_o), part_q, part_o, hat_near)


def near_sum_kernel(near, got, norm, state, norm_out):
    state[...] = (near[...] + got[...].astype(f32)).astype(bf16)
    norm_out[...] = norm[...]


def error_columns(column, hat, hat_row, half, mat_q, mat_o, new, error_q, error_o, stage_q, stage_o, sems, slot):
    size_q, size_o = mat_q.shape[0], mat_o.shape[0]
    wide_q, wide_o = stage_q.shape[1], stage_o.shape[1]
    copies = []
    chunk_q, chunk_o = size_q // 2, size_o // 2
    cols_q, cols_o = half_at(column, wide_q), half_at(column, wide_o)
    for chunk in range(2):
        part = pl.ds(chunk * chunk_q, chunk_q)
        stage = pl.ds(hat_row * size_q + chunk * chunk_q, chunk_q)
        approx = dot(hat[:, part], new[:, :wide_q], 0, 0)
        stage_q[stage] = (mat_q[part, cols_q].astype(f32) - approx).astype(bf16)
        there = pl.ds(pl.multiple_of(half * size_q + chunk * chunk_q, chunk_q), chunk_q)
        copies.append(load(stage_q.at[stage], error_q.at[there, cols_q], sems.at[slot]))
        part = pl.ds(chunk * chunk_o, chunk_o)
        stage = pl.ds(hat_row * size_o + chunk * chunk_o, chunk_o)
        approx = dot(hat[:, size_q + chunk * chunk_o:size_q + (chunk + 1) * chunk_o], new[:, wide_q:], 0, 0)
        stage_o[stage] = (mat_o[part, cols_o].astype(f32) - approx).astype(bf16)
        there = pl.ds(pl.multiple_of(half * size_o + chunk * chunk_o, chunk_o), chunk_o)
        copies.append(load(stage_o.at[stage], error_o.at[there, cols_o], sems.at[slot + 1]))
        slot += 2
    return copies


def finish_near_kernel(
    hat_near, hat_far, mat_q_near, mat_o_near, mat_q_far, mat_o_far, new,
    error_q, error_o, stage_q, stage_o, sems
):
    mine = parity()
    copies = error_columns(
        mine, hat_near, 0, mine, mat_q_near, mat_o_near, new, error_q, error_o, stage_q, stage_o, sems, 0
    ) + error_columns(
        mine, hat_far, 1, 1 - mine, mat_q_far, mat_o_far, new, error_q, error_o, stage_q, stage_o, sems, 4
    )
    for copy in copies:
        copy.wait()


def piece_of(near, far, index, count, size, pieces):
    half = count // 2
    here = index // half == parity()
    slot = lax.rem(index, half)
    if size % lanes == 0:
        part = half_at(slot, size)
        return jnp.where(here, near[:, part].astype(f32), far[:, part].astype(f32)).astype(bf16)
    width = half * size
    chosen = jnp.where(here, near[:, :width].astype(f32), far[:, :width].astype(f32))
    for place in range(half):
        pieces[place] = chosen[:, place * size:(place + 1) * size]
    return pieces[slot].astype(bf16)


def finish_far_kernel(
    count, norm_count, hat_near, hat_far, mat_q_near, mat_o_near, mat_q_far, mat_o_far,
    new_near, new_far, weight_q, momentum_q, weight_o, momentum_o, norm, norm_got,
    error_q_in, error_o_in,
    error_q, error_o, new_q_h, new_o_h, momentum_q_h, weight_q_h, momentum_o_h, weight_o_h, norm_h,
    stage_q, stage_o, new_q, new_o, momentum_q_new, weight_q_new, momentum_o_new, weight_o_new,
    norm_mean, pieces_q, pieces_o, sems, out_sems
):
    mine = parity()
    me = lax.axis_index("replica")
    wide_q, wide_o = stage_q.shape[1], stage_o.shape[1]
    size_q = mat_q_near.shape[0]
    size_o = mat_o_near.shape[0]
    new_q[:, half_at(mine, wide_q)] = new_near[:, :wide_q]
    new_q[:, half_at(1 - mine, wide_q)] = new_far[:, :wide_q]
    new_o[:, half_at(mine, wide_o)] = new_near[:, wide_q:]
    new_o[:, half_at(1 - mine, wide_o)] = new_far[:, wide_q:]
    norm_mean[...] = (norm[...] + norm_got[...]) / norm_count
    copies = [
        load(new_q, new_q_h, out_sems.at[0]),
        load(new_o, new_o_h, out_sems.at[1]),
        load(norm_mean, norm_h, out_sems.at[2]),
    ]
    copies += error_columns(
        1 - mine, hat_near, 0, mine, mat_q_near, mat_o_near, new_far,
        error_q, error_o, stage_q, stage_o, sems, 0
    )
    piece = piece_of(hat_near, hat_far, me, count, weight_q.shape[0], pieces_q)
    moved = momentum_decay * momentum_q[...] + dot(piece, new_q[...], 0, 0)
    momentum_q_new[...] = moved
    weight_q_new[...] = weight_q[...] - step_size * moved
    copies.append(load(momentum_q_new, momentum_q_h, out_sems.at[3]))
    copies.append(load(weight_q_new, weight_q_h, out_sems.at[4]))
    copies += error_columns(
        1 - mine, hat_far, 1, 1 - mine, mat_q_far, mat_o_far, new_far,
        error_q, error_o, stage_q, stage_o, sems, 4
    )
    piece = piece_of(
        new_near.at[:, wide_q:], new_far.at[:, wide_q:], me, count, weight_o.shape[1], pieces_o
    )
    for which, hat in ((mine, hat_near), (1 - mine, hat_far)):
        rows = half_at(which, size_o)
        moved = momentum_decay * momentum_o[rows] + dot(hat[:, size_q:size_q + size_o], piece, 0, 0)
        momentum_o_new[rows] = moved
        weight_o_new[rows] = weight_o[rows] - step_size * moved
    copies.append(load(momentum_o_new, momentum_o_h, out_sems.at[5]))
    copies.append(load(weight_o_new, weight_o_h, out_sems.at[6]))
    for copy in copies:
        copy.wait()


def finish(
    count, norm_count, hat_near, hat_far, mats, new_near, weights, norm
):
    mat_q, mat_o = mats[0], mats[1]
    weight_q, _, weight_o, _ = weights
    rank = hat_near.shape[0]
    size_q, size_o = mat_q.shape[0], mat_o.shape[0]
    error_q = shaped((2 * size_q, mat_q.shape[1]), bf16)
    error_o = shaped((2 * size_o, mat_o.shape[1]), bf16)
    stages = [
        pltpu.VMEM((2 * size_q, mat_q.shape[1] // 2), bf16),
        pltpu.VMEM((2 * size_o, mat_o.shape[1] // 2), bf16),
    ]
    moved = 4 * (mat_q.size + mat_o.size)
    mats = [in_vmem(mat) for mat in mats]
    new_far = swap(new_near, 1)
    norm_got = swap(norm, 2, "tensor")
    error_q_part, error_o_part = pl.pallas_call(
        finish_near_kernel,
        out_shape=(error_q, error_o),
        in_specs=[whole] * 7,
        out_specs=(in_place,) * 2,
        scratch_shapes=stages + [pltpu.SemaphoreType.DMA((8,))],
        compiler_params=params(12),
        cost_estimate=cost(2 * rank * (mat_q.size + mat_o.size), moved),
        name="finish_near",
    )(hat_near, hat_far, *mats, new_near)
    outs = (
        error_q,
        error_o,
        shaped((rank, mat_q.shape[1]), bf16),
        shaped((rank, mat_o.shape[1]), bf16),
        shaped(weight_q.shape, f32),
        shaped(weight_q.shape, f32),
        shaped(weight_o.shape, f32),
        shaped(weight_o.shape, f32),
        shaped(norm.shape, f32),
    )
    return pl.pallas_call(
        functools.partial(finish_far_kernel, count, norm_count),
        out_shape=outs,
        in_specs=[whole] * 14 + [in_place] * 2,
        out_specs=(in_place,) * len(outs),
        scratch_shapes=stages + [pltpu.VMEM(out.shape, out.dtype) for out in outs[2:]] + [
            pltpu.VMEM((count // 2, rank, weight_q.shape[0]), f32),
            pltpu.VMEM((count // 2, rank, weight_o.shape[1]), f32),
            pltpu.SemaphoreType.DMA((8,)),
            pltpu.SemaphoreType.DMA((7,)),
        ],
        input_output_aliases={14: 0, 15: 1},
        compiler_params=params(16),
        cost_estimate=cost(2 * rank * (mat_q.size + mat_o.size), moved),
        name="finish_far",
    )(
        hat_near, hat_far, *mats, new_near, new_far, *(in_vmem(value) for value in weights),
        norm, norm_got, error_q_part, error_o_part,
    )


def swap(value, bit, axis="replica"):
    count = lax.axis_size(axis)
    return lax.ppermute(value, axis, [(source, source ^ bit) for source in range(count)])


def exchange(state, bits):
    offsets = [0]
    for bit in bits:
        offsets += [offset | bit for offset in offsets]
    got = {0: state}
    for offset in offsets[:0:-1]:
        got[offset] = swap(state, offset)
    return [got[offset] for offset in offsets]


def rounds_of(count):
    bits = [1 << place for place in range(1, count.bit_length() - 1)]
    return [bits[place:place + 2] for place in range(0, len(bits), 2)]


def on_device(
    grad_q,
    error_q,
    qfac_q,
    ginv_q,
    weight_q,
    momentum_q,
    grad_o,
    error_o,
    qfac_o,
    ginv_o,
    weight_o,
    momentum_o,
    norm_grads,
):
    replicas = lax.axis_size("replica")
    tensors = lax.axis_size("tensor")
    rank = qfac_q.shape[1]
    half_q = grad_q.shape[0] // 2
    norm_rows = norm_grads.size // lanes
    mat_q_far, mat_o_far, send, mat_q_near, mat_o_near, part, norm = project(
        grad_q, error_q, grad_o, error_o, qfac_q.T, qfac_o.T, norm_grads
    )
    columns = part.shape[1]
    rounds = rounds_of(replicas)
    state = small(
        first_sum_kernel, "first_sum", shaped((rank, columns + lanes), bf16), part, norm, swap(send, 1)
    )
    wide = shaped((rank, columns + 2 * lanes), bf16)
    for bits in rounds[:-1]:
        state = small(
            functools.partial(norm_sum_kernel, columns), "norm_sum", wide, *exchange(state, bits)
        )
    hat_near = small(
        functools.partial(hat_kernel, half_q, columns), "hats", wide,
        ginv_q, ginv_o, *exchange(state, rounds[-1]),
    )
    hat_far = swap(hat_near, 1)
    part_q, part_o = right_near(hat_near, mat_q_near, mat_o_near)
    send, near, norm = right_far(
        hat_far, mat_q_far, mat_o_far, part_q, part_o, hat_near, norm_rows
    )
    state, norm = small(
        near_sum_kernel, "near_sum", (shaped(send.shape, bf16), shaped(norm.shape, f32)),
        near, swap(send, 1), norm,
    )
    for bits in rounds[:-1]:
        state = small(
            plain_sum_kernel, "plain_sum", shaped(state.shape, bf16), *exchange(state, bits)
        )
    states = exchange(state, rounds[-1])
    new_near, norm = small(
        functools.partial(mean_kernel, replicas), "mean",
        (shaped(state.shape, bf16), shaped(norm.shape, f32)),
        norm, swap(norm, 1, "tensor"), *states,
    )
    (
        error_q_new, error_o_new, new_q, new_o,
        momentum_q_new, weight_q_new, momentum_o_new, weight_o_new, norm_mean,
    ) = finish(
        replicas, replicas * tensors, hat_near, hat_far,
        (mat_q_near, mat_o_near, mat_q_far, mat_o_far), new_near,
        (weight_q, momentum_q, weight_o, momentum_o), norm,
    )
    return (
        error_q_new,
        new_q.T,
        momentum_q_new,
        weight_q_new,
        error_o_new,
        new_o.T,
        momentum_o_new,
        weight_o_new,
        norm_mean.reshape(-1),
    )


def solution(mesh):
    in_specs = (
        P("replica", "tensor"),
        P("replica", "tensor"),
        P("tensor", None),
        P("tensor", None),
        P("replica", "tensor"),
        P("replica", "tensor"),
        P(("replica", "tensor"), None),
        P(("replica", "tensor"), None),
        P("tensor", None),
        P("tensor", None),
        P("tensor", "replica"),
        P("tensor", "replica"),
        P("replica", "tensor", None),
    )
    out_specs = (
        P("replica", "tensor"),
        P("tensor", None),
        P("replica", "tensor"),
        P("replica", "tensor"),
        P(("replica", "tensor"), None),
        P("tensor", None),
        P("tensor", "replica"),
        P("tensor", "replica"),
        P(),
    )
    return jax.shard_map(
        on_device, mesh=mesh, in_specs=in_specs, out_specs=out_specs, check_vma=False
    )
```

```python
import functools

import jax
import jax.numpy as jnp
from jax import lax
from jax.experimental import pallas as pl
from jax.experimental.pallas import tpu as pltpu
from jax.sharding import PartitionSpec as P

momentum_decay = 0.9
step_size = 0.5
lanes = 128
mib = 1024 * 1024
bf16 = jnp.bfloat16
f32 = jnp.float32

whole = pl.BlockSpec(memory_space=pltpu.VMEM)
in_place = pl.BlockSpec(memory_space=pl.ANY)


def dot(left, right, left_dim, right_dim, precision=None):
    return lax.dot_general(
        left,
        right,
        (((left_dim,), (right_dim,)), ((), ())),
        precision=precision,
        preferred_element_type=f32,
    )


def params(limit):
    return pltpu.CompilerParams(vmem_limit_bytes=limit * mib)


def cost(flops, moved):
    return pl.CostEstimate(flops=flops, bytes_accessed=moved, transcendentals=0)


def in_hbm(value):
    return pltpu.with_memory_space_constraint(value, pltpu.HBM)


def in_vmem(value):
    return pltpu.with_memory_space_constraint(value, pltpu.VMEM)


def shaped(shape, dtype):
    return jax.ShapeDtypeStruct(shape, dtype)


def parity():
    replica = lax.axis_index("replica")
    odd = lax.rem(lax.axis_index("tensor"), 2) == 1
    return jnp.where(odd, replica // (lax.axis_size("replica") // 2), lax.rem(replica, 2))


def half_at(which, size):
    return pl.ds(pl.multiple_of(which * size, size), size)


def load(source, target, sem):
    copy = pltpu.make_async_copy(source, target, sem)
    copy.start()
    return copy


def project_half(
    which, fac_q_h, fac_o_h, grad_q, error_q, grad_o, error_o, mat_q, mat_o, store,
    fac_q, fac_o, grad_q_v, error_q_v, grad_o_v, error_o_v, sems,
):
    half_q, half_o = mat_q.shape[0], mat_o.shape[0]
    jobs = []
    fac_copies = [load(fac_q_h, fac_q, sems.at[0]), load(fac_o_h, fac_o, sems.at[1])]
    chunks_q, chunks_o = 4, 2
    rows_q, rows_o = half_q // chunks_q, half_o // chunks_o
    slot = 2
    for chunk in range(chunks_q):
        part = pl.ds(chunk * rows_q, rows_q)
        there = pl.ds(pl.multiple_of(which * half_q + chunk * rows_q, rows_q), rows_q)
        jobs.append((grad_q_v, error_q_v, mat_q, fac_q, part, chunk * rows_q, (
            load(grad_q.at[there], grad_q_v.at[part], sems.at[slot]),
            load(error_q.at[there], error_q_v.at[part], sems.at[slot + 1]),
        )))
        slot += 2
        if chunk % 2 == 0:
            continue
        chunk = chunk // 2
        part = pl.ds(chunk * rows_o, rows_o)
        there = pl.ds(pl.multiple_of(which * half_o + chunk * rows_o, rows_o), rows_o)
        jobs.append((grad_o_v, error_o_v, mat_o, fac_o, part, half_q + chunk * rows_o, (
            load(grad_o.at[there], grad_o_v.at[part], sems.at[slot]),
            load(error_o.at[there], error_o_v.at[part], sems.at[slot + 1]),
        )))
        slot += 2
    for copy in fac_copies:
        copy.wait()
    for grad_v, error_v, mat, fac, part, column, copies in jobs:
        for copy in copies:
            copy.wait()
        block = (grad_v[part].astype(f32) + error_v[part].astype(f32)).astype(bf16)
        mat[part] = block
        store(column, dot(fac[...], block, 1, 1))


def far_kernel(
    fac_q_h, fac_o_h, grad_q, error_q, grad_o, error_o, mat_q, mat_o, send, *scratch
):
    def store(column, value):
        send[:, column:column + value.shape[1]] = value.astype(bf16)

    project_half(
        1 - parity(), fac_q_h, fac_o_h, grad_q, error_q, grad_o, error_o,
        mat_q, mat_o, store, *scratch
    )


def near_kernel(
    fac_q_h, fac_o_h, grad_q, error_q, grad_o, error_o, norm_grads,
    mat_q, mat_o, part, norm, *scratch
):
    def store(column, value):
        part[:, column:column + value.shape[1]] = value

    project_half(
        parity(), fac_q_h, fac_o_h, grad_q, error_q, grad_o, error_o,
        mat_q, mat_o, store, *scratch
    )
    values = norm_grads[0].astype(f32)
    for row in range(norm.shape[0]):
        norm[row:row + 1, :] = values[:, row * lanes:(row + 1) * lanes]


def project(grad_q, error_q, grad_o, error_o, fac_q, fac_o, norm_grads):
    rank = fac_q.shape[0]
    half_q = (grad_q.shape[0] // 2, grad_q.shape[1])
    half_o = (grad_o.shape[0] // 2, grad_o.shape[1])
    columns = half_q[0] + half_o[0]
    norm_rows = norm_grads.size // lanes
    mats = (pltpu.VMEM(half_q, bf16), pltpu.VMEM(half_o, bf16))
    scratch = [
        pltpu.VMEM(fac_q.shape, bf16),
        pltpu.VMEM(fac_o.shape, bf16),
        pltpu.VMEM(half_q, bf16),
        pltpu.VMEM(half_q, bf16),
        pltpu.VMEM(half_o, bf16),
        pltpu.VMEM(half_o, bf16),
        pltpu.SemaphoreType.DMA((14,)),
    ]
    operands = [
        in_hbm(value) for value in (fac_q, fac_o, grad_q, error_q, grad_o, error_o)
    ]
    effort = cost(2 * rank * (grad_q.size + grad_o.size) // 2, 4 * grad_q.size)
    mat_q_far, mat_o_far, send = pl.pallas_call(
        far_kernel,
        out_shape=mats + (shaped((rank, columns), bf16),),
        in_specs=[in_place] * 6,
        out_specs=(whole,) * 3,
        scratch_shapes=scratch,
        compiler_params=params(16),
        cost_estimate=effort,
        name="project_far",
    )(*operands)
    mat_q_near, mat_o_near, part, norm = pl.pallas_call(
        near_kernel,
        out_shape=mats + (shaped((rank, columns), f32), shaped((norm_rows, lanes), f32)),
        in_specs=[in_place] * 6 + [whole],
        out_specs=(whole,) * 4,
        scratch_shapes=scratch,
        compiler_params=params(16),
        cost_estimate=effort,
        name="project_near",
    )(*operands, norm_grads)
    return mat_q_far, mat_o_far, send, mat_q_near, mat_o_near, part, norm


def small(kernel, name, outs, *operands):
    return pl.pallas_call(
        kernel,
        out_shape=outs,
        in_specs=[whole] * len(operands),
        out_specs=(whole,) * len(outs) if isinstance(outs, tuple) else whole,
        compiler_params=params(8),
        name=name,
    )(*operands)


def tree(parts):
    while len(parts) > 1:
        parts = [parts[place] + parts[place + 1] for place in range(0, len(parts), 2)]
    return parts[0]


def total_of(states, columns):
    return tree([state[:, :columns].astype(f32) for state in states])


def norm_of(states, columns):
    parts = []
    for state in states:
        part = state[:, columns:columns + lanes].astype(f32)
        if state.shape[1] > columns + lanes:
            part = part + state[:, columns + lanes:columns + 2 * lanes].astype(f32)
        parts.append(part)
    return tree(parts)


def store_norm(state, columns, total):
    high = total.astype(bf16)
    state[:, columns:columns + lanes] = high
    state[:, columns + lanes:columns + 2 * lanes] = (total - high.astype(f32)).astype(bf16)


def first_sum_kernel(part, norm, got, state):
    columns = part.shape[1]
    state[:, :columns] = (part[...] + got[...].astype(f32)).astype(bf16)
    state[:, columns:] = norm[...].astype(bf16)


def norm_sum_kernel(columns, *refs):
    *states, out = refs
    out[:, :columns] = total_of(states, columns).astype(bf16)
    store_norm(out, columns, norm_of(states, columns))


def plain_sum_kernel(*refs):
    *states, out = refs
    out[...] = total_of(states, out.shape[1]).astype(bf16)


def hat_kernel(size_q, columns, ginv_q, ginv_o, *refs):
    *states, out = refs
    total = total_of(states, columns)
    highest = lax.Precision.HIGHEST
    out[:, :size_q] = dot(ginv_q[...].T, total[:, :size_q], 1, 0, highest).astype(bf16)
    out[:, size_q:columns] = dot(ginv_o[...].T, total[:, size_q:], 1, 0, highest).astype(bf16)
    store_norm(out, columns, norm_of(states, columns))


def mean_kernel(count, norm, norm_got, *refs):
    *states, new, norm_sum = refs
    new[...] = (total_of(states, new.shape[1]) / count).astype(bf16)
    norm_sum[...] = norm[...] + norm_got[...]


def right_near_kernel(hat, mat_q, mat_o, part_q, part_o):
    size_q, size_o = mat_q.shape[0], mat_o.shape[0]
    part_q[...] = dot(hat[:, :size_q], mat_q[...], 1, 0)
    part_o[...] = dot(hat[:, size_q:size_q + size_o], mat_o[...], 1, 0)


def right_near(hat, mat_q, mat_o):
    rank = hat.shape[0]
    return pl.pallas_call(
        right_near_kernel,
        out_shape=(shaped((rank, mat_q.shape[1]), f32), shaped((rank, mat_o.shape[1]), f32)),
        in_specs=[whole] * 3,
        out_specs=(whole,) * 2,
        compiler_params=params(8),
        cost_estimate=cost(2 * rank * (mat_q.size + mat_o.size), 2 * (mat_q.size + mat_o.size)),
        name="right_near",
    )(hat, in_vmem(mat_q), in_vmem(mat_o))


def right_half(which, hat, mat_q, mat_o, part_q, part_o, store):
    size_q, size_o = mat_q.shape[0], mat_o.shape[0]
    half_q, half_o = mat_q.shape[1] // 2, mat_o.shape[1] // 2
    columns = half_at(which, half_q)
    store(0, half_q, part_q[:, columns] + dot(hat[:, :size_q], mat_q[:, columns], 1, 0))
    columns = half_at(which, half_o)
    store(half_q, half_o, part_o[:, columns] + dot(
        hat[:, size_q:size_q + size_o], mat_o[:, columns], 1, 0
    ))


def right_send_kernel(hat, mat_q, mat_o, part_q, part_o, send):
    def store(column, width, value):
        send[:, column:column + width] = value.astype(bf16)

    right_half(1 - parity(), hat, mat_q, mat_o, part_q, part_o, store)


def right_keep_kernel(hat, mat_q, mat_o, part_q, part_o, hat_near, near, norm):
    def store(column, width, value):
        near[:, column:column + width] = value

    right_half(parity(), hat, mat_q, mat_o, part_q, part_o, store)
    norm[...] = norm_of([hat_near, hat], mat_q.shape[0] + mat_o.shape[0])


def right_far(hat, mat_q, mat_o, part_q, part_o, hat_near, norm_rows):
    rank = hat.shape[0]
    columns = (mat_q.shape[1] + mat_o.shape[1]) // 2
    operands = (hat, in_vmem(mat_q), in_vmem(mat_o), part_q, part_o)
    effort = cost(rank * (mat_q.size + mat_o.size), mat_q.size + mat_o.size)
    send = pl.pallas_call(
        right_send_kernel,
        out_shape=shaped((rank, columns), bf16),
        in_specs=[whole] * 5,
        out_specs=whole,
        compiler_params=params(8),
        cost_estimate=effort,
        name="right_send",
    )(*operands)
    near, norm = pl.pallas_call(
        right_keep_kernel,
        out_shape=(shaped((rank, columns), f32), shaped((norm_rows, lanes), f32)),
        in_specs=[whole] * 6,
        out_specs=(whole,) * 2,
        compiler_params=params(8),
        cost_estimate=effort,
        name="right_keep",
    )(*operands, hat_near)
    return send, near, norm


def near_sum_kernel(near, got, norm, state, norm_out):
    state[...] = (near[...] + got[...].astype(f32)).astype(bf16)
    norm_out[...] = norm[...]


def error_columns(column, hat, hat_row, half, mat_q, mat_o, new, error_q, error_o, stage_q, stage_o, sems, slot):
    size_q, size_o = mat_q.shape[0], mat_o.shape[0]
    wide_q, wide_o = stage_q.shape[1], stage_o.shape[1]
    copies = []
    chunk_q, chunk_o = size_q // 2, size_o // 2
    cols_q, cols_o = half_at(column, wide_q), half_at(column, wide_o)
    for chunk in range(2):
        part = pl.ds(chunk * chunk_q, chunk_q)
        stage = pl.ds(hat_row * size_q + chunk * chunk_q, chunk_q)
        approx = dot(hat[:, part], new[:, :wide_q], 0, 0)
        stage_q[stage] = (mat_q[part, cols_q].astype(f32) - approx).astype(bf16)
        there = pl.ds(pl.multiple_of(half * size_q + chunk * chunk_q, chunk_q), chunk_q)
        copies.append(load(stage_q.at[stage], error_q.at[there, cols_q], sems.at[slot]))
        part = pl.ds(chunk * chunk_o, chunk_o)
        stage = pl.ds(hat_row * size_o + chunk * chunk_o, chunk_o)
        approx = dot(hat[:, size_q + chunk * chunk_o:size_q + (chunk + 1) * chunk_o], new[:, wide_q:], 0, 0)
        stage_o[stage] = (mat_o[part, cols_o].astype(f32) - approx).astype(bf16)
        there = pl.ds(pl.multiple_of(half * size_o + chunk * chunk_o, chunk_o), chunk_o)
        copies.append(load(stage_o.at[stage], error_o.at[there, cols_o], sems.at[slot + 1]))
        slot += 2
    return copies


def finish_near_kernel(
    hat_near, hat_far, mat_q_near, mat_o_near, mat_q_far, mat_o_far, new,
    error_q, error_o, stage_q, stage_o, sems
):
    mine = parity()
    copies = error_columns(
        mine, hat_near, 0, mine, mat_q_near, mat_o_near, new, error_q, error_o, stage_q, stage_o, sems, 0
    ) + error_columns(
        mine, hat_far, 1, 1 - mine, mat_q_far, mat_o_far, new, error_q, error_o, stage_q, stage_o, sems, 4
    )
    for copy in copies:
        copy.wait()


def piece_of(near, far, index, count, size, pieces):
    half = count // 2
    here = index // half == parity()
    slot = lax.rem(index, half)
    if size % lanes == 0:
        part = half_at(slot, size)
        return jnp.where(here, near[:, part].astype(f32), far[:, part].astype(f32)).astype(bf16)
    width = half * size
    chosen = jnp.where(here, near[:, :width].astype(f32), far[:, :width].astype(f32))
    for place in range(half):
        pieces[place] = chosen[:, place * size:(place + 1) * size]
    return pieces[slot].astype(bf16)


def finish_far_kernel(
    count, norm_count, hat_near, hat_far, mat_q_near, mat_o_near, mat_q_far, mat_o_far,
    new_near, new_far, weight_q, momentum_q, weight_o, momentum_o, norm, norm_got,
    error_q_in, error_o_in,
    error_q, error_o, new_q_h, new_o_h, momentum_q_h, weight_q_h, momentum_o_h, weight_o_h, norm_h,
    stage_q, stage_o, new_q, new_o, momentum_q_new, weight_q_new, momentum_o_new, weight_o_new,
    norm_mean, pieces_q, pieces_o, sems, out_sems
):
    mine = parity()
    me = lax.axis_index("replica")
    wide_q, wide_o = stage_q.shape[1], stage_o.shape[1]
    size_q = mat_q_near.shape[0]
    size_o = mat_o_near.shape[0]
    new_q[:, half_at(mine, wide_q)] = new_near[:, :wide_q]
    new_q[:, half_at(1 - mine, wide_q)] = new_far[:, :wide_q]
    new_o[:, half_at(mine, wide_o)] = new_near[:, wide_q:]
    new_o[:, half_at(1 - mine, wide_o)] = new_far[:, wide_q:]
    norm_mean[...] = (norm[...] + norm_got[...]) / norm_count
    copies = [
        load(new_q, new_q_h, out_sems.at[0]),
        load(new_o, new_o_h, out_sems.at[1]),
        load(norm_mean, norm_h, out_sems.at[2]),
    ]
    copies += error_columns(
        1 - mine, hat_near, 0, mine, mat_q_near, mat_o_near, new_far,
        error_q, error_o, stage_q, stage_o, sems, 0
    )
    piece = piece_of(hat_near, hat_far, me, count, weight_q.shape[0], pieces_q)
    moved = momentum_decay * momentum_q[...] + dot(piece, new_q[...], 0, 0)
    momentum_q_new[...] = moved
    weight_q_new[...] = weight_q[...] - step_size * moved
    copies.append(load(momentum_q_new, momentum_q_h, out_sems.at[3]))
    copies.append(load(weight_q_new, weight_q_h, out_sems.at[4]))
    copies += error_columns(
        1 - mine, hat_far, 1, 1 - mine, mat_q_far, mat_o_far, new_far,
        error_q, error_o, stage_q, stage_o, sems, 4
    )
    piece = piece_of(
        new_near.at[:, wide_q:], new_far.at[:, wide_q:], me, count, weight_o.shape[1], pieces_o
    )
    for which, hat in ((mine, hat_near), (1 - mine, hat_far)):
        rows = half_at(which, size_o)
        moved = momentum_decay * momentum_o[rows] + dot(hat[:, size_q:size_q + size_o], piece, 0, 0)
        momentum_o_new[rows] = moved
        weight_o_new[rows] = weight_o[rows] - step_size * moved
    copies.append(load(momentum_o_new, momentum_o_h, out_sems.at[5]))
    copies.append(load(weight_o_new, weight_o_h, out_sems.at[6]))
    for copy in copies:
        copy.wait()


def finish(
    count, norm_count, hat_near, hat_far, mats, new_near, weights, norm
):
    mat_q, mat_o = mats[0], mats[1]
    weight_q, _, weight_o, _ = weights
    rank = hat_near.shape[0]
    size_q, size_o = mat_q.shape[0], mat_o.shape[0]
    error_q = shaped((2 * size_q, mat_q.shape[1]), bf16)
    error_o = shaped((2 * size_o, mat_o.shape[1]), bf16)
    stages = [
        pltpu.VMEM((2 * size_q, mat_q.shape[1] // 2), bf16),
        pltpu.VMEM((2 * size_o, mat_o.shape[1] // 2), bf16),
    ]
    moved = 4 * (mat_q.size + mat_o.size)
    mats = [in_vmem(mat) for mat in mats]
    new_far = swap_halves(new_near)
    norm_got = swap_tensor(norm, 2)
    error_q_part, error_o_part = pl.pallas_call(
        finish_near_kernel,
        out_shape=(error_q, error_o),
        in_specs=[whole] * 7,
        out_specs=(in_place,) * 2,
        scratch_shapes=stages + [pltpu.SemaphoreType.DMA((8,))],
        compiler_params=params(12),
        cost_estimate=cost(2 * rank * (mat_q.size + mat_o.size), moved),
        name="finish_near",
    )(hat_near, hat_far, *mats, new_near)
    outs = (
        error_q,
        error_o,
        shaped((rank, mat_q.shape[1]), bf16),
        shaped((rank, mat_o.shape[1]), bf16),
        shaped(weight_q.shape, f32),
        shaped(weight_q.shape, f32),
        shaped(weight_o.shape, f32),
        shaped(weight_o.shape, f32),
        shaped(norm.shape, f32),
    )
    return pl.pallas_call(
        functools.partial(finish_far_kernel, count, norm_count),
        out_shape=outs,
        in_specs=[whole] * 14 + [in_place] * 2,
        out_specs=(in_place,) * len(outs),
        scratch_shapes=stages + [pltpu.VMEM(out.shape, out.dtype) for out in outs[2:]] + [
            pltpu.VMEM((count // 2, rank, weight_q.shape[0]), f32),
            pltpu.VMEM((count // 2, rank, weight_o.shape[1]), f32),
            pltpu.SemaphoreType.DMA((8,)),
            pltpu.SemaphoreType.DMA((7,)),
        ],
        input_output_aliases={14: 0, 15: 1},
        compiler_params=params(16),
        cost_estimate=cost(2 * rank * (mat_q.size + mat_o.size), moved),
        name="finish_far",
    )(
        hat_near, hat_far, *mats, new_near, new_far, *(in_vmem(value) for value in weights),
        norm, norm_got, error_q_part, error_o_part,
    )


def swap(value, even, odd):
    replicas, tensors = lax.axis_size("replica"), lax.axis_size("tensor")
    pairs = []
    for replica in range(replicas):
        for tensor in range(tensors):
            target = replica ^ (odd if tensor % 2 else even)
            pairs.append((replica * tensors + tensor, target * tensors + tensor))
    return lax.ppermute(value, ("replica", "tensor"), pairs)


def swap_halves(value):
    return swap(value, 1, lax.axis_size("replica") // 2)


def swap_tensor(value, bit):
    count = lax.axis_size("tensor")
    return lax.ppermute(value, "tensor", [(source, source ^ bit) for source in range(count)])


def exchange(state, bits):
    offsets = [(0, 0)]
    for even, odd in bits:
        offsets += [(first | even, second | odd) for first, second in offsets]
    got = [swap(state, *offset) for offset in offsets[:0:-1]]
    return [state] + got[::-1]


def rounds_of(count):
    places = range(1, count.bit_length() - 1)
    bits = [(1 << place, 1 << (place - 1)) for place in places]
    return [bits[place:place + 2] for place in range(0, len(bits), 2)]


def on_device(
    grad_q,
    error_q,
    qfac_q,
    ginv_q,
    weight_q,
    momentum_q,
    grad_o,
    error_o,
    qfac_o,
    ginv_o,
    weight_o,
    momentum_o,
    norm_grads,
):
    replicas = lax.axis_size("replica")
    tensors = lax.axis_size("tensor")
    rank = qfac_q.shape[1]
    half_q = grad_q.shape[0] // 2
    norm_rows = norm_grads.size // lanes
    mat_q_far, mat_o_far, send, mat_q_near, mat_o_near, part, norm = project(
        grad_q, error_q, grad_o, error_o, qfac_q.T, qfac_o.T, norm_grads
    )
    columns = part.shape[1]
    rounds = rounds_of(replicas)
    state = small(
        first_sum_kernel, "first_sum", shaped((rank, columns + lanes), bf16), part, norm, swap_halves(send)
    )
    wide = shaped((rank, columns + 2 * lanes), bf16)
    for bits in rounds[:-1]:
        state = small(
            functools.partial(norm_sum_kernel, columns), "norm_sum", wide, *exchange(state, bits)
        )
    hat_near = small(
        functools.partial(hat_kernel, half_q, columns), "hats", wide,
        ginv_q, ginv_o, *exchange(state, rounds[-1]),
    )
    hat_far = swap_halves(hat_near)
    part_q, part_o = right_near(hat_near, mat_q_near, mat_o_near)
    send, near, norm = right_far(
        hat_far, mat_q_far, mat_o_far, part_q, part_o, hat_near, norm_rows
    )
    state, norm = small(
        near_sum_kernel, "near_sum", (shaped(send.shape, bf16), shaped(norm.shape, f32)),
        near, swap_halves(send), norm,
    )
    for bits in rounds[:-1]:
        state = small(
            plain_sum_kernel, "plain_sum", shaped(state.shape, bf16), *exchange(state, bits)
        )
    states = exchange(state, rounds[-1])
    new_near, norm = small(
        functools.partial(mean_kernel, replicas), "mean",
        (shaped(state.shape, bf16), shaped(norm.shape, f32)),
        norm, swap_tensor(norm, 1), *states,
    )
    (
        error_q_new, error_o_new, new_q, new_o,
        momentum_q_new, weight_q_new, momentum_o_new, weight_o_new, norm_mean,
    ) = finish(
        replicas, replicas * tensors, hat_near, hat_far,
        (mat_q_near, mat_o_near, mat_q_far, mat_o_far), new_near,
        (weight_q, momentum_q, weight_o, momentum_o), norm,
    )
    return (
        error_q_new,
        new_q.T,
        momentum_q_new,
        weight_q_new,
        error_o_new,
        new_o.T,
        momentum_o_new,
        weight_o_new,
        norm_mean.reshape(-1),
    )


def solution(mesh):
    in_specs = (
        P("replica", "tensor"),
        P("replica", "tensor"),
        P("tensor", None),
        P("tensor", None),
        P("replica", "tensor"),
        P("replica", "tensor"),
        P(("replica", "tensor"), None),
        P(("replica", "tensor"), None),
        P("tensor", None),
        P("tensor", None),
        P("tensor", "replica"),
        P("tensor", "replica"),
        P("replica", "tensor", None),
    )
    out_specs = (
        P("replica", "tensor"),
        P("tensor", None),
        P("replica", "tensor"),
        P("replica", "tensor"),
        P(("replica", "tensor"), None),
        P("tensor", None),
        P("tensor", "replica"),
        P("tensor", "replica"),
        P(),
    )
    return jax.shard_map(
        on_device, mesh=mesh, in_specs=in_specs, out_specs=out_specs, check_vma=False
    )
```

```python
import functools

import jax
import jax.numpy as jnp
from jax import lax
from jax.experimental import pallas as pl
from jax.experimental.pallas import tpu as pltpu
from jax.sharding import PartitionSpec as P

momentum_decay = 0.9
step_size = 0.5
lanes = 128
mib = 1024 * 1024
bf16 = jnp.bfloat16
f32 = jnp.float32

whole = pl.BlockSpec(memory_space=pltpu.VMEM)
in_place = pl.BlockSpec(memory_space=pl.ANY)


def dot(left, right, left_dim, right_dim, precision=None):
    return lax.dot_general(
        left,
        right,
        (((left_dim,), (right_dim,)), ((), ())),
        precision=precision,
        preferred_element_type=f32,
    )


def params(limit):
    return pltpu.CompilerParams(vmem_limit_bytes=limit * mib)


def cost(flops, moved):
    return pl.CostEstimate(flops=flops, bytes_accessed=moved, transcendentals=0)


def in_hbm(value):
    return pltpu.with_memory_space_constraint(value, pltpu.HBM)


def in_vmem(value):
    return pltpu.with_memory_space_constraint(value, pltpu.VMEM)


def shaped(shape, dtype):
    return jax.ShapeDtypeStruct(shape, dtype)


def parity():
    replica = lax.axis_index("replica")
    odd = lax.rem(lax.axis_index("tensor"), 2) == 1
    return jnp.where(odd, replica // (lax.axis_size("replica") // 2), lax.rem(replica, 2))


def half_at(which, size):
    return pl.ds(pl.multiple_of(which * size, size), size)


def load(source, target, sem):
    copy = pltpu.make_async_copy(source, target, sem)
    copy.start()
    return copy


def project_half(
    which, fac_q_h, fac_o_h, grad_q, error_q, grad_o, error_o, mat_q, mat_o, store,
    fac_q, fac_o, grad_q_v, error_q_v, grad_o_v, error_o_v, sems,
):
    half_q, half_o = mat_q.shape[0], mat_o.shape[0]
    jobs = []
    fac_copies = [load(fac_q_h, fac_q, sems.at[0]), load(fac_o_h, fac_o, sems.at[1])]
    chunks_q, chunks_o = 4, 2
    rows_q, rows_o = half_q // chunks_q, half_o // chunks_o
    slot = 2
    for chunk in range(chunks_q):
        part = pl.ds(chunk * rows_q, rows_q)
        there = pl.ds(pl.multiple_of(which * half_q + chunk * rows_q, rows_q), rows_q)
        jobs.append((grad_q_v, error_q_v, mat_q, fac_q, part, chunk * rows_q, (
            load(grad_q.at[there], grad_q_v.at[part], sems.at[slot]),
            load(error_q.at[there], error_q_v.at[part], sems.at[slot + 1]),
        )))
        slot += 2
        if chunk % 2 == 0:
            continue
        chunk = chunk // 2
        part = pl.ds(chunk * rows_o, rows_o)
        there = pl.ds(pl.multiple_of(which * half_o + chunk * rows_o, rows_o), rows_o)
        jobs.append((grad_o_v, error_o_v, mat_o, fac_o, part, half_q + chunk * rows_o, (
            load(grad_o.at[there], grad_o_v.at[part], sems.at[slot]),
            load(error_o.at[there], error_o_v.at[part], sems.at[slot + 1]),
        )))
        slot += 2
    for copy in fac_copies:
        copy.wait()
    for grad_v, error_v, mat, fac, part, column, copies in jobs:
        for copy in copies:
            copy.wait()
        block = grad_v[part] + error_v[part]
        mat[part] = block
        store(column, dot(block, fac[...], 1, 1).T)


def far_kernel(
    fac_q_h, fac_o_h, grad_q, error_q, grad_o, error_o, mat_q, mat_o, send, *scratch
):
    def store(column, value):
        send[:, column:column + value.shape[1]] = value.astype(bf16)

    project_half(
        1 - parity(), fac_q_h, fac_o_h, grad_q, error_q, grad_o, error_o,
        mat_q, mat_o, store, *scratch
    )


def near_kernel(
    fac_q_h, fac_o_h, grad_q, error_q, grad_o, error_o, norm_grads,
    mat_q, mat_o, part, norm, *scratch
):
    def store(column, value):
        part[:, column:column + value.shape[1]] = value

    project_half(
        parity(), fac_q_h, fac_o_h, grad_q, error_q, grad_o, error_o,
        mat_q, mat_o, store, *scratch
    )
    values = norm_grads[0].astype(f32)
    for row in range(norm.shape[0]):
        norm[row:row + 1, :] = values[:, row * lanes:(row + 1) * lanes]


def project(grad_q, error_q, grad_o, error_o, fac_q, fac_o, norm_grads):
    rank = fac_q.shape[0]
    half_q = (grad_q.shape[0] // 2, grad_q.shape[1])
    half_o = (grad_o.shape[0] // 2, grad_o.shape[1])
    columns = half_q[0] + half_o[0]
    norm_rows = norm_grads.size // lanes
    mats = (pltpu.VMEM(half_q, bf16), pltpu.VMEM(half_o, bf16))
    scratch = [
        pltpu.VMEM(fac_q.shape, bf16),
        pltpu.VMEM(fac_o.shape, bf16),
        pltpu.VMEM(half_q, bf16),
        pltpu.VMEM(half_q, bf16),
        pltpu.VMEM(half_o, bf16),
        pltpu.VMEM(half_o, bf16),
        pltpu.SemaphoreType.DMA((14,)),
    ]
    operands = [
        in_hbm(value) for value in (fac_q, fac_o, grad_q, error_q, grad_o, error_o)
    ]
    effort = cost(2 * rank * (grad_q.size + grad_o.size) // 2, 4 * grad_q.size)
    mat_q_far, mat_o_far, send = pl.pallas_call(
        far_kernel,
        out_shape=mats + (shaped((rank, columns), bf16),),
        in_specs=[in_place] * 6,
        out_specs=(whole,) * 3,
        scratch_shapes=scratch,
        compiler_params=params(16),
        cost_estimate=effort,
        name="project_far",
    )(*operands)
    mat_q_near, mat_o_near, part, norm = pl.pallas_call(
        near_kernel,
        out_shape=mats + (shaped((rank, columns), f32), shaped((norm_rows, lanes), f32)),
        in_specs=[in_place] * 6 + [whole],
        out_specs=(whole,) * 4,
        scratch_shapes=scratch,
        compiler_params=params(16),
        cost_estimate=effort,
        name="project_near",
    )(*operands, norm_grads)
    return mat_q_far, mat_o_far, send, mat_q_near, mat_o_near, part, norm


def small(kernel, name, outs, *operands):
    return pl.pallas_call(
        kernel,
        out_shape=outs,
        in_specs=[whole] * len(operands),
        out_specs=(whole,) * len(outs) if isinstance(outs, tuple) else whole,
        compiler_params=params(8),
        name=name,
    )(*operands)


def tree(parts):
    while len(parts) > 1:
        parts = [parts[place] + parts[place + 1] for place in range(0, len(parts), 2)]
    return parts[0]


def total_of(states, columns):
    return tree([state[:, :columns].astype(f32) for state in states])


def norm_of(states, columns):
    parts = []
    for state in states:
        part = state[:, columns:columns + lanes].astype(f32)
        if state.shape[1] > columns + lanes:
            part = part + state[:, columns + lanes:columns + 2 * lanes].astype(f32)
        parts.append(part)
    return tree(parts)


def store_norm(state, columns, total):
    high = total.astype(bf16)
    state[:, columns:columns + lanes] = high
    state[:, columns + lanes:columns + 2 * lanes] = (total - high.astype(f32)).astype(bf16)


def first_sum_kernel(part, norm, got, state):
    columns = part.shape[1]
    state[:, :columns] = (part[...] + got[...].astype(f32)).astype(bf16)
    state[:, columns:] = norm[...].astype(bf16)


def norm_sum_kernel(columns, *refs):
    *states, out = refs
    out[:, :columns] = total_of(states, columns).astype(bf16)
    store_norm(out, columns, norm_of(states, columns))


def plain_sum_kernel(*refs):
    *states, out = refs
    out[...] = total_of(states, out.shape[1]).astype(bf16)


def hat_kernel(size_q, columns, ginv_q, ginv_o, *refs):
    *states, out = refs
    total = total_of(states, columns)
    highest = lax.Precision.HIGHEST
    out[:, :size_q] = dot(ginv_q[...].T, total[:, :size_q], 1, 0, highest).astype(bf16)
    out[:, size_q:columns] = dot(ginv_o[...].T, total[:, size_q:], 1, 0, highest).astype(bf16)
    store_norm(out, columns, norm_of(states, columns))


def norm_add_kernel(mine, got, total):
    total[...] = mine[...] + got[...]


def mean_kernel(count, norm_count, norm, norm_got, *refs):
    *states, new, norm_mean = refs
    new[...] = (total_of(states, new.shape[1]) / count).astype(bf16)
    norm_mean[...] = (norm[...] + norm_got[...]) / norm_count


def right_near_kernel(hat, mat_q, mat_o, part_q, part_o):
    size_q, size_o = mat_q.shape[0], mat_o.shape[0]
    part_q[...] = dot(hat[:, :size_q], mat_q[...], 1, 0)
    part_o[...] = dot(hat[:, size_q:size_q + size_o], mat_o[...], 1, 0)


def right_near(hat, mat_q, mat_o):
    rank = hat.shape[0]
    return pl.pallas_call(
        right_near_kernel,
        out_shape=(shaped((rank, mat_q.shape[1]), f32), shaped((rank, mat_o.shape[1]), f32)),
        in_specs=[whole] * 3,
        out_specs=(whole,) * 2,
        compiler_params=params(8),
        cost_estimate=cost(2 * rank * (mat_q.size + mat_o.size), 2 * (mat_q.size + mat_o.size)),
        name="right_near",
    )(hat, in_vmem(mat_q), in_vmem(mat_o))


def right_half(which, hat, mat_q, mat_o, part_q, part_o, store):
    size_q, size_o = mat_q.shape[0], mat_o.shape[0]
    half_q, half_o = mat_q.shape[1] // 2, mat_o.shape[1] // 2
    columns = half_at(which, half_q)
    store(0, half_q, part_q[:, columns] + dot(hat[:, :size_q], mat_q[:, columns], 1, 0))
    columns = half_at(which, half_o)
    store(half_q, half_o, part_o[:, columns] + dot(
        hat[:, size_q:size_q + size_o], mat_o[:, columns], 1, 0
    ))


def right_send_kernel(hat, mat_q, mat_o, part_q, part_o, send):
    def store(column, width, value):
        send[:, column:column + width] = value.astype(bf16)

    right_half(1 - parity(), hat, mat_q, mat_o, part_q, part_o, store)


def right_keep_kernel(hat, mat_q, mat_o, part_q, part_o, hat_near, near, norm):
    def store(column, width, value):
        near[:, column:column + width] = value

    right_half(parity(), hat, mat_q, mat_o, part_q, part_o, store)
    norm[...] = norm_of([hat_near, hat], mat_q.shape[0] + mat_o.shape[0])


def right_far(hat, mat_q, mat_o, part_q, part_o, hat_near, norm_rows):
    rank = hat.shape[0]
    columns = (mat_q.shape[1] + mat_o.shape[1]) // 2
    operands = (hat, in_vmem(mat_q), in_vmem(mat_o), part_q, part_o)
    effort = cost(rank * (mat_q.size + mat_o.size), mat_q.size + mat_o.size)
    send = pl.pallas_call(
        right_send_kernel,
        out_shape=shaped((rank, columns), bf16),
        in_specs=[whole] * 5,
        out_specs=whole,
        compiler_params=params(8),
        cost_estimate=effort,
        name="right_send",
    )(*operands)
    near, norm = pl.pallas_call(
        right_keep_kernel,
        out_shape=(shaped((rank, columns), f32), shaped((norm_rows, lanes), f32)),
        in_specs=[whole] * 6,
        out_specs=(whole,) * 2,
        compiler_params=params(8),
        cost_estimate=effort,
        name="right_keep",
    )(*operands, hat_near)
    return send, near, norm


def near_sum_kernel(near, got, norm, state, norm_out):
    state[...] = (near[...] + got[...].astype(f32)).astype(bf16)
    norm_out[...] = norm[...]


def error_columns(column, hat, hat_row, half, mat_q, mat_o, new, error_q, error_o, stage_q, stage_o, sems, slot):
    size_q, size_o = mat_q.shape[0], mat_o.shape[0]
    wide_q, wide_o = stage_q.shape[1], stage_o.shape[1]
    copies = []
    chunk_q, chunk_o = size_q // 2, size_o // 2
    cols_q, cols_o = half_at(column, wide_q), half_at(column, wide_o)
    for chunk in range(2):
        part = pl.ds(chunk * chunk_q, chunk_q)
        stage = pl.ds(hat_row * size_q + chunk * chunk_q, chunk_q)
        approx = dot(hat[:, part], new[:, :wide_q], 0, 0)
        stage_q[stage] = (mat_q[part, cols_q].astype(f32) - approx).astype(bf16)
        there = pl.ds(pl.multiple_of(half * size_q + chunk * chunk_q, chunk_q), chunk_q)
        copies.append(load(stage_q.at[stage], error_q.at[there, cols_q], sems.at[slot]))
        part = pl.ds(chunk * chunk_o, chunk_o)
        stage = pl.ds(hat_row * size_o + chunk * chunk_o, chunk_o)
        approx = dot(hat[:, size_q + chunk * chunk_o:size_q + (chunk + 1) * chunk_o], new[:, wide_q:], 0, 0)
        stage_o[stage] = (mat_o[part, cols_o].astype(f32) - approx).astype(bf16)
        there = pl.ds(pl.multiple_of(half * size_o + chunk * chunk_o, chunk_o), chunk_o)
        copies.append(load(stage_o.at[stage], error_o.at[there, cols_o], sems.at[slot + 1]))
        slot += 2
    return copies


def piece_of(near, far, index, count, size, pieces):
    half = count // 2
    here = index // half == parity()
    slot = lax.rem(index, half)
    if size % lanes == 0:
        part = half_at(slot, size)
        return jnp.where(here, near[:, part].astype(f32), far[:, part].astype(f32)).astype(bf16)
    width = half * size
    chosen = jnp.where(here, near[:, :width].astype(f32), far[:, :width].astype(f32))
    for place in range(half):
        pieces[place] = chosen[:, place * size:(place + 1) * size]
    return pieces[slot].astype(bf16)


def finish_near_kernel(
    count, hat_near, hat_far, mat_q_near, mat_o_near, mat_q_far, mat_o_far, new, weight_q, momentum_q,
    error_q, error_o, momentum_q_h, weight_q_h,
    stage_q, stage_o, momentum_q_new, weight_q_new, pieces, sems, out_sems
):
    mine = parity()
    me = lax.axis_index("replica")
    copies = error_columns(
        mine, hat_near, 0, mine, mat_q_near, mat_o_near, new, error_q, error_o, stage_q, stage_o, sems, 0
    ) + error_columns(
        mine, hat_far, 1, 1 - mine, mat_q_far, mat_o_far, new, error_q, error_o, stage_q, stage_o, sems, 4
    )
    piece = piece_of(hat_near, hat_far, me, count, weight_q.shape[0], pieces)
    copies += query_columns(
        mine, piece, new, weight_q, momentum_q, momentum_q_new, weight_q_new,
        momentum_q_h, weight_q_h, out_sems
    )
    for copy in copies:
        copy.wait()


def query_columns(
    which, piece, new, weight, momentum, momentum_new, weight_new, momentum_h, weight_h, sems
):
    wide = momentum_new.shape[1]
    columns = half_at(which, wide)
    moved = momentum_decay * momentum[:, columns] + dot(piece, new[:, :wide], 0, 0)
    momentum_new[...] = moved
    weight_new[...] = weight[:, columns] - step_size * moved
    return [
        load(momentum_new, momentum_h.at[:, columns], sems.at[0]),
        load(weight_new, weight_h.at[:, columns], sems.at[1]),
    ]


def finish_far_kernel(
    count, hat_near, hat_far, mat_q_near, mat_o_near, mat_q_far, mat_o_far,
    new_near, new_far, weight_q, momentum_q, weight_o, momentum_o, norm,
    error_q_in, error_o_in, momentum_q_in, weight_q_in,
    error_q, error_o, momentum_q_h, weight_q_h, new_q_h, new_o_h, momentum_o_h, weight_o_h, norm_h,
    stage_q, stage_o, momentum_q_new, weight_q_new, new_q, new_o, momentum_o_new, weight_o_new,
    pieces_q, pieces_o, sems, out_sems
):
    mine = parity()
    me = lax.axis_index("replica")
    wide_q, wide_o = stage_q.shape[1], stage_o.shape[1]
    size_q = mat_q_near.shape[0]
    size_o = mat_o_near.shape[0]
    new_q[:, half_at(mine, wide_q)] = new_near[:, :wide_q]
    new_q[:, half_at(1 - mine, wide_q)] = new_far[:, :wide_q]
    new_o[:, half_at(mine, wide_o)] = new_near[:, wide_q:]
    new_o[:, half_at(1 - mine, wide_o)] = new_far[:, wide_q:]
    copies = [
        load(new_q, new_q_h, out_sems.at[0]),
        load(new_o, new_o_h, out_sems.at[1]),
        load(norm, norm_h, out_sems.at[2]),
    ]
    copies += error_columns(
        1 - mine, hat_near, 0, mine, mat_q_near, mat_o_near, new_far,
        error_q, error_o, stage_q, stage_o, sems, 0
    )
    piece = piece_of(
        new_near.at[:, wide_q:], new_far.at[:, wide_q:], me, count, weight_o.shape[1], pieces_o
    )
    for which, hat in ((mine, hat_near), (1 - mine, hat_far)):
        rows = half_at(which, size_o)
        moved = momentum_decay * momentum_o[rows] + dot(hat[:, size_q:size_q + size_o], piece, 0, 0)
        momentum_o_new[rows] = moved
        weight_o_new[rows] = weight_o[rows] - step_size * moved
    copies.append(load(momentum_o_new, momentum_o_h, out_sems.at[3]))
    copies.append(load(weight_o_new, weight_o_h, out_sems.at[4]))
    copies += error_columns(
        1 - mine, hat_far, 1, 1 - mine, mat_q_far, mat_o_far, new_far,
        error_q, error_o, stage_q, stage_o, sems, 4
    )
    piece = piece_of(hat_near, hat_far, me, count, weight_q.shape[0], pieces_q)
    copies += query_columns(
        1 - mine, piece, new_far, weight_q, momentum_q, momentum_q_new, weight_q_new,
        momentum_q_h, weight_q_h, out_sems.at[5:7]
    )
    for copy in copies:
        copy.wait()


def finish(count, hat_near, hat_far, mats, new_near, weights, norm):
    mat_q, mat_o = mats[0], mats[1]
    weight_q, _, weight_o, _ = weights
    rank = hat_near.shape[0]
    size_q, size_o = mat_q.shape[0], mat_o.shape[0]
    early = (
        shaped((2 * size_q, mat_q.shape[1]), bf16),
        shaped((2 * size_o, mat_o.shape[1]), bf16),
        shaped(weight_q.shape, f32),
        shaped(weight_q.shape, f32),
    )
    late = (
        shaped((rank, mat_q.shape[1]), bf16),
        shaped((rank, mat_o.shape[1]), bf16),
        shaped(weight_o.shape, f32),
        shaped(weight_o.shape, f32),
    )
    piece_q = (weight_q.shape[0], weight_q.shape[1] // 2)
    stages = [
        pltpu.VMEM((2 * size_q, mat_q.shape[1] // 2), bf16),
        pltpu.VMEM((2 * size_o, mat_o.shape[1] // 2), bf16),
        pltpu.VMEM(piece_q, f32),
        pltpu.VMEM(piece_q, f32),
    ]
    pieces_q = pltpu.VMEM((count // 2, rank, weight_q.shape[0]), f32)
    pieces_o = pltpu.VMEM((count // 2, rank, weight_o.shape[1]), f32)
    moved = 4 * (mat_q.size + mat_o.size)
    mats = [in_vmem(mat) for mat in mats]
    weights = [in_vmem(value) for value in weights]
    new_far = swap_halves(new_near)
    parts = pl.pallas_call(
        functools.partial(finish_near_kernel, count),
        out_shape=early,
        in_specs=[whole] * 9,
        out_specs=(in_place,) * 4,
        scratch_shapes=stages + [
            pieces_q, pltpu.SemaphoreType.DMA((8,)), pltpu.SemaphoreType.DMA((2,))
        ],
        compiler_params=params(12),
        cost_estimate=cost(2 * rank * (mat_q.size + mat_o.size), moved),
        name="finish_near",
    )(hat_near, hat_far, *mats, new_near, *weights[:2])
    return pl.pallas_call(
        functools.partial(finish_far_kernel, count),
        out_shape=early + late + (shaped(norm.shape, f32),),
        in_specs=[whole] * 13 + [in_place] * 4,
        out_specs=(in_place,) * 9,
        scratch_shapes=stages + [pltpu.VMEM(out.shape, out.dtype) for out in late] + [
            pieces_q, pieces_o, pltpu.SemaphoreType.DMA((8,)), pltpu.SemaphoreType.DMA((7,))
        ],
        input_output_aliases={13: 0, 14: 1, 15: 2, 16: 3},
        compiler_params=params(16),
        cost_estimate=cost(2 * rank * (mat_q.size + mat_o.size), moved),
        name="finish_far",
    )(hat_near, hat_far, *mats, new_near, new_far, *weights, norm, *parts)


def swap(value, even, odd):
    replicas, tensors = lax.axis_size("replica"), lax.axis_size("tensor")
    pairs = []
    for replica in range(replicas):
        for tensor in range(tensors):
            target = replica ^ (odd if tensor % 2 else even)
            pairs.append((replica * tensors + tensor, target * tensors + tensor))
    return lax.ppermute(value, ("replica", "tensor"), pairs)


def swap_halves(value):
    return swap(value, 1, lax.axis_size("replica") // 2)


def swap_tensor(value, bit):
    count = lax.axis_size("tensor")
    return lax.ppermute(value, "tensor", [(source, source ^ bit) for source in range(count)])


def exchange(state, bits):
    offsets = [(0, 0)]
    for even, odd in bits:
        offsets += [(first | even, second | odd) for first, second in offsets]
    got = [swap(state, *offset) for offset in offsets[:0:-1]]
    return [state] + got[::-1]


def rounds_of(count):
    places = range(1, count.bit_length() - 1)
    bits = [(1 << place, 1 << (place - 1)) for place in places]
    return [bits[place:place + 2] for place in range(0, len(bits), 2)]


def on_device(
    grad_q,
    error_q,
    qfac_q,
    ginv_q,
    weight_q,
    momentum_q,
    grad_o,
    error_o,
    qfac_o,
    ginv_o,
    weight_o,
    momentum_o,
    norm_grads,
):
    replicas = lax.axis_size("replica")
    tensors = lax.axis_size("tensor")
    rank = qfac_q.shape[1]
    half_q = grad_q.shape[0] // 2
    norm_rows = norm_grads.size // lanes
    mat_q_far, mat_o_far, send, mat_q_near, mat_o_near, part, norm = project(
        grad_q, error_q, grad_o, error_o, qfac_q.T, qfac_o.T, norm_grads
    )
    columns = part.shape[1]
    rounds = rounds_of(replicas)
    state = small(
        first_sum_kernel, "first_sum", shaped((rank, columns + lanes), bf16), part, norm, swap_halves(send)
    )
    wide = shaped((rank, columns + 2 * lanes), bf16)
    for bits in rounds[:-1]:
        state = small(
            functools.partial(norm_sum_kernel, columns), "norm_sum", wide, *exchange(state, bits)
        )
    hat_near = small(
        functools.partial(hat_kernel, half_q, columns), "hats", wide,
        ginv_q, ginv_o, *exchange(state, rounds[-1]),
    )
    hat_far = swap_halves(hat_near)
    part_q, part_o = right_near(hat_near, mat_q_near, mat_o_near)
    send, near, norm = right_far(
        hat_far, mat_q_far, mat_o_far, part_q, part_o, hat_near, norm_rows
    )
    state, norm = small(
        near_sum_kernel, "near_sum", (shaped(send.shape, bf16), shaped(norm.shape, f32)),
        near, swap_halves(send), norm,
    )
    for bits in rounds[:-1]:
        state = small(
            plain_sum_kernel, "plain_sum", shaped(state.shape, bf16), *exchange(state, bits)
        )
    states = exchange(state, rounds[-1])
    norm = small(
        norm_add_kernel, "norm_add", shaped(norm.shape, f32), norm, swap_tensor(norm, 1)
    )
    new_near, norm = small(
        functools.partial(mean_kernel, replicas, replicas * tensors), "mean",
        (shaped(state.shape, bf16), shaped(norm.shape, f32)),
        norm, swap_tensor(norm, 2), *states,
    )
    (
        error_q_new, error_o_new, momentum_q_new, weight_q_new,
        new_q, new_o, momentum_o_new, weight_o_new, norm_mean,
    ) = finish(
        replicas, hat_near, hat_far,
        (mat_q_near, mat_o_near, mat_q_far, mat_o_far), new_near,
        (weight_q, momentum_q, weight_o, momentum_o), norm,
    )
    return (
        error_q_new,
        new_q.T,
        momentum_q_new,
        weight_q_new,
        error_o_new,
        new_o.T,
        momentum_o_new,
        weight_o_new,
        norm_mean.reshape(-1),
    )


def solution(mesh):
    in_specs = (
        P("replica", "tensor"),
        P("replica", "tensor"),
        P("tensor", None),
        P("tensor", None),
        P("replica", "tensor"),
        P("replica", "tensor"),
        P(("replica", "tensor"), None),
        P(("replica", "tensor"), None),
        P("tensor", None),
        P("tensor", None),
        P("tensor", "replica"),
        P("tensor", "replica"),
        P("replica", "tensor", None),
    )
    out_specs = (
        P("replica", "tensor"),
        P("tensor", None),
        P("replica", "tensor"),
        P("replica", "tensor"),
        P(("replica", "tensor"), None),
        P("tensor", None),
        P("tensor", "replica"),
        P("tensor", "replica"),
        P(),
    )
    return jax.shard_map(
        on_device, mesh=mesh, in_specs=in_specs, out_specs=out_specs, check_vma=False
    )
```

```python
import functools

import jax
import jax.numpy as jnp
from jax import lax
from jax.experimental import pallas as pl
from jax.experimental.pallas import tpu as pltpu
from jax.sharding import PartitionSpec as P

momentum_decay = 0.9
step_size = 0.5
lanes = 128
mib = 1024 * 1024
bf16 = jnp.bfloat16
f32 = jnp.float32

whole = pl.BlockSpec(memory_space=pltpu.VMEM)
in_place = pl.BlockSpec(memory_space=pl.ANY)


def dot(left, right, left_dim, right_dim, precision=None):
    return lax.dot_general(
        left,
        right,
        (((left_dim,), (right_dim,)), ((), ())),
        precision=precision,
        preferred_element_type=f32,
    )


def params(limit):
    return pltpu.CompilerParams(vmem_limit_bytes=limit * mib)


def cost(flops, moved):
    return pl.CostEstimate(flops=flops, bytes_accessed=moved, transcendentals=0)


def in_hbm(value):
    return pltpu.with_memory_space_constraint(value, pltpu.HBM)


def in_vmem(value):
    return pltpu.with_memory_space_constraint(value, pltpu.VMEM)


def shaped(shape, dtype):
    return jax.ShapeDtypeStruct(shape, dtype)


def parity():
    replica = lax.axis_index("replica")
    odd = lax.rem(lax.axis_index("tensor"), 2) == 1
    return jnp.where(odd, replica // (lax.axis_size("replica") // 2), lax.rem(replica, 2))


def half_at(which, size):
    return pl.ds(pl.multiple_of(which * size, size), size)


def load(source, target, sem):
    copy = pltpu.make_async_copy(source, target, sem)
    copy.start()
    return copy


def project_half(
    which, fac_q_h, fac_o_h, grad_q, error_q, grad_o, error_o, mat_q, mat_o, store,
    fac_q, fac_o, grad_q_v, error_q_v, grad_o_v, error_o_v, sems,
):
    half_q, half_o = mat_q.shape[0], mat_o.shape[0]
    jobs = []
    fac_copies = [load(fac_q_h, fac_q, sems.at[0]), load(fac_o_h, fac_o, sems.at[1])]
    chunks_q, chunks_o = 4, 2
    rows_q, rows_o = half_q // chunks_q, half_o // chunks_o
    slot = 2
    for chunk in range(chunks_q):
        part = pl.ds(chunk * rows_q, rows_q)
        there = pl.ds(pl.multiple_of(which * half_q + chunk * rows_q, rows_q), rows_q)
        jobs.append((grad_q_v, error_q_v, mat_q, fac_q, part, chunk * rows_q, (
            load(grad_q.at[there], grad_q_v.at[part], sems.at[slot]),
            load(error_q.at[there], error_q_v.at[part], sems.at[slot + 1]),
        )))
        slot += 2
        if chunk % 2 == 0:
            continue
        chunk = chunk // 2
        part = pl.ds(chunk * rows_o, rows_o)
        there = pl.ds(pl.multiple_of(which * half_o + chunk * rows_o, rows_o), rows_o)
        jobs.append((grad_o_v, error_o_v, mat_o, fac_o, part, half_q + chunk * rows_o, (
            load(grad_o.at[there], grad_o_v.at[part], sems.at[slot]),
            load(error_o.at[there], error_o_v.at[part], sems.at[slot + 1]),
        )))
        slot += 2
    for copy in fac_copies:
        copy.wait()
    for grad_v, error_v, mat, fac, part, column, copies in jobs:
        for copy in copies:
            copy.wait()
        block = grad_v[part] + error_v[part]
        mat[part] = block
        store(column, dot(fac[...], block, 1, 1))


def far_kernel(
    fac_q_h, fac_o_h, grad_q, error_q, grad_o, error_o, mat_q, mat_o, send, *scratch
):
    def store(column, value):
        send[:, column:column + value.shape[1]] = value.astype(bf16)

    project_half(
        1 - parity(), fac_q_h, fac_o_h, grad_q, error_q, grad_o, error_o,
        mat_q, mat_o, store, *scratch
    )


def near_kernel(
    fac_q_h, fac_o_h, grad_q, error_q, grad_o, error_o, norm_grads,
    mat_q, mat_o, part, norm, *scratch
):
    def store(column, value):
        part[:, column:column + value.shape[1]] = value

    project_half(
        parity(), fac_q_h, fac_o_h, grad_q, error_q, grad_o, error_o,
        mat_q, mat_o, store, *scratch
    )
    values = norm_grads[0].astype(f32)
    for row in range(norm.shape[0]):
        norm[row:row + 1, :] = values[:, row * lanes:(row + 1) * lanes]


def project(grad_q, error_q, grad_o, error_o, fac_q, fac_o, norm_grads):
    rank = fac_q.shape[0]
    half_q = (grad_q.shape[0] // 2, grad_q.shape[1])
    half_o = (grad_o.shape[0] // 2, grad_o.shape[1])
    columns = half_q[0] + half_o[0]
    norm_rows = norm_grads.size // lanes
    mats = (pltpu.VMEM(half_q, bf16), pltpu.VMEM(half_o, bf16))
    scratch = [
        pltpu.VMEM(fac_q.shape, bf16),
        pltpu.VMEM(fac_o.shape, bf16),
        pltpu.VMEM(half_q, bf16),
        pltpu.VMEM(half_q, bf16),
        pltpu.VMEM(half_o, bf16),
        pltpu.VMEM(half_o, bf16),
        pltpu.SemaphoreType.DMA((14,)),
    ]
    operands = [
        in_hbm(value) for value in (fac_q, fac_o, grad_q, error_q, grad_o, error_o)
    ]
    effort = cost(2 * rank * (grad_q.size + grad_o.size) // 2, 4 * grad_q.size)
    mat_q_far, mat_o_far, send = pl.pallas_call(
        far_kernel,
        out_shape=mats + (shaped((rank, columns), bf16),),
        in_specs=[in_place] * 6,
        out_specs=(whole,) * 3,
        scratch_shapes=scratch,
        compiler_params=params(16),
        cost_estimate=effort,
        name="project_far",
    )(*operands)
    mat_q_near, mat_o_near, part, norm = pl.pallas_call(
        near_kernel,
        out_shape=mats + (shaped((rank, columns), f32), shaped((norm_rows, lanes), f32)),
        in_specs=[in_place] * 6 + [whole],
        out_specs=(whole,) * 4,
        scratch_shapes=scratch,
        compiler_params=params(16),
        cost_estimate=effort,
        name="project_near",
    )(*operands, norm_grads)
    return mat_q_far, mat_o_far, send, mat_q_near, mat_o_near, part, norm


def small(kernel, name, outs, *operands):
    return pl.pallas_call(
        kernel,
        out_shape=outs,
        in_specs=[whole] * len(operands),
        out_specs=(whole,) * len(outs) if isinstance(outs, tuple) else whole,
        compiler_params=params(8),
        name=name,
    )(*operands)


def tree(parts):
    while len(parts) > 1:
        parts = [parts[place] + parts[place + 1] for place in range(0, len(parts), 2)]
    return parts[0]


def total_of(states, columns):
    return tree([state[:, :columns].astype(f32) for state in states])


def norm_of(states, columns):
    parts = []
    for state in states:
        part = state[:, columns:columns + lanes].astype(f32)
        if state.shape[1] > columns + lanes:
            part = part + state[:, columns + lanes:columns + 2 * lanes].astype(f32)
        parts.append(part)
    return tree(parts)


def store_norm(state, columns, total):
    high = total.astype(bf16)
    state[:, columns:columns + lanes] = high
    state[:, columns + lanes:columns + 2 * lanes] = (total - high.astype(f32)).astype(bf16)


def first_sum_kernel(part, norm, got, state):
    columns = part.shape[1]
    state[:, :columns] = (part[...] + got[...].astype(f32)).astype(bf16)
    state[:, columns:] = norm[...].astype(bf16)


def norm_sum_kernel(columns, *refs):
    *states, out = refs
    out[:, :columns] = total_of(states, columns).astype(bf16)
    store_norm(out, columns, norm_of(states, columns))


def plain_sum_kernel(*refs):
    *states, out = refs
    out[...] = total_of(states, out.shape[1]).astype(bf16)


def hat_kernel(size_q, columns, ginv_q, ginv_o, *refs):
    *states, out = refs
    total = total_of(states, columns)
    highest = lax.Precision.HIGHEST
    out[:, :size_q] = dot(ginv_q[...].T, total[:, :size_q], 1, 0, highest).astype(bf16)
    out[:, size_q:columns] = dot(ginv_o[...].T, total[:, size_q:], 1, 0, highest).astype(bf16)
    store_norm(out, columns, norm_of(states, columns))


def mean_kernel(count, norm_count, norm, norm_got, *refs):
    *states, new, norm_mean = refs
    new[...] = (total_of(states, new.shape[1]) / count).astype(bf16)
    norm_mean[...] = (norm[...] + norm_got[...]) / norm_count


def right_near_kernel(hat, mat_q, mat_o, part_q, part_o):
    size_q, size_o = mat_q.shape[0], mat_o.shape[0]
    part_q[...] = dot(hat[:, :size_q], mat_q[...], 1, 0)
    part_o[...] = dot(hat[:, size_q:size_q + size_o], mat_o[...], 1, 0)


def right_near(hat, mat_q, mat_o):
    rank = hat.shape[0]
    return pl.pallas_call(
        right_near_kernel,
        out_shape=(shaped((rank, mat_q.shape[1]), f32), shaped((rank, mat_o.shape[1]), f32)),
        in_specs=[whole] * 3,
        out_specs=(whole,) * 2,
        compiler_params=params(8),
        cost_estimate=cost(2 * rank * (mat_q.size + mat_o.size), 2 * (mat_q.size + mat_o.size)),
        name="right_near",
    )(hat, in_vmem(mat_q), in_vmem(mat_o))


def right_half(which, hat, mat_q, mat_o, part_q, part_o, store):
    size_q, size_o = mat_q.shape[0], mat_o.shape[0]
    half_q, half_o = mat_q.shape[1] // 2, mat_o.shape[1] // 2
    columns = half_at(which, half_q)
    store(0, half_q, part_q[:, columns] + dot(hat[:, :size_q], mat_q[:, columns], 1, 0))
    columns = half_at(which, half_o)
    store(half_q, half_o, part_o[:, columns] + dot(
        hat[:, size_q:size_q + size_o], mat_o[:, columns], 1, 0
    ))


def right_send_kernel(hat, mat_q, mat_o, part_q, part_o, send):
    def store(column, width, value):
        send[:, column:column + width] = value.astype(bf16)

    right_half(1 - parity(), hat, mat_q, mat_o, part_q, part_o, store)


def right_keep_kernel(hat, mat_q, mat_o, part_q, part_o, hat_near, near, norm):
    def store(column, width, value):
        near[:, column:column + width] = value

    right_half(parity(), hat, mat_q, mat_o, part_q, part_o, store)
    norm[...] = norm_of([hat_near, hat], mat_q.shape[0] + mat_o.shape[0])


def right_far(hat, mat_q, mat_o, part_q, part_o, hat_near, norm_rows):
    rank = hat.shape[0]
    columns = (mat_q.shape[1] + mat_o.shape[1]) // 2
    operands = (hat, in_vmem(mat_q), in_vmem(mat_o), part_q, part_o)
    effort = cost(rank * (mat_q.size + mat_o.size), mat_q.size + mat_o.size)
    send = pl.pallas_call(
        right_send_kernel,
        out_shape=shaped((rank, columns), bf16),
        in_specs=[whole] * 5,
        out_specs=whole,
        compiler_params=params(8),
        cost_estimate=effort,
        name="right_send",
    )(*operands)
    near, norm = pl.pallas_call(
        right_keep_kernel,
        out_shape=(shaped((rank, columns), f32), shaped((norm_rows, lanes), f32)),
        in_specs=[whole] * 6,
        out_specs=(whole,) * 2,
        compiler_params=params(8),
        cost_estimate=effort,
        name="right_keep",
    )(*operands, hat_near)
    return send, near, norm


def near_sum_kernel(near, got, norm, norm_got, state, norm_sum):
    state[...] = (near[...] + got[...].astype(f32)).astype(bf16)
    norm_sum[...] = norm[...] + norm_got[...]


def error_columns(column, hat, hat_row, half, mat_q, mat_o, new, error_q, error_o, stage_q, stage_o, sems, slot):
    size_q, size_o = mat_q.shape[0], mat_o.shape[0]
    wide_q, wide_o = stage_q.shape[1], stage_o.shape[1]
    copies = []
    chunk_q, chunk_o = size_q // 2, size_o // 2
    cols_q, cols_o = half_at(column, wide_q), half_at(column, wide_o)
    for chunk in range(2):
        part = pl.ds(chunk * chunk_q, chunk_q)
        stage = pl.ds(hat_row * size_q + chunk * chunk_q, chunk_q)
        approx = dot(hat[:, part], new[:, :wide_q], 0, 0)
        stage_q[stage] = (mat_q[part, cols_q].astype(f32) - approx).astype(bf16)
        there = pl.ds(pl.multiple_of(half * size_q + chunk * chunk_q, chunk_q), chunk_q)
        copies.append(load(stage_q.at[stage], error_q.at[there, cols_q], sems.at[slot]))
        part = pl.ds(chunk * chunk_o, chunk_o)
        stage = pl.ds(hat_row * size_o + chunk * chunk_o, chunk_o)
        approx = dot(hat[:, size_q + chunk * chunk_o:size_q + (chunk + 1) * chunk_o], new[:, wide_q:], 0, 0)
        stage_o[stage] = (mat_o[part, cols_o].astype(f32) - approx).astype(bf16)
        there = pl.ds(pl.multiple_of(half * size_o + chunk * chunk_o, chunk_o), chunk_o)
        copies.append(load(stage_o.at[stage], error_o.at[there, cols_o], sems.at[slot + 1]))
        slot += 2
    return copies


def piece_of(near, far, index, count, size, pieces):
    half = count // 2
    here = index // half == parity()
    slot = lax.rem(index, half)
    if size % lanes == 0:
        part = half_at(slot, size)
        return jnp.where(here, near[:, part].astype(f32), far[:, part].astype(f32)).astype(bf16)
    width = half * size
    chosen = jnp.where(here, near[:, :width].astype(f32), far[:, :width].astype(f32))
    for place in range(half):
        pieces[place] = chosen[:, place * size:(place + 1) * size]
    return pieces[slot].astype(bf16)


def finish_near_kernel(
    count, hat_near, hat_far, mat_q_near, mat_o_near, mat_q_far, mat_o_far, new, weight_q, momentum_q,
    error_q, error_o, momentum_q_h, weight_q_h,
    stage_q, stage_o, momentum_q_new, weight_q_new, pieces, sems, out_sems
):
    mine = parity()
    me = lax.axis_index("replica")
    copies = error_columns(
        mine, hat_near, 0, mine, mat_q_near, mat_o_near, new, error_q, error_o, stage_q, stage_o, sems, 0
    ) + error_columns(
        mine, hat_far, 1, 1 - mine, mat_q_far, mat_o_far, new, error_q, error_o, stage_q, stage_o, sems, 4
    )
    piece = piece_of(hat_near, hat_far, me, count, weight_q.shape[0], pieces)
    copies += query_columns(
        mine, piece, new, weight_q, momentum_q, momentum_q_new, weight_q_new,
        momentum_q_h, weight_q_h, out_sems
    )
    for copy in copies:
        copy.wait()


def query_columns(
    which, piece, new, weight, momentum, momentum_new, weight_new, momentum_h, weight_h, sems
):
    wide = momentum_new.shape[1]
    columns = half_at(which, wide)
    moved = momentum_decay * momentum[:, columns] + dot(piece, new[:, :wide], 0, 0)
    momentum_new[...] = moved
    weight_new[...] = weight[:, columns] - step_size * moved
    return [
        load(momentum_new, momentum_h.at[:, columns], sems.at[0]),
        load(weight_new, weight_h.at[:, columns], sems.at[1]),
    ]


def finish_far_kernel(
    count, hat_near, hat_far, mat_q_near, mat_o_near, mat_q_far, mat_o_far,
    new_near, new_far, weight_q, momentum_q, weight_o, momentum_o, norm,
    error_q_in, error_o_in, momentum_q_in, weight_q_in,
    error_q, error_o, momentum_q_h, weight_q_h, new_q_h, new_o_h, momentum_o_h, weight_o_h, norm_h,
    stage_q, stage_o, momentum_q_new, weight_q_new, new_q, new_o, momentum_o_new, weight_o_new,
    pieces_q, pieces_o, sems, out_sems
):
    mine = parity()
    me = lax.axis_index("replica")
    wide_q, wide_o = stage_q.shape[1], stage_o.shape[1]
    size_q = mat_q_near.shape[0]
    size_o = mat_o_near.shape[0]
    new_q[:, half_at(mine, wide_q)] = new_near[:, :wide_q]
    new_q[:, half_at(1 - mine, wide_q)] = new_far[:, :wide_q]
    new_o[:, half_at(mine, wide_o)] = new_near[:, wide_q:]
    new_o[:, half_at(1 - mine, wide_o)] = new_far[:, wide_q:]
    copies = [
        load(new_q, new_q_h, out_sems.at[0]),
        load(new_o, new_o_h, out_sems.at[1]),
        load(norm, norm_h, out_sems.at[2]),
    ]
    copies += error_columns(
        1 - mine, hat_near, 0, mine, mat_q_near, mat_o_near, new_far,
        error_q, error_o, stage_q, stage_o, sems, 0
    )
    piece = piece_of(
        new_near.at[:, wide_q:], new_far.at[:, wide_q:], me, count, weight_o.shape[1], pieces_o
    )
    for which, hat in ((mine, hat_near), (1 - mine, hat_far)):
        rows = half_at(which, size_o)
        moved = momentum_decay * momentum_o[rows] + dot(hat[:, size_q:size_q + size_o], piece, 0, 0)
        momentum_o_new[rows] = moved
        weight_o_new[rows] = weight_o[rows] - step_size * moved
    copies.append(load(momentum_o_new, momentum_o_h, out_sems.at[3]))
    copies.append(load(weight_o_new, weight_o_h, out_sems.at[4]))
    copies += error_columns(
        1 - mine, hat_far, 1, 1 - mine, mat_q_far, mat_o_far, new_far,
        error_q, error_o, stage_q, stage_o, sems, 4
    )
    piece = piece_of(hat_near, hat_far, me, count, weight_q.shape[0], pieces_q)
    copies += query_columns(
        1 - mine, piece, new_far, weight_q, momentum_q, momentum_q_new, weight_q_new,
        momentum_q_h, weight_q_h, out_sems.at[5:7]
    )
    for copy in copies:
        copy.wait()


def finish(count, hat_near, hat_far, mats, new_near, weights, norm):
    mat_q, mat_o = mats[0], mats[1]
    weight_q, _, weight_o, _ = weights
    rank = hat_near.shape[0]
    size_q, size_o = mat_q.shape[0], mat_o.shape[0]
    early = (
        shaped((2 * size_q, mat_q.shape[1]), bf16),
        shaped((2 * size_o, mat_o.shape[1]), bf16),
        shaped(weight_q.shape, f32),
        shaped(weight_q.shape, f32),
    )
    late = (
        shaped((rank, mat_q.shape[1]), bf16),
        shaped((rank, mat_o.shape[1]), bf16),
        shaped(weight_o.shape, f32),
        shaped(weight_o.shape, f32),
    )
    piece_q = (weight_q.shape[0], weight_q.shape[1] // 2)
    stages = [
        pltpu.VMEM((2 * size_q, mat_q.shape[1] // 2), bf16),
        pltpu.VMEM((2 * size_o, mat_o.shape[1] // 2), bf16),
        pltpu.VMEM(piece_q, f32),
        pltpu.VMEM(piece_q, f32),
    ]
    pieces_q = pltpu.VMEM((count // 2, rank, weight_q.shape[0]), f32)
    pieces_o = pltpu.VMEM((count // 2, rank, weight_o.shape[1]), f32)
    moved = 4 * (mat_q.size + mat_o.size)
    mats = [in_vmem(mat) for mat in mats]
    weights = [in_vmem(value) for value in weights]
    new_far = swap_halves(new_near)
    parts = pl.pallas_call(
        functools.partial(finish_near_kernel, count),
        out_shape=early,
        in_specs=[whole] * 9,
        out_specs=(in_place,) * 4,
        scratch_shapes=stages + [
            pieces_q, pltpu.SemaphoreType.DMA((8,)), pltpu.SemaphoreType.DMA((2,))
        ],
        compiler_params=params(12),
        cost_estimate=cost(2 * rank * (mat_q.size + mat_o.size), moved),
        name="finish_near",
    )(hat_near, hat_far, *mats, new_near, *weights[:2])
    return pl.pallas_call(
        functools.partial(finish_far_kernel, count),
        out_shape=early + late + (shaped(norm.shape, f32),),
        in_specs=[whole] * 13 + [in_place] * 4,
        out_specs=(in_place,) * 9,
        scratch_shapes=stages + [pltpu.VMEM(out.shape, out.dtype) for out in late] + [
            pieces_q, pieces_o, pltpu.SemaphoreType.DMA((8,)), pltpu.SemaphoreType.DMA((7,))
        ],
        input_output_aliases={13: 0, 14: 1, 15: 2, 16: 3},
        compiler_params=params(16),
        cost_estimate=cost(2 * rank * (mat_q.size + mat_o.size), moved),
        name="finish_far",
    )(hat_near, hat_far, *mats, new_near, new_far, *weights, norm, *parts)


def swap(value, even, odd):
    replicas, tensors = lax.axis_size("replica"), lax.axis_size("tensor")
    pairs = []
    for replica in range(replicas):
        for tensor in range(tensors):
            target = replica ^ (odd if tensor % 2 else even)
            pairs.append((replica * tensors + tensor, target * tensors + tensor))
    return lax.ppermute(value, ("replica", "tensor"), pairs)


def swap_halves(value):
    return swap(value, 1, lax.axis_size("replica") // 2)


def swap_tensor(value, bit):
    count = lax.axis_size("tensor")
    return lax.ppermute(value, "tensor", [(source, source ^ bit) for source in range(count)])


def exchange(state, bits):
    offsets = [(0, 0)]
    for even, odd in bits:
        offsets += [(first | even, second | odd) for first, second in offsets]
    got = [swap(state, *offset) for offset in offsets[:0:-1]]
    return [state] + got[::-1]


def rounds_of(count):
    places = range(1, count.bit_length() - 1)
    bits = [(1 << place, 1 << (place - 1)) for place in places]
    return [bits[place:place + 2] for place in range(0, len(bits), 2)]


def on_device(
    grad_q,
    error_q,
    qfac_q,
    ginv_q,
    weight_q,
    momentum_q,
    grad_o,
    error_o,
    qfac_o,
    ginv_o,
    weight_o,
    momentum_o,
    norm_grads,
):
    replicas = lax.axis_size("replica")
    tensors = lax.axis_size("tensor")
    rank = qfac_q.shape[1]
    half_q = grad_q.shape[0] // 2
    norm_rows = norm_grads.size // lanes
    mat_q_far, mat_o_far, send, mat_q_near, mat_o_near, part, norm = project(
        grad_q, error_q, grad_o, error_o, qfac_q.T, qfac_o.T, norm_grads
    )
    columns = part.shape[1]
    rounds = rounds_of(replicas)
    state = small(
        first_sum_kernel, "first_sum", shaped((rank, columns + lanes), bf16), part, norm, swap_halves(send)
    )
    wide = shaped((rank, columns + 2 * lanes), bf16)
    for bits in rounds[:-1]:
        state = small(
            functools.partial(norm_sum_kernel, columns), "norm_sum", wide, *exchange(state, bits)
        )
    hat_near = small(
        functools.partial(hat_kernel, half_q, columns), "hats", wide,
        ginv_q, ginv_o, *exchange(state, rounds[-1]),
    )
    hat_far = swap_halves(hat_near)
    part_q, part_o = right_near(hat_near, mat_q_near, mat_o_near)
    send, near, norm = right_far(
        hat_far, mat_q_far, mat_o_far, part_q, part_o, hat_near, norm_rows
    )
    state, norm = small(
        near_sum_kernel, "near_sum", (shaped(send.shape, bf16), shaped(norm.shape, f32)),
        near, swap_halves(send), norm, swap_tensor(norm, 1),
    )
    for bits in rounds[:-1]:
        state = small(
            plain_sum_kernel, "plain_sum", shaped(state.shape, bf16), *exchange(state, bits)
        )
    states = exchange(state, rounds[-1])
    new_near, norm = small(
        functools.partial(mean_kernel, replicas, replicas * tensors), "mean",
        (shaped(state.shape, bf16), shaped(norm.shape, f32)),
        norm, swap_tensor(norm, 2), *states,
    )
    (
        error_q_new, error_o_new, momentum_q_new, weight_q_new,
        new_q, new_o, momentum_o_new, weight_o_new, norm_mean,
    ) = finish(
        replicas, hat_near, hat_far,
        (mat_q_near, mat_o_near, mat_q_far, mat_o_far), new_near,
        (weight_q, momentum_q, weight_o, momentum_o), norm,
    )
    return (
        error_q_new,
        new_q.T,
        momentum_q_new,
        weight_q_new,
        error_o_new,
        new_o.T,
        momentum_o_new,
        weight_o_new,
        norm_mean.reshape(-1),
    )


def solution(mesh):
    in_specs = (
        P("replica", "tensor"),
        P("replica", "tensor"),
        P("tensor", None),
        P("tensor", None),
        P("replica", "tensor"),
        P("replica", "tensor"),
        P(("replica", "tensor"), None),
        P(("replica", "tensor"), None),
        P("tensor", None),
        P("tensor", None),
        P("tensor", "replica"),
        P("tensor", "replica"),
        P("replica", "tensor", None),
    )
    out_specs = (
        P("replica", "tensor"),
        P("tensor", None),
        P("replica", "tensor"),
        P("replica", "tensor"),
        P(("replica", "tensor"), None),
        P("tensor", None),
        P("tensor", "replica"),
        P("tensor", "replica"),
        P(),
    )
    return jax.shard_map(
        on_device, mesh=mesh, in_specs=in_specs, out_specs=out_specs, check_vma=False
    )
```

```python
import functools

import jax
import jax.numpy as jnp
from jax import lax
from jax.experimental import pallas as pl
from jax.experimental.pallas import tpu as pltpu
from jax.sharding import PartitionSpec as P

momentum_decay = 0.9
step_size = 0.5
lanes = 128
mib = 1024 * 1024
bf16 = jnp.bfloat16
f32 = jnp.float32

whole = pl.BlockSpec(memory_space=pltpu.VMEM)
in_place = pl.BlockSpec(memory_space=pl.ANY)


def dot(left, right, left_dim, right_dim, precision=None):
    return lax.dot_general(
        left,
        right,
        (((left_dim,), (right_dim,)), ((), ())),
        precision=precision,
        preferred_element_type=f32,
    )


def params(limit):
    return pltpu.CompilerParams(vmem_limit_bytes=limit * mib)


def cost(flops, moved):
    return pl.CostEstimate(flops=flops, bytes_accessed=moved, transcendentals=0)


def in_hbm(value):
    return pltpu.with_memory_space_constraint(value, pltpu.HBM)


def in_vmem(value):
    return pltpu.with_memory_space_constraint(value, pltpu.VMEM)


def shaped(shape, dtype):
    return jax.ShapeDtypeStruct(shape, dtype)


def parity():
    replica = lax.axis_index("replica")
    odd = lax.rem(lax.axis_index("tensor"), 2) == 1
    return jnp.where(odd, replica // (lax.axis_size("replica") // 2), lax.rem(replica, 2))


def half_at(which, size):
    return pl.ds(pl.multiple_of(which * size, size), size)


def load(source, target, sem, queue=0):
    copy = pltpu.make_async_copy(source, target, sem)
    copy.start(priority=queue)
    return copy


def project_half(
    which, fac_q_h, fac_o_h, grad_q, error_q, grad_o, error_o, mat_q, mat_o, store,
    fac_q, fac_o, grad_q_v, error_q_v, grad_o_v, error_o_v, sems,
):
    half_q, half_o = mat_q.shape[0], mat_o.shape[0]
    jobs = []
    fac_copies = [load(fac_o_h, fac_o, sems.at[0]), load(fac_q_h, fac_q, sems.at[1], 1)]
    slot = 2
    for chunks, half, column, grad, error, grad_v, error_v, mat, fac in (
        (2, half_o, half_q, grad_o, error_o, grad_o_v, error_o_v, mat_o, fac_o),
        (4, half_q, 0, grad_q, error_q, grad_q_v, error_q_v, mat_q, fac_q),
    ):
        rows = half // chunks
        for chunk in range(chunks):
            part = pl.ds(chunk * rows, rows)
            there = pl.ds(pl.multiple_of(which * half + chunk * rows, rows), rows)
            jobs.append((grad_v, error_v, mat, fac, part, column + chunk * rows, (
                load(grad.at[there], grad_v.at[part], sems.at[slot]),
                load(error.at[there], error_v.at[part], sems.at[slot + 1], 1),
            )))
            slot += 2
    for copy in fac_copies:
        copy.wait()
    for grad_v, error_v, mat, fac, part, column, copies in jobs:
        for copy in copies:
            copy.wait()
        block = grad_v[part] + error_v[part]
        mat[part] = block
        store(column, dot(fac[...], block, 1, 1))


def far_kernel(
    fac_q_h, fac_o_h, grad_q, error_q, grad_o, error_o, mat_q, mat_o, send, *scratch
):
    def store(column, value):
        send[:, column:column + value.shape[1]] = value.astype(bf16)

    project_half(
        1 - parity(), fac_q_h, fac_o_h, grad_q, error_q, grad_o, error_o,
        mat_q, mat_o, store, *scratch
    )


def near_kernel(
    fac_q_h, fac_o_h, grad_q, error_q, grad_o, error_o, norm_grads,
    mat_q, mat_o, part, norm, *scratch
):
    def store(column, value):
        part[:, column:column + value.shape[1]] = value

    project_half(
        parity(), fac_q_h, fac_o_h, grad_q, error_q, grad_o, error_o,
        mat_q, mat_o, store, *scratch
    )
    values = norm_grads[0].astype(f32)
    for row in range(norm.shape[0]):
        norm[row:row + 1, :] = values[:, row * lanes:(row + 1) * lanes]


def project(grad_q, error_q, grad_o, error_o, fac_q, fac_o, norm_grads):
    rank = fac_q.shape[0]
    half_q = (grad_q.shape[0] // 2, grad_q.shape[1])
    half_o = (grad_o.shape[0] // 2, grad_o.shape[1])
    columns = half_q[0] + half_o[0]
    norm_rows = norm_grads.size // lanes
    mats = (pltpu.VMEM(half_q, bf16), pltpu.VMEM(half_o, bf16))
    scratch = [
        pltpu.VMEM(fac_q.shape, bf16),
        pltpu.VMEM(fac_o.shape, bf16),
        pltpu.VMEM(half_q, bf16),
        pltpu.VMEM(half_q, bf16),
        pltpu.VMEM(half_o, bf16),
        pltpu.VMEM(half_o, bf16),
        pltpu.SemaphoreType.DMA((14,)),
    ]
    operands = [
        in_hbm(value) for value in (fac_q, fac_o, grad_q, error_q, grad_o, error_o)
    ]
    effort = cost(2 * rank * (grad_q.size + grad_o.size) // 2, 4 * grad_q.size)
    mat_q_far, mat_o_far, send = pl.pallas_call(
        far_kernel,
        out_shape=mats + (shaped((rank, columns), bf16),),
        in_specs=[in_place] * 6,
        out_specs=(whole,) * 3,
        scratch_shapes=scratch,
        compiler_params=params(16),
        cost_estimate=effort,
        name="project_far",
    )(*operands)
    mat_q_near, mat_o_near, part, norm = pl.pallas_call(
        near_kernel,
        out_shape=mats + (shaped((rank, columns), f32), shaped((norm_rows, lanes), f32)),
        in_specs=[in_place] * 6 + [whole],
        out_specs=(whole,) * 4,
        scratch_shapes=scratch,
        compiler_params=params(16),
        cost_estimate=effort,
        name="project_near",
    )(*operands, norm_grads)
    return mat_q_far, mat_o_far, send, mat_q_near, mat_o_near, part, norm


def small(kernel, name, outs, *operands):
    return pl.pallas_call(
        kernel,
        out_shape=outs,
        in_specs=[whole] * len(operands),
        out_specs=(whole,) * len(outs) if isinstance(outs, tuple) else whole,
        compiler_params=params(8),
        name=name,
    )(*operands)


def tree(parts):
    while len(parts) > 1:
        parts = [parts[place] + parts[place + 1] for place in range(0, len(parts), 2)]
    return parts[0]


def total_of(states, columns):
    return tree([state[:, :columns].astype(f32) for state in states])


def norm_of(states, columns):
    parts = []
    for state in states:
        part = state[:, columns:columns + lanes].astype(f32)
        if state.shape[1] > columns + lanes:
            part = part + state[:, columns + lanes:columns + 2 * lanes].astype(f32)
        parts.append(part)
    return tree(parts)


def store_norm(state, columns, total):
    high = total.astype(bf16)
    state[:, columns:columns + lanes] = high
    state[:, columns + lanes:columns + 2 * lanes] = (total - high.astype(f32)).astype(bf16)


def first_sum_kernel(part, norm, got, state):
    columns = part.shape[1]
    state[:, :columns] = (part[...] + got[...].astype(f32)).astype(bf16)
    state[:, columns:] = norm[...].astype(bf16)


def norm_sum_kernel(columns, *refs):
    *states, out = refs
    out[:, :columns] = total_of(states, columns).astype(bf16)
    store_norm(out, columns, norm_of(states, columns))


def plain_sum_kernel(*refs):
    *states, out = refs
    out[...] = total_of(states, out.shape[1]).astype(bf16)


def hat_kernel(size_q, columns, ginv_q, ginv_o, *refs):
    *states, out = refs
    total = total_of(states, columns)
    highest = lax.Precision.HIGHEST
    out[:, :size_q] = dot(ginv_q[...].T, total[:, :size_q], 1, 0, highest).astype(bf16)
    out[:, size_q:columns] = dot(ginv_o[...].T, total[:, size_q:], 1, 0, highest).astype(bf16)
    store_norm(out, columns, norm_of(states, columns))


def mean_kernel(count, norm_count, norm, norm_got, *refs):
    *states, new, norm_mean = refs
    new[...] = (total_of(states, new.shape[1]) / count).astype(bf16)
    norm_mean[...] = (norm[...] + norm_got[...]) / norm_count


def right_near_kernel(hat, mat_q, mat_o, part_q, part_o):
    size_q, size_o = mat_q.shape[0], mat_o.shape[0]
    part_q[...] = dot(hat[:, :size_q], mat_q[...], 1, 0)
    part_o[...] = dot(hat[:, size_q:size_q + size_o], mat_o[...], 1, 0)


def right_near(hat, mat_q, mat_o):
    rank = hat.shape[0]
    return pl.pallas_call(
        right_near_kernel,
        out_shape=(shaped((rank, mat_q.shape[1]), f32), shaped((rank, mat_o.shape[1]), f32)),
        in_specs=[whole] * 3,
        out_specs=(whole,) * 2,
        compiler_params=params(8),
        cost_estimate=cost(2 * rank * (mat_q.size + mat_o.size), 2 * (mat_q.size + mat_o.size)),
        name="right_near",
    )(hat, in_vmem(mat_q), in_vmem(mat_o))


def right_half(which, hat, mat_q, mat_o, part_q, part_o, store):
    size_q, size_o = mat_q.shape[0], mat_o.shape[0]
    half_q, half_o = mat_q.shape[1] // 2, mat_o.shape[1] // 2
    columns = half_at(which, half_q)
    store(0, half_q, part_q[:, columns] + dot(hat[:, :size_q], mat_q[:, columns], 1, 0))
    columns = half_at(which, half_o)
    store(half_q, half_o, part_o[:, columns] + dot(
        hat[:, size_q:size_q + size_o], mat_o[:, columns], 1, 0
    ))


def right_send_kernel(hat, mat_q, mat_o, part_q, part_o, send):
    def store(column, width, value):
        send[:, column:column + width] = value.astype(bf16)

    right_half(1 - parity(), hat, mat_q, mat_o, part_q, part_o, store)


def right_keep_kernel(hat, mat_q, mat_o, part_q, part_o, hat_near, near, norm):
    def store(column, width, value):
        near[:, column:column + width] = value

    right_half(parity(), hat, mat_q, mat_o, part_q, part_o, store)
    norm[...] = norm_of([hat_near, hat], mat_q.shape[0] + mat_o.shape[0])


def right_far(hat, mat_q, mat_o, part_q, part_o, hat_near, norm_rows):
    rank = hat.shape[0]
    columns = (mat_q.shape[1] + mat_o.shape[1]) // 2
    operands = (hat, in_vmem(mat_q), in_vmem(mat_o), part_q, part_o)
    effort = cost(rank * (mat_q.size + mat_o.size), mat_q.size + mat_o.size)
    send = pl.pallas_call(
        right_send_kernel,
        out_shape=shaped((rank, columns), bf16),
        in_specs=[whole] * 5,
        out_specs=whole,
        compiler_params=params(8),
        cost_estimate=effort,
        name="right_send",
    )(*operands)
    near, norm = pl.pallas_call(
        right_keep_kernel,
        out_shape=(shaped((rank, columns), f32), shaped((norm_rows, lanes), f32)),
        in_specs=[whole] * 6,
        out_specs=(whole,) * 2,
        compiler_params=params(8),
        cost_estimate=effort,
        name="right_keep",
    )(*operands, hat_near)
    return send, near, norm


def near_sum_kernel(near, got, norm, norm_got, state, norm_sum):
    state[...] = (near[...] + got[...].astype(f32)).astype(bf16)
    norm_sum[...] = norm[...] + norm_got[...]


def error_columns(column, hat, hat_row, half, mat_q, mat_o, new, error_q, error_o, stage_q, stage_o, sems, slot):
    size_q, size_o = mat_q.shape[0], mat_o.shape[0]
    wide_q, wide_o = stage_q.shape[1], stage_o.shape[1]
    copies = []
    chunk_q, chunk_o = size_q // 2, size_o // 2
    cols_q, cols_o = half_at(column, wide_q), half_at(column, wide_o)
    for chunk in range(2):
        part = pl.ds(chunk * chunk_q, chunk_q)
        stage = pl.ds(hat_row * size_q + chunk * chunk_q, chunk_q)
        approx = dot(hat[:, part], new[:, :wide_q], 0, 0)
        stage_q[stage] = (mat_q[part, cols_q].astype(f32) - approx).astype(bf16)
        there = pl.ds(pl.multiple_of(half * size_q + chunk * chunk_q, chunk_q), chunk_q)
        copies.append(load(stage_q.at[stage], error_q.at[there, cols_q], sems.at[slot]))
        part = pl.ds(chunk * chunk_o, chunk_o)
        stage = pl.ds(hat_row * size_o + chunk * chunk_o, chunk_o)
        approx = dot(hat[:, size_q + chunk * chunk_o:size_q + (chunk + 1) * chunk_o], new[:, wide_q:], 0, 0)
        stage_o[stage] = (mat_o[part, cols_o].astype(f32) - approx).astype(bf16)
        there = pl.ds(pl.multiple_of(half * size_o + chunk * chunk_o, chunk_o), chunk_o)
        copies.append(load(stage_o.at[stage], error_o.at[there, cols_o], sems.at[slot + 1], 1))
        slot += 2
    return copies


def piece_of(near, far, index, count, size, pieces):
    half = count // 2
    here = index // half == parity()
    slot = lax.rem(index, half)
    if size % lanes == 0:
        part = half_at(slot, size)
        return jnp.where(here, near[:, part].astype(f32), far[:, part].astype(f32)).astype(bf16)
    width = half * size
    chosen = jnp.where(here, near[:, :width].astype(f32), far[:, :width].astype(f32))
    for place in range(half):
        pieces[place] = chosen[:, place * size:(place + 1) * size]
    return pieces[slot].astype(bf16)


def finish_near_kernel(
    count, hat_near, hat_far, mat_q_near, mat_o_near, mat_q_far, mat_o_far, new, weight_q, momentum_q,
    error_q, error_o, momentum_q_h, weight_q_h,
    stage_q, stage_o, momentum_q_new, weight_q_new, pieces, sems, out_sems
):
    mine = parity()
    me = lax.axis_index("replica")
    copies = error_columns(
        mine, hat_near, 0, mine, mat_q_near, mat_o_near, new, error_q, error_o, stage_q, stage_o, sems, 0
    ) + error_columns(
        mine, hat_far, 1, 1 - mine, mat_q_far, mat_o_far, new, error_q, error_o, stage_q, stage_o, sems, 4
    )
    piece = piece_of(hat_near, hat_far, me, count, weight_q.shape[0], pieces)
    copies += query_columns(
        mine, piece, new, weight_q, momentum_q, momentum_q_new, weight_q_new,
        momentum_q_h, weight_q_h, out_sems
    )
    for copy in copies:
        copy.wait()


def query_columns(
    which, piece, new, weight, momentum, momentum_new, weight_new, momentum_h, weight_h, sems
):
    wide = momentum_new.shape[1]
    columns = half_at(which, wide)
    moved = momentum_decay * momentum[:, columns] + dot(piece, new[:, :wide], 0, 0)
    momentum_new[...] = moved
    weight_new[...] = weight[:, columns] - step_size * moved
    return [
        load(momentum_new, momentum_h.at[:, columns], sems.at[0]),
        load(weight_new, weight_h.at[:, columns], sems.at[1], 1),
    ]


def finish_far_kernel(
    count, hat_near, hat_far, mat_q_near, mat_o_near, mat_q_far, mat_o_far,
    new_near, new_far, weight_q, momentum_q, weight_o, momentum_o, norm,
    error_q_in, error_o_in, momentum_q_in, weight_q_in,
    error_q, error_o, momentum_q_h, weight_q_h, new_q_h, new_o_h, momentum_o_h, weight_o_h, norm_h,
    stage_q, stage_o, momentum_q_new, weight_q_new, new_q, new_o, momentum_o_new, weight_o_new,
    pieces_q, pieces_o, sems, out_sems
):
    mine = parity()
    me = lax.axis_index("replica")
    wide_q, wide_o = stage_q.shape[1], stage_o.shape[1]
    size_q = mat_q_near.shape[0]
    size_o = mat_o_near.shape[0]
    new_q[:, half_at(mine, wide_q)] = new_near[:, :wide_q]
    new_q[:, half_at(1 - mine, wide_q)] = new_far[:, :wide_q]
    new_o[:, half_at(mine, wide_o)] = new_near[:, wide_q:]
    new_o[:, half_at(1 - mine, wide_o)] = new_far[:, wide_q:]
    copies = [
        load(new_q, new_q_h, out_sems.at[0]),
        load(new_o, new_o_h, out_sems.at[1], 1),
        load(norm, norm_h, out_sems.at[2]),
    ]
    copies += error_columns(
        1 - mine, hat_near, 0, mine, mat_q_near, mat_o_near, new_far,
        error_q, error_o, stage_q, stage_o, sems, 0
    )
    piece = piece_of(
        new_near.at[:, wide_q:], new_far.at[:, wide_q:], me, count, weight_o.shape[1], pieces_o
    )
    for which, hat in ((mine, hat_near), (1 - mine, hat_far)):
        rows = half_at(which, size_o)
        moved = momentum_decay * momentum_o[rows] + dot(hat[:, size_q:size_q + size_o], piece, 0, 0)
        momentum_o_new[rows] = moved
        weight_o_new[rows] = weight_o[rows] - step_size * moved
    copies.append(load(momentum_o_new, momentum_o_h, out_sems.at[3]))
    copies.append(load(weight_o_new, weight_o_h, out_sems.at[4], 1))
    copies += error_columns(
        1 - mine, hat_far, 1, 1 - mine, mat_q_far, mat_o_far, new_far,
        error_q, error_o, stage_q, stage_o, sems, 4
    )
    piece = piece_of(hat_near, hat_far, me, count, weight_q.shape[0], pieces_q)
    copies += query_columns(
        1 - mine, piece, new_far, weight_q, momentum_q, momentum_q_new, weight_q_new,
        momentum_q_h, weight_q_h, out_sems.at[5:7]
    )
    for copy in copies:
        copy.wait()


def finish(count, hat_near, hat_far, mats, new_near, weights, norm):
    mat_q, mat_o = mats[0], mats[1]
    weight_q, _, weight_o, _ = weights
    rank = hat_near.shape[0]
    size_q, size_o = mat_q.shape[0], mat_o.shape[0]
    early = (
        shaped((2 * size_q, mat_q.shape[1]), bf16),
        shaped((2 * size_o, mat_o.shape[1]), bf16),
        shaped(weight_q.shape, f32),
        shaped(weight_q.shape, f32),
    )
    late = (
        shaped((rank, mat_q.shape[1]), bf16),
        shaped((rank, mat_o.shape[1]), bf16),
        shaped(weight_o.shape, f32),
        shaped(weight_o.shape, f32),
    )
    piece_q = (weight_q.shape[0], weight_q.shape[1] // 2)
    stages = [
        pltpu.VMEM((2 * size_q, mat_q.shape[1] // 2), bf16),
        pltpu.VMEM((2 * size_o, mat_o.shape[1] // 2), bf16),
        pltpu.VMEM(piece_q, f32),
        pltpu.VMEM(piece_q, f32),
    ]
    pieces_q = pltpu.VMEM((count // 2, rank, weight_q.shape[0]), f32)
    pieces_o = pltpu.VMEM((count // 2, rank, weight_o.shape[1]), f32)
    moved = 4 * (mat_q.size + mat_o.size)
    mats = [in_vmem(mat) for mat in mats]
    weights = [in_vmem(value) for value in weights]
    new_far = swap_halves(new_near)
    parts = pl.pallas_call(
        functools.partial(finish_near_kernel, count),
        out_shape=early,
        in_specs=[whole] * 9,
        out_specs=(in_place,) * 4,
        scratch_shapes=stages + [
            pieces_q, pltpu.SemaphoreType.DMA((8,)), pltpu.SemaphoreType.DMA((2,))
        ],
        compiler_params=params(12),
        cost_estimate=cost(2 * rank * (mat_q.size + mat_o.size), moved),
        name="finish_near",
    )(hat_near, hat_far, *mats, new_near, *weights[:2])
    return pl.pallas_call(
        functools.partial(finish_far_kernel, count),
        out_shape=early + late + (shaped(norm.shape, f32),),
        in_specs=[whole] * 13 + [in_place] * 4,
        out_specs=(in_place,) * 9,
        scratch_shapes=stages + [pltpu.VMEM(out.shape, out.dtype) for out in late] + [
            pieces_q, pieces_o, pltpu.SemaphoreType.DMA((8,)), pltpu.SemaphoreType.DMA((7,))
        ],
        input_output_aliases={13: 0, 14: 1, 15: 2, 16: 3},
        compiler_params=params(16),
        cost_estimate=cost(2 * rank * (mat_q.size + mat_o.size), moved),
        name="finish_far",
    )(hat_near, hat_far, *mats, new_near, new_far, *weights, norm, *parts)


def swap(value, even, odd):
    replicas, tensors = lax.axis_size("replica"), lax.axis_size("tensor")
    pairs = []
    for replica in range(replicas):
        for tensor in range(tensors):
            target = replica ^ (odd if tensor % 2 else even)
            pairs.append((replica * tensors + tensor, target * tensors + tensor))
    return lax.ppermute(value, ("replica", "tensor"), pairs)


def swap_halves(value):
    return swap(value, 1, lax.axis_size("replica") // 2)


def swap_tensor(value, bit):
    count = lax.axis_size("tensor")
    return lax.ppermute(value, "tensor", [(source, source ^ bit) for source in range(count)])


def exchange(state, bits):
    offsets = [(0, 0)]
    for even, odd in bits:
        offsets += [(first | even, second | odd) for first, second in offsets]
    got = [swap(state, *offset) for offset in offsets[:0:-1]]
    return [state] + got[::-1]


def rounds_of(count):
    places = range(1, count.bit_length() - 1)
    bits = [(1 << place, 1 << (place - 1)) for place in places]
    return [bits[place:place + 2] for place in range(0, len(bits), 2)]


def on_device(
    grad_q,
    error_q,
    qfac_q,
    ginv_q,
    weight_q,
    momentum_q,
    grad_o,
    error_o,
    qfac_o,
    ginv_o,
    weight_o,
    momentum_o,
    norm_grads,
):
    replicas = lax.axis_size("replica")
    tensors = lax.axis_size("tensor")
    rank = qfac_q.shape[1]
    half_q = grad_q.shape[0] // 2
    norm_rows = norm_grads.size // lanes
    mat_q_far, mat_o_far, send, mat_q_near, mat_o_near, part, norm = project(
        grad_q, error_q, grad_o, error_o, qfac_q.T, qfac_o.T, norm_grads
    )
    columns = part.shape[1]
    rounds = rounds_of(replicas)
    state = small(
        first_sum_kernel, "first_sum", shaped((rank, columns + lanes), bf16), part, norm, swap_halves(send)
    )
    wide = shaped((rank, columns + 2 * lanes), bf16)
    for bits in rounds[:-1]:
        state = small(
            functools.partial(norm_sum_kernel, columns), "norm_sum", wide, *exchange(state, bits)
        )
    hat_near = small(
        functools.partial(hat_kernel, half_q, columns), "hats", wide,
        ginv_q, ginv_o, *exchange(state, rounds[-1]),
    )
    hat_far = swap_halves(hat_near)
    part_q, part_o = right_near(hat_near, mat_q_near, mat_o_near)
    send, near, norm = right_far(
        hat_far, mat_q_far, mat_o_far, part_q, part_o, hat_near, norm_rows
    )
    state, norm = small(
        near_sum_kernel, "near_sum", (shaped(send.shape, bf16), shaped(norm.shape, f32)),
        near, swap_halves(send), norm, swap_tensor(norm, 1),
    )
    for bits in rounds[:-1]:
        state = small(
            plain_sum_kernel, "plain_sum", shaped(state.shape, bf16), *exchange(state, bits)
        )
    states = exchange(state, rounds[-1])
    new_near, norm = small(
        functools.partial(mean_kernel, replicas, replicas * tensors), "mean",
        (shaped(state.shape, bf16), shaped(norm.shape, f32)),
        norm, swap_tensor(norm, 2), *states,
    )
    (
        error_q_new, error_o_new, momentum_q_new, weight_q_new,
        new_q, new_o, momentum_o_new, weight_o_new, norm_mean,
    ) = finish(
        replicas, hat_near, hat_far,
        (mat_q_near, mat_o_near, mat_q_far, mat_o_far), new_near,
        (weight_q, momentum_q, weight_o, momentum_o), norm,
    )
    return (
        error_q_new,
        new_q.T,
        momentum_q_new,
        weight_q_new,
        error_o_new,
        new_o.T,
        momentum_o_new,
        weight_o_new,
        norm_mean.reshape(-1),
    )


def solution(mesh):
    in_specs = (
        P("replica", "tensor"),
        P("replica", "tensor"),
        P("tensor", None),
        P("tensor", None),
        P("replica", "tensor"),
        P("replica", "tensor"),
        P(("replica", "tensor"), None),
        P(("replica", "tensor"), None),
        P("tensor", None),
        P("tensor", None),
        P("tensor", "replica"),
        P("tensor", "replica"),
        P("replica", "tensor", None),
    )
    out_specs = (
        P("replica", "tensor"),
        P("tensor", None),
        P("replica", "tensor"),
        P("replica", "tensor"),
        P(("replica", "tensor"), None),
        P("tensor", None),
        P("tensor", "replica"),
        P("tensor", "replica"),
        P(),
    )
    return jax.shard_map(
        on_device, mesh=mesh, in_specs=in_specs, out_specs=out_specs, check_vma=False
    )
```

```python
import functools

import jax
import jax.numpy as jnp
from jax import lax
from jax.experimental import pallas as pl
from jax.experimental.pallas import tpu as pltpu
from jax.sharding import PartitionSpec as P

momentum_decay = 0.9
step_size = 0.5
lanes = 128
mib = 1024 * 1024
bf16 = jnp.bfloat16
f32 = jnp.float32

whole = pl.BlockSpec(memory_space=pltpu.VMEM)
in_place = pl.BlockSpec(memory_space=pl.ANY)


def dot(left, right, left_dim, right_dim, precision=None):
    return lax.dot_general(
        left,
        right,
        (((left_dim,), (right_dim,)), ((), ())),
        precision=precision,
        preferred_element_type=f32,
    )


def params(limit):
    return pltpu.CompilerParams(vmem_limit_bytes=limit * mib)


def cost(flops, moved):
    return pl.CostEstimate(flops=flops, bytes_accessed=moved, transcendentals=0)


def in_hbm(value):
    return pltpu.with_memory_space_constraint(value, pltpu.HBM)


def in_vmem(value):
    return pltpu.with_memory_space_constraint(value, pltpu.VMEM)


def shaped(shape, dtype):
    return jax.ShapeDtypeStruct(shape, dtype)


def parity():
    replica = lax.axis_index("replica")
    odd = lax.rem(lax.axis_index("tensor"), 2) == 1
    return jnp.where(odd, replica // (lax.axis_size("replica") // 2), lax.rem(replica, 2))


def half_at(which, size):
    return pl.ds(pl.multiple_of(which * size, size), size)


def load(source, target, sem):
    copy = pltpu.make_async_copy(source, target, sem)
    copy.start()
    return copy


def project_half(
    which, fac_q_h, fac_o_h, grad_q, error_q, grad_o, error_o, mat_q, mat_o, store,
    fac_q, fac_o, grad_q_v, error_q_v, grad_o_v, error_o_v, sems,
):
    half_q, half_o = mat_q.shape[0], mat_o.shape[0]
    steps = 4
    rows_q, rows_o = half_q // steps, half_o // steps
    fac_copies = [load(fac_q_h, fac_q, sems.at[0]), load(fac_o_h, fac_o, sems.at[1])]
    jobs = []
    for step in range(steps):
        slot = 2 + 4 * step
        part_q = pl.ds(step * rows_q, rows_q)
        part_o = pl.ds(step * rows_o, rows_o)
        there_q = pl.ds(pl.multiple_of(which * half_q + step * rows_q, rows_q), rows_q)
        there_o = pl.ds(pl.multiple_of(which * half_o + step * rows_o, rows_o), rows_o)
        jobs.append((step, part_q, part_o, (
            load(grad_q.at[there_q], grad_q_v.at[part_q], sems.at[slot]),
            load(error_q.at[there_q], error_q_v.at[part_q], sems.at[slot + 1]),
            load(grad_o.at[there_o], grad_o_v.at[part_o], sems.at[slot + 2]),
            load(error_o.at[there_o], error_o_v.at[part_o], sems.at[slot + 3]),
        )))
    for copy in fac_copies:
        copy.wait()
    columns_o = fac_o[...].T
    for step, part_q, part_o, copies in jobs:
        for copy in copies:
            copy.wait()
        block_q = grad_q_v[part_q] + error_q_v[part_q]
        block_o = grad_o_v[part_o] + error_o_v[part_o]
        mat_q[part_q] = block_q
        mat_o[part_o] = block_o
        store(step * rows_q, dot(fac_q[...], block_q, 1, 1))
        store(half_q + step * rows_o, dot(block_o, columns_o, 1, 0).T)


def far_kernel(
    fac_q_h, fac_o_h, grad_q, error_q, grad_o, error_o, mat_q, mat_o, send, *scratch
):
    def store(column, value):
        send[:, column:column + value.shape[1]] = value.astype(bf16)

    project_half(
        1 - parity(), fac_q_h, fac_o_h, grad_q, error_q, grad_o, error_o,
        mat_q, mat_o, store, *scratch
    )


def near_kernel(
    fac_q_h, fac_o_h, grad_q, error_q, grad_o, error_o, norm_grads,
    mat_q, mat_o, part, norm, *scratch
):
    def store(column, value):
        part[:, column:column + value.shape[1]] = value

    project_half(
        parity(), fac_q_h, fac_o_h, grad_q, error_q, grad_o, error_o,
        mat_q, mat_o, store, *scratch
    )
    values = norm_grads[0].astype(f32)
    for row in range(norm.shape[0]):
        norm[row:row + 1, :] = values[:, row * lanes:(row + 1) * lanes]


def project(grad_q, error_q, grad_o, error_o, fac_q, fac_o, norm_grads):
    rank = fac_q.shape[0]
    half_q = (grad_q.shape[0] // 2, grad_q.shape[1])
    half_o = (grad_o.shape[0] // 2, grad_o.shape[1])
    columns = half_q[0] + half_o[0]
    norm_rows = norm_grads.size // lanes
    mats = (pltpu.VMEM(half_q, bf16), pltpu.VMEM(half_o, bf16))
    scratch = [
        pltpu.VMEM(fac_q.shape, bf16),
        pltpu.VMEM(fac_o.shape, bf16),
        pltpu.VMEM(half_q, bf16),
        pltpu.VMEM(half_q, bf16),
        pltpu.VMEM(half_o, bf16),
        pltpu.VMEM(half_o, bf16),
        pltpu.SemaphoreType.DMA((18,)),
    ]
    operands = [
        in_hbm(value) for value in (fac_q, fac_o, grad_q, error_q, grad_o, error_o)
    ]
    effort = cost(2 * rank * (grad_q.size + grad_o.size) // 2, 4 * grad_q.size)
    mat_q_far, mat_o_far, send = pl.pallas_call(
        far_kernel,
        out_shape=mats + (shaped((rank, columns), bf16),),
        in_specs=[in_place] * 6,
        out_specs=(whole,) * 3,
        scratch_shapes=scratch,
        compiler_params=params(16),
        cost_estimate=effort,
        name="project_far",
    )(*operands)
    mat_q_near, mat_o_near, part, norm = pl.pallas_call(
        near_kernel,
        out_shape=mats + (shaped((rank, columns), f32), shaped((norm_rows, lanes), f32)),
        in_specs=[in_place] * 6 + [whole],
        out_specs=(whole,) * 4,
        scratch_shapes=scratch,
        compiler_params=params(16),
        cost_estimate=effort,
        name="project_near",
    )(*operands, norm_grads)
    return mat_q_far, mat_o_far, send, mat_q_near, mat_o_near, part, norm


def small(kernel, name, outs, *operands):
    return pl.pallas_call(
        kernel,
        out_shape=outs,
        in_specs=[whole] * len(operands),
        out_specs=(whole,) * len(outs) if isinstance(outs, tuple) else whole,
        compiler_params=params(8),
        name=name,
    )(*operands)


def tree(parts):
    while len(parts) > 1:
        parts = [parts[place] + parts[place + 1] for place in range(0, len(parts), 2)]
    return parts[0]


def total_of(states, columns):
    return tree([state[:, :columns].astype(f32) for state in states])


def norm_of(states, columns):
    parts = []
    for state in states:
        part = state[:, columns:columns + lanes].astype(f32)
        if state.shape[1] > columns + lanes:
            part = part + state[:, columns + lanes:columns + 2 * lanes].astype(f32)
        parts.append(part)
    return tree(parts)


def store_norm(state, columns, total):
    high = total.astype(bf16)
    state[:, columns:columns + lanes] = high
    state[:, columns + lanes:columns + 2 * lanes] = (total - high.astype(f32)).astype(bf16)


def first_sum_kernel(part, norm, got, state):
    columns = part.shape[1]
    state[:, :columns] = (part[...] + got[...].astype(f32)).astype(bf16)
    state[:, columns:] = norm[...].astype(bf16)


def norm_sum_kernel(columns, *refs):
    *states, out = refs
    out[:, :columns] = total_of(states, columns).astype(bf16)
    store_norm(out, columns, norm_of(states, columns))


def plain_sum_kernel(*refs):
    *states, out = refs
    out[...] = total_of(states, out.shape[1]).astype(bf16)


def hat_kernel(size_q, columns, ginv_q, ginv_o, *refs):
    *states, out = refs
    total = total_of(states, columns)
    highest = lax.Precision.HIGHEST
    out[:, :size_q] = dot(ginv_q[...].T, total[:, :size_q], 1, 0, highest).astype(bf16)
    out[:, size_q:columns] = dot(ginv_o[...].T, total[:, size_q:], 1, 0, highest).astype(bf16)
    store_norm(out, columns, norm_of(states, columns))


def mean_kernel(count, norm_count, norm, norm_got, *refs):
    *states, new, norm_mean = refs
    new[...] = (total_of(states, new.shape[1]) / count).astype(bf16)
    norm_mean[...] = (norm[...] + norm_got[...]) / norm_count


def right_near_kernel(hat, mat_q, mat_o, part_q, part_o):
    size_q, size_o = mat_q.shape[0], mat_o.shape[0]
    part_q[...] = dot(hat[:, :size_q], mat_q[...], 1, 0)
    part_o[...] = dot(hat[:, size_q:size_q + size_o], mat_o[...], 1, 0)


def right_near(hat, mat_q, mat_o):
    rank = hat.shape[0]
    return pl.pallas_call(
        right_near_kernel,
        out_shape=(shaped((rank, mat_q.shape[1]), f32), shaped((rank, mat_o.shape[1]), f32)),
        in_specs=[whole] * 3,
        out_specs=(whole,) * 2,
        compiler_params=params(8),
        cost_estimate=cost(2 * rank * (mat_q.size + mat_o.size), 2 * (mat_q.size + mat_o.size)),
        name="right_near",
    )(hat, in_vmem(mat_q), in_vmem(mat_o))


def right_half(which, hat, mat_q, mat_o, part_q, part_o, store):
    size_q, size_o = mat_q.shape[0], mat_o.shape[0]
    half_q, half_o = mat_q.shape[1] // 2, mat_o.shape[1] // 2
    columns = half_at(which, half_q)
    store(0, half_q, part_q[:, columns] + dot(hat[:, :size_q], mat_q[:, columns], 1, 0))
    columns = half_at(which, half_o)
    store(half_q, half_o, part_o[:, columns] + dot(
        hat[:, size_q:size_q + size_o], mat_o[:, columns], 1, 0
    ))


def right_send_kernel(hat, mat_q, mat_o, part_q, part_o, send):
    def store(column, width, value):
        send[:, column:column + width] = value.astype(bf16)

    right_half(1 - parity(), hat, mat_q, mat_o, part_q, part_o, store)


def right_keep_kernel(hat, mat_q, mat_o, part_q, part_o, hat_near, near, norm):
    def store(column, width, value):
        near[:, column:column + width] = value

    right_half(parity(), hat, mat_q, mat_o, part_q, part_o, store)
    norm[...] = norm_of([hat_near, hat], mat_q.shape[0] + mat_o.shape[0])


def right_far(hat, mat_q, mat_o, part_q, part_o, hat_near, norm_rows):
    rank = hat.shape[0]
    columns = (mat_q.shape[1] + mat_o.shape[1]) // 2
    operands = (hat, in_vmem(mat_q), in_vmem(mat_o), part_q, part_o)
    effort = cost(rank * (mat_q.size + mat_o.size), mat_q.size + mat_o.size)
    send = pl.pallas_call(
        right_send_kernel,
        out_shape=shaped((rank, columns), bf16),
        in_specs=[whole] * 5,
        out_specs=whole,
        compiler_params=params(8),
        cost_estimate=effort,
        name="right_send",
    )(*operands)
    near, norm = pl.pallas_call(
        right_keep_kernel,
        out_shape=(shaped((rank, columns), f32), shaped((norm_rows, lanes), f32)),
        in_specs=[whole] * 6,
        out_specs=(whole,) * 2,
        compiler_params=params(8),
        cost_estimate=effort,
        name="right_keep",
    )(*operands, hat_near)
    return send, near, norm


def near_sum_kernel(near, got, norm, norm_got, state, norm_sum):
    state[...] = (near[...] + got[...].astype(f32)).astype(bf16)
    norm_sum[...] = norm[...] + norm_got[...]


def error_columns(column, hat, hat_row, half, mat_q, mat_o, new, error_q, error_o, stage_q, stage_o, sems, slot):
    size_q, size_o = mat_q.shape[0], mat_o.shape[0]
    wide_q, wide_o = stage_q.shape[1], stage_o.shape[1]
    copies = []
    chunk_q, chunk_o = size_q // 2, size_o // 2
    cols_q, cols_o = half_at(column, wide_q), half_at(column, wide_o)
    for chunk in range(2):
        part = pl.ds(chunk * chunk_q, chunk_q)
        stage = pl.ds(hat_row * size_q + chunk * chunk_q, chunk_q)
        approx = dot(hat[:, part], new[:, :wide_q], 0, 0)
        stage_q[stage] = (mat_q[part, cols_q].astype(f32) - approx).astype(bf16)
        there = pl.ds(pl.multiple_of(half * size_q + chunk * chunk_q, chunk_q), chunk_q)
        copies.append(load(stage_q.at[stage], error_q.at[there, cols_q], sems.at[slot]))
        part = pl.ds(chunk * chunk_o, chunk_o)
        stage = pl.ds(hat_row * size_o + chunk * chunk_o, chunk_o)
        approx = dot(hat[:, size_q + chunk * chunk_o:size_q + (chunk + 1) * chunk_o], new[:, wide_q:], 0, 0)
        stage_o[stage] = (mat_o[part, cols_o].astype(f32) - approx).astype(bf16)
        there = pl.ds(pl.multiple_of(half * size_o + chunk * chunk_o, chunk_o), chunk_o)
        copies.append(load(stage_o.at[stage], error_o.at[there, cols_o], sems.at[slot + 1]))
        slot += 2
    return copies


def piece_of(near, far, index, count, size, pieces):
    half = count // 2
    here = index // half == parity()
    slot = lax.rem(index, half)
    if size % lanes == 0:
        part = half_at(slot, size)
        return jnp.where(here, near[:, part].astype(f32), far[:, part].astype(f32)).astype(bf16)
    width = half * size
    chosen = jnp.where(here, near[:, :width].astype(f32), far[:, :width].astype(f32))
    for place in range(half):
        pieces[place] = chosen[:, place * size:(place + 1) * size]
    return pieces[slot].astype(bf16)


def finish_near_kernel(
    count, hat_near, hat_far, mat_q_near, mat_o_near, mat_q_far, mat_o_far, new, weight_q, momentum_q,
    error_q, error_o, momentum_q_h, weight_q_h,
    stage_q, stage_o, momentum_q_new, weight_q_new, pieces, sems, out_sems
):
    mine = parity()
    me = lax.axis_index("replica")
    copies = error_columns(
        mine, hat_near, 0, mine, mat_q_near, mat_o_near, new, error_q, error_o, stage_q, stage_o, sems, 0
    ) + error_columns(
        mine, hat_far, 1, 1 - mine, mat_q_far, mat_o_far, new, error_q, error_o, stage_q, stage_o, sems, 4
    )
    piece = piece_of(hat_near, hat_far, me, count, weight_q.shape[0], pieces)
    copies += query_columns(
        mine, piece, new, weight_q, momentum_q, momentum_q_new, weight_q_new,
        momentum_q_h, weight_q_h, out_sems
    )
    for copy in copies:
        copy.wait()


def query_columns(
    which, piece, new, weight, momentum, momentum_new, weight_new, momentum_h, weight_h, sems
):
    wide = momentum_new.shape[1]
    columns = half_at(which, wide)
    moved = momentum_decay * momentum[:, columns] + dot(piece, new[:, :wide], 0, 0)
    momentum_new[...] = moved
    weight_new[...] = weight[:, columns] - step_size * moved
    return [
        load(momentum_new, momentum_h.at[:, columns], sems.at[0]),
        load(weight_new, weight_h.at[:, columns], sems.at[1]),
    ]


def finish_far_kernel(
    count, hat_near, hat_far, mat_q_near, mat_o_near, mat_q_far, mat_o_far,
    new_near, new_far, weight_q, momentum_q, weight_o, momentum_o, norm,
    error_q_in, error_o_in, momentum_q_in, weight_q_in,
    error_q, error_o, momentum_q_h, weight_q_h, new_q_h, new_o_h, momentum_o_h, weight_o_h, norm_h,
    stage_q, stage_o, momentum_q_new, weight_q_new, new_q, new_o, momentum_o_new, weight_o_new,
    pieces_q, pieces_o, sems, out_sems
):
    mine = parity()
    me = lax.axis_index("replica")
    wide_q, wide_o = stage_q.shape[1], stage_o.shape[1]
    size_q = mat_q_near.shape[0]
    size_o = mat_o_near.shape[0]
    new_q[:, half_at(mine, wide_q)] = new_near[:, :wide_q]
    new_q[:, half_at(1 - mine, wide_q)] = new_far[:, :wide_q]
    new_o[:, half_at(mine, wide_o)] = new_near[:, wide_q:]
    new_o[:, half_at(1 - mine, wide_o)] = new_far[:, wide_q:]
    copies = [
        load(new_q, new_q_h, out_sems.at[0]),
        load(new_o, new_o_h, out_sems.at[1]),
        load(norm, norm_h, out_sems.at[2]),
    ]
    copies += error_columns(
        1 - mine, hat_near, 0, mine, mat_q_near, mat_o_near, new_far,
        error_q, error_o, stage_q, stage_o, sems, 0
    )
    piece = piece_of(
        new_near.at[:, wide_q:], new_far.at[:, wide_q:], me, count, weight_o.shape[1], pieces_o
    )
    for which, hat in ((mine, hat_near), (1 - mine, hat_far)):
        rows = half_at(which, size_o)
        moved = momentum_decay * momentum_o[rows] + dot(hat[:, size_q:size_q + size_o], piece, 0, 0)
        momentum_o_new[rows] = moved
        weight_o_new[rows] = weight_o[rows] - step_size * moved
    copies.append(load(momentum_o_new, momentum_o_h, out_sems.at[3]))
    copies.append(load(weight_o_new, weight_o_h, out_sems.at[4]))
    copies += error_columns(
        1 - mine, hat_far, 1, 1 - mine, mat_q_far, mat_o_far, new_far,
        error_q, error_o, stage_q, stage_o, sems, 4
    )
    piece = piece_of(hat_near, hat_far, me, count, weight_q.shape[0], pieces_q)
    copies += query_columns(
        1 - mine, piece, new_far, weight_q, momentum_q, momentum_q_new, weight_q_new,
        momentum_q_h, weight_q_h, out_sems.at[5:7]
    )
    for copy in copies:
        copy.wait()


def finish(count, hat_near, hat_far, mats, new_near, weights, norm):
    mat_q, mat_o = mats[0], mats[1]
    weight_q, _, weight_o, _ = weights
    rank = hat_near.shape[0]
    size_q, size_o = mat_q.shape[0], mat_o.shape[0]
    early = (
        shaped((2 * size_q, mat_q.shape[1]), bf16),
        shaped((2 * size_o, mat_o.shape[1]), bf16),
        shaped(weight_q.shape, f32),
        shaped(weight_q.shape, f32),
    )
    late = (
        shaped((rank, mat_q.shape[1]), bf16),
        shaped((rank, mat_o.shape[1]), bf16),
        shaped(weight_o.shape, f32),
        shaped(weight_o.shape, f32),
    )
    piece_q = (weight_q.shape[0], weight_q.shape[1] // 2)
    stages = [
        pltpu.VMEM((2 * size_q, mat_q.shape[1] // 2), bf16),
        pltpu.VMEM((2 * size_o, mat_o.shape[1] // 2), bf16),
        pltpu.VMEM(piece_q, f32),
        pltpu.VMEM(piece_q, f32),
    ]
    pieces_q = pltpu.VMEM((count // 2, rank, weight_q.shape[0]), f32)
    pieces_o = pltpu.VMEM((count // 2, rank, weight_o.shape[1]), f32)
    moved = 4 * (mat_q.size + mat_o.size)
    mats = [in_vmem(mat) for mat in mats]
    weights = [in_vmem(value) for value in weights]
    new_far = swap_halves(new_near)
    parts = pl.pallas_call(
        functools.partial(finish_near_kernel, count),
        out_shape=early,
        in_specs=[whole] * 9,
        out_specs=(in_place,) * 4,
        scratch_shapes=stages + [
            pieces_q, pltpu.SemaphoreType.DMA((8,)), pltpu.SemaphoreType.DMA((2,))
        ],
        compiler_params=params(12),
        cost_estimate=cost(2 * rank * (mat_q.size + mat_o.size), moved),
        name="finish_near",
    )(hat_near, hat_far, *mats, new_near, *weights[:2])
    return pl.pallas_call(
        functools.partial(finish_far_kernel, count),
        out_shape=early + late + (shaped(norm.shape, f32),),
        in_specs=[whole] * 13 + [in_place] * 4,
        out_specs=(in_place,) * 9,
        scratch_shapes=stages + [pltpu.VMEM(out.shape, out.dtype) for out in late] + [
            pieces_q, pieces_o, pltpu.SemaphoreType.DMA((8,)), pltpu.SemaphoreType.DMA((7,))
        ],
        input_output_aliases={13: 0, 14: 1, 15: 2, 16: 3},
        compiler_params=params(16),
        cost_estimate=cost(2 * rank * (mat_q.size + mat_o.size), moved),
        name="finish_far",
    )(hat_near, hat_far, *mats, new_near, new_far, *weights, norm, *parts)


def swap(value, even, odd):
    replicas, tensors = lax.axis_size("replica"), lax.axis_size("tensor")
    pairs = []
    for replica in range(replicas):
        for tensor in range(tensors):
            target = replica ^ (odd if tensor % 2 else even)
            pairs.append((replica * tensors + tensor, target * tensors + tensor))
    return lax.ppermute(value, ("replica", "tensor"), pairs)


def swap_halves(value):
    return swap(value, 1, lax.axis_size("replica") // 2)


def swap_tensor(value, bit):
    count = lax.axis_size("tensor")
    return lax.ppermute(value, "tensor", [(source, source ^ bit) for source in range(count)])


def exchange(state, bits):
    offsets = [(0, 0)]
    for even, odd in bits:
        offsets += [(first | even, second | odd) for first, second in offsets]
    got = [swap(state, *offset) for offset in offsets[:0:-1]]
    return [state] + got[::-1]


def rounds_of(count):
    places = range(1, count.bit_length() - 1)
    bits = [(1 << place, 1 << (place - 1)) for place in places]
    return [bits[place:place + 2] for place in range(0, len(bits), 2)]


def on_device(
    grad_q,
    error_q,
    qfac_q,
    ginv_q,
    weight_q,
    momentum_q,
    grad_o,
    error_o,
    qfac_o,
    ginv_o,
    weight_o,
    momentum_o,
    norm_grads,
):
    replicas = lax.axis_size("replica")
    tensors = lax.axis_size("tensor")
    rank = qfac_q.shape[1]
    half_q = grad_q.shape[0] // 2
    norm_rows = norm_grads.size // lanes
    mat_q_far, mat_o_far, send, mat_q_near, mat_o_near, part, norm = project(
        grad_q, error_q, grad_o, error_o, qfac_q.T, qfac_o.T, norm_grads
    )
    columns = part.shape[1]
    rounds = rounds_of(replicas)
    state = small(
        first_sum_kernel, "first_sum", shaped((rank, columns + lanes), bf16), part, norm, swap_halves(send)
    )
    wide = shaped((rank, columns + 2 * lanes), bf16)
    for bits in rounds[:-1]:
        state = small(
            functools.partial(norm_sum_kernel, columns), "norm_sum", wide, *exchange(state, bits)
        )
    hat_near = small(
        functools.partial(hat_kernel, half_q, columns), "hats", wide,
        ginv_q, ginv_o, *exchange(state, rounds[-1]),
    )
    hat_far = swap_halves(hat_near)
    part_q, part_o = right_near(hat_near, mat_q_near, mat_o_near)
    send, near, norm = right_far(
        hat_far, mat_q_far, mat_o_far, part_q, part_o, hat_near, norm_rows
    )
    state, norm = small(
        near_sum_kernel, "near_sum", (shaped(send.shape, bf16), shaped(norm.shape, f32)),
        near, swap_halves(send), norm, swap_tensor(norm, 1),
    )
    for bits in rounds[:-1]:
        state = small(
            plain_sum_kernel, "plain_sum", shaped(state.shape, bf16), *exchange(state, bits)
        )
    states = exchange(state, rounds[-1])
    new_near, norm = small(
        functools.partial(mean_kernel, replicas, replicas * tensors), "mean",
        (shaped(state.shape, bf16), shaped(norm.shape, f32)),
        norm, swap_tensor(norm, 2), *states,
    )
    (
        error_q_new, error_o_new, momentum_q_new, weight_q_new,
        new_q, new_o, momentum_o_new, weight_o_new, norm_mean,
    ) = finish(
        replicas, hat_near, hat_far,
        (mat_q_near, mat_o_near, mat_q_far, mat_o_far), new_near,
        (weight_q, momentum_q, weight_o, momentum_o), norm,
    )
    return (
        error_q_new,
        new_q.T,
        momentum_q_new,
        weight_q_new,
        error_o_new,
        new_o.T,
        momentum_o_new,
        weight_o_new,
        norm_mean.reshape(-1),
    )


def solution(mesh):
    in_specs = (
        P("replica", "tensor"),
        P("replica", "tensor"),
        P("tensor", None),
        P("tensor", None),
        P("replica", "tensor"),
        P("replica", "tensor"),
        P(("replica", "tensor"), None),
        P(("replica", "tensor"), None),
        P("tensor", None),
        P("tensor", None),
        P("tensor", "replica"),
        P("tensor", "replica"),
        P("replica", "tensor", None),
    )
    out_specs = (
        P("replica", "tensor"),
        P("tensor", None),
        P("replica", "tensor"),
        P("replica", "tensor"),
        P(("replica", "tensor"), None),
        P("tensor", None),
        P("tensor", "replica"),
        P("tensor", "replica"),
        P(),
    )
    return jax.shard_map(
        on_device, mesh=mesh, in_specs=in_specs, out_specs=out_specs, check_vma=False
    )
```

```python
import functools

import jax
import jax.numpy as jnp
from jax import lax
from jax.experimental import pallas as pl
from jax.experimental.pallas import tpu as pltpu
from jax.sharding import PartitionSpec as P

momentum_decay = 0.9
step_size = 0.5
lanes = 128
mib = 1024 * 1024
bf16 = jnp.bfloat16
f32 = jnp.float32

whole = pl.BlockSpec(memory_space=pltpu.VMEM)
in_place = pl.BlockSpec(memory_space=pl.ANY)


def dot(left, right, left_dim, right_dim, precision=None):
    return lax.dot_general(
        left,
        right,
        (((left_dim,), (right_dim,)), ((), ())),
        precision=precision,
        preferred_element_type=f32,
    )


def params(limit):
    return pltpu.CompilerParams(vmem_limit_bytes=limit * mib)


def cost(flops, moved):
    return pl.CostEstimate(flops=flops, bytes_accessed=moved, transcendentals=0)


def in_hbm(value):
    return pltpu.with_memory_space_constraint(value, pltpu.HBM)


def in_vmem(value):
    return pltpu.with_memory_space_constraint(value, pltpu.VMEM)


def shaped(shape, dtype):
    return jax.ShapeDtypeStruct(shape, dtype)


def parity():
    replica = lax.axis_index("replica")
    odd = lax.rem(lax.axis_index("tensor"), 2) == 1
    return jnp.where(odd, replica // (lax.axis_size("replica") // 2), lax.rem(replica, 2))


def half_at(which, size):
    return pl.ds(pl.multiple_of(which * size, size), size)


def load(source, target, sem):
    copy = pltpu.make_async_copy(source, target, sem)
    copy.start()
    return copy


def project_half(
    which, fac_q_h, fac_o_h, grad_q, error_q, grad_o, error_o, mat_q, mat_o, store,
    fac_q, fac_o, grad_q_v, error_q_v, grad_o_v, error_o_v, sems,
):
    half_q, half_o = mat_q.shape[0], mat_o.shape[0]
    steps = 4
    rows_q, rows_o = half_q // steps, half_o // steps
    fac_copies = [load(fac_q_h, fac_q, sems.at[0]), load(fac_o_h, fac_o, sems.at[1])]
    jobs = []
    for step in range(steps):
        slot = 2 + 4 * step
        part_q = pl.ds(step * rows_q, rows_q)
        part_o = pl.ds(step * rows_o, rows_o)
        there_q = pl.ds(pl.multiple_of(which * half_q + step * rows_q, rows_q), rows_q)
        there_o = pl.ds(pl.multiple_of(which * half_o + step * rows_o, rows_o), rows_o)
        jobs.append((step, part_q, part_o, (
            load(grad_q.at[there_q], grad_q_v.at[part_q], sems.at[slot]),
            load(error_q.at[there_q], error_q_v.at[part_q], sems.at[slot + 1]),
            load(grad_o.at[there_o], grad_o_v.at[part_o], sems.at[slot + 2]),
            load(error_o.at[there_o], error_o_v.at[part_o], sems.at[slot + 3]),
        )))
    for copy in fac_copies:
        copy.wait()
    columns_o = fac_o[...].T
    for step, part_q, part_o, copies in jobs:
        for copy in copies:
            copy.wait()
        block_q = grad_q_v[part_q] + error_q_v[part_q]
        block_o = grad_o_v[part_o] + error_o_v[part_o]
        mat_q[part_q] = block_q
        mat_o[part_o] = block_o
        store(step * rows_q, dot(fac_q[...], block_q, 1, 1))
        store(half_q + step * rows_o, dot(block_o, columns_o, 1, 0).T)


def far_kernel(
    fac_q_h, fac_o_h, grad_q, error_q, grad_o, error_o, mat_q, mat_o, send, *scratch
):
    def store(column, value):
        send[:, column:column + value.shape[1]] = value.astype(bf16)

    project_half(
        1 - parity(), fac_q_h, fac_o_h, grad_q, error_q, grad_o, error_o,
        mat_q, mat_o, store, *scratch
    )


def near_kernel(
    fac_q_h, fac_o_h, grad_q, error_q, grad_o, error_o, norm_grads,
    mat_q, mat_o, part, norm, *scratch
):
    def store(column, value):
        part[:, column:column + value.shape[1]] = value

    project_half(
        parity(), fac_q_h, fac_o_h, grad_q, error_q, grad_o, error_o,
        mat_q, mat_o, store, *scratch
    )
    values = norm_grads[0].astype(f32)
    for row in range(norm.shape[0]):
        norm[row:row + 1, :] = values[:, row * lanes:(row + 1) * lanes]


def project(grad_q, error_q, grad_o, error_o, fac_q, fac_o, norm_grads):
    rank = fac_q.shape[0]
    half_q = (grad_q.shape[0] // 2, grad_q.shape[1])
    half_o = (grad_o.shape[0] // 2, grad_o.shape[1])
    columns = half_q[0] + half_o[0]
    norm_rows = norm_grads.size // lanes
    mats = (pltpu.VMEM(half_q, bf16), pltpu.VMEM(half_o, bf16))
    scratch = [
        pltpu.VMEM(fac_q.shape, bf16),
        pltpu.VMEM(fac_o.shape, bf16),
        pltpu.VMEM(half_q, bf16),
        pltpu.VMEM(half_q, bf16),
        pltpu.VMEM(half_o, bf16),
        pltpu.VMEM(half_o, bf16),
        pltpu.SemaphoreType.DMA((18,)),
    ]
    operands = [
        in_hbm(value) for value in (fac_q, fac_o, grad_q, error_q, grad_o, error_o)
    ]
    effort = cost(2 * rank * (grad_q.size + grad_o.size) // 2, 4 * grad_q.size)
    mat_q_far, mat_o_far, send = pl.pallas_call(
        far_kernel,
        out_shape=mats + (shaped((rank, columns), bf16),),
        in_specs=[in_place] * 6,
        out_specs=(whole,) * 3,
        scratch_shapes=scratch,
        compiler_params=params(16),
        cost_estimate=effort,
        name="project_far",
    )(*operands)
    mat_q_near, mat_o_near, part, norm = pl.pallas_call(
        near_kernel,
        out_shape=mats + (shaped((rank, columns), f32), shaped((norm_rows, lanes), f32)),
        in_specs=[in_place] * 6 + [whole],
        out_specs=(whole,) * 4,
        scratch_shapes=scratch,
        compiler_params=params(16),
        cost_estimate=effort,
        name="project_near",
    )(*operands, norm_grads)
    return mat_q_far, mat_o_far, send, mat_q_near, mat_o_near, part, norm


def small(kernel, name, outs, *operands):
    return pl.pallas_call(
        kernel,
        out_shape=outs,
        in_specs=[whole] * len(operands),
        out_specs=(whole,) * len(outs) if isinstance(outs, tuple) else whole,
        compiler_params=params(8),
        name=name,
    )(*operands)


def store_all(out, column, value):
    for slot in range(out.shape[0]):
        out[slot, :, column:column + value.shape[1]] = value


def tree(parts):
    while len(parts) > 1:
        parts = [parts[place] + parts[place + 1] for place in range(0, len(parts), 2)]
    return parts[0]


def total_of(states, columns):
    return tree([states[slot, :, :columns].astype(f32) for slot in range(states.shape[0])])


def norm_of(states, columns):
    parts = []
    if not isinstance(states, list):
        states = [states.at[slot] for slot in range(states.shape[0])]
    for state in states:
        part = state[:, columns:columns + lanes].astype(f32)
        if state.shape[1] > columns + lanes:
            part = part + state[:, columns + lanes:columns + 2 * lanes].astype(f32)
        parts.append(part)
    return tree(parts)


def store_norm(state, columns, total):
    high = total.astype(bf16)
    state[:, columns:columns + lanes] = high
    state[:, columns + lanes:columns + 2 * lanes] = (total - high.astype(f32)).astype(bf16)


def first_sum_kernel(part, norm, got, state):
    store_all(state, 0, (part[...] + got[...].astype(f32)).astype(bf16))
    store_all(state, part.shape[1], norm[...].astype(bf16))


def norm_sum_kernel(columns, states, out):
    store_all(out, 0, total_of(states, columns).astype(bf16))
    total = norm_of(states, columns)
    high = total.astype(bf16)
    store_all(out, columns, high)
    store_all(out, columns + lanes, (total - high.astype(f32)).astype(bf16))


def plain_sum_kernel(states, out):
    store_all(out, 0, total_of(states, out.shape[2]).astype(bf16))


def hat_kernel(size_q, columns, ginv_q, ginv_o, states, out):
    total = total_of(states, columns)
    highest = lax.Precision.HIGHEST
    out[:, :size_q] = dot(ginv_q[...].T, total[:, :size_q], 1, 0, highest).astype(bf16)
    out[:, size_q:columns] = dot(ginv_o[...].T, total[:, size_q:], 1, 0, highest).astype(bf16)
    store_norm(out, columns, norm_of(states, columns))


def mean_kernel(count, norm_count, norm, norm_got, states, new, norm_mean):
    new[...] = (total_of(states, new.shape[1]) / count).astype(bf16)
    norm_mean[...] = (norm[...] + norm_got[...]) / norm_count


def right_near_kernel(hat, mat_q, mat_o, part_q, part_o):
    size_q, size_o = mat_q.shape[0], mat_o.shape[0]
    part_q[...] = dot(hat[:, :size_q], mat_q[...], 1, 0)
    part_o[...] = dot(hat[:, size_q:size_q + size_o], mat_o[...], 1, 0)


def right_near(hat, mat_q, mat_o):
    rank = hat.shape[0]
    return pl.pallas_call(
        right_near_kernel,
        out_shape=(shaped((rank, mat_q.shape[1]), f32), shaped((rank, mat_o.shape[1]), f32)),
        in_specs=[whole] * 3,
        out_specs=(whole,) * 2,
        compiler_params=params(8),
        cost_estimate=cost(2 * rank * (mat_q.size + mat_o.size), 2 * (mat_q.size + mat_o.size)),
        name="right_near",
    )(hat, in_vmem(mat_q), in_vmem(mat_o))


def right_half(which, hat, mat_q, mat_o, part_q, part_o, store):
    size_q, size_o = mat_q.shape[0], mat_o.shape[0]
    half_q, half_o = mat_q.shape[1] // 2, mat_o.shape[1] // 2
    columns = half_at(which, half_q)
    store(0, half_q, part_q[:, columns] + dot(hat[:, :size_q], mat_q[:, columns], 1, 0))
    columns = half_at(which, half_o)
    store(half_q, half_o, part_o[:, columns] + dot(
        hat[:, size_q:size_q + size_o], mat_o[:, columns], 1, 0
    ))


def right_send_kernel(hat, mat_q, mat_o, part_q, part_o, send):
    def store(column, width, value):
        send[:, column:column + width] = value.astype(bf16)

    right_half(1 - parity(), hat, mat_q, mat_o, part_q, part_o, store)


def right_keep_kernel(hat, mat_q, mat_o, part_q, part_o, hat_near, near, norm):
    def store(column, width, value):
        near[:, column:column + width] = value

    right_half(parity(), hat, mat_q, mat_o, part_q, part_o, store)
    norm[...] = norm_of([hat_near, hat], mat_q.shape[0] + mat_o.shape[0])


def right_far(hat, mat_q, mat_o, part_q, part_o, hat_near, norm_rows):
    rank = hat.shape[0]
    columns = (mat_q.shape[1] + mat_o.shape[1]) // 2
    operands = (hat, in_vmem(mat_q), in_vmem(mat_o), part_q, part_o)
    effort = cost(rank * (mat_q.size + mat_o.size), mat_q.size + mat_o.size)
    send = pl.pallas_call(
        right_send_kernel,
        out_shape=shaped((rank, columns), bf16),
        in_specs=[whole] * 5,
        out_specs=whole,
        compiler_params=params(8),
        cost_estimate=effort,
        name="right_send",
    )(*operands)
    near, norm = pl.pallas_call(
        right_keep_kernel,
        out_shape=(shaped((rank, columns), f32), shaped((norm_rows, lanes), f32)),
        in_specs=[whole] * 6,
        out_specs=(whole,) * 2,
        compiler_params=params(8),
        cost_estimate=effort,
        name="right_keep",
    )(*operands, hat_near)
    return send, near, norm


def near_sum_kernel(near, got, norm, norm_got, state, norm_sum):
    store_all(state, 0, (near[...] + got[...].astype(f32)).astype(bf16))
    norm_sum[...] = norm[...] + norm_got[...]


def error_columns(column, hat, hat_row, half, mat_q, mat_o, new, error_q, error_o, stage_q, stage_o, sems, slot):
    size_q, size_o = mat_q.shape[0], mat_o.shape[0]
    wide_q, wide_o = stage_q.shape[1], stage_o.shape[1]
    copies = []
    chunk_q, chunk_o = size_q // 2, size_o // 2
    cols_q, cols_o = half_at(column, wide_q), half_at(column, wide_o)
    for chunk in range(2):
        part = pl.ds(chunk * chunk_q, chunk_q)
        stage = pl.ds(hat_row * size_q + chunk * chunk_q, chunk_q)
        approx = dot(hat[:, part], new[:, :wide_q], 0, 0)
        stage_q[stage] = (mat_q[part, cols_q].astype(f32) - approx).astype(bf16)
        there = pl.ds(pl.multiple_of(half * size_q + chunk * chunk_q, chunk_q), chunk_q)
        copies.append(load(stage_q.at[stage], error_q.at[there, cols_q], sems.at[slot]))
        part = pl.ds(chunk * chunk_o, chunk_o)
        stage = pl.ds(hat_row * size_o + chunk * chunk_o, chunk_o)
        approx = dot(hat[:, size_q + chunk * chunk_o:size_q + (chunk + 1) * chunk_o], new[:, wide_q:], 0, 0)
        stage_o[stage] = (mat_o[part, cols_o].astype(f32) - approx).astype(bf16)
        there = pl.ds(pl.multiple_of(half * size_o + chunk * chunk_o, chunk_o), chunk_o)
        copies.append(load(stage_o.at[stage], error_o.at[there, cols_o], sems.at[slot + 1]))
        slot += 2
    return copies


def piece_of(near, far, index, count, size, pieces):
    half = count // 2
    here = index // half == parity()
    slot = lax.rem(index, half)
    if size % lanes == 0:
        part = half_at(slot, size)
        return jnp.where(here, near[:, part].astype(f32), far[:, part].astype(f32)).astype(bf16)
    width = half * size
    chosen = jnp.where(here, near[:, :width].astype(f32), far[:, :width].astype(f32))
    for place in range(half):
        pieces[place] = chosen[:, place * size:(place + 1) * size]
    return pieces[slot].astype(bf16)


def finish_near_kernel(
    count, hat_near, hat_far, mat_q_near, mat_o_near, mat_q_far, mat_o_far, new, weight_q, momentum_q,
    error_q, error_o, momentum_q_h, weight_q_h,
    stage_q, stage_o, momentum_q_new, weight_q_new, pieces, sems, out_sems
):
    mine = parity()
    me = lax.axis_index("replica")
    copies = error_columns(
        mine, hat_near, 0, mine, mat_q_near, mat_o_near, new, error_q, error_o, stage_q, stage_o, sems, 0
    ) + error_columns(
        mine, hat_far, 1, 1 - mine, mat_q_far, mat_o_far, new, error_q, error_o, stage_q, stage_o, sems, 4
    )
    piece = piece_of(hat_near, hat_far, me, count, weight_q.shape[0], pieces)
    copies += query_columns(
        mine, piece, new, weight_q, momentum_q, momentum_q_new, weight_q_new,
        momentum_q_h, weight_q_h, out_sems
    )
    for copy in copies:
        copy.wait()


def query_columns(
    which, piece, new, weight, momentum, momentum_new, weight_new, momentum_h, weight_h, sems
):
    wide = momentum_new.shape[1]
    columns = half_at(which, wide)
    moved = momentum_decay * momentum[:, columns] + dot(piece, new[:, :wide], 0, 0)
    momentum_new[...] = moved
    weight_new[...] = weight[:, columns] - step_size * moved
    return [
        load(momentum_new, momentum_h.at[:, columns], sems.at[0]),
        load(weight_new, weight_h.at[:, columns], sems.at[1]),
    ]


def finish_far_kernel(
    count, hat_near, hat_far, mat_q_near, mat_o_near, mat_q_far, mat_o_far,
    new_near, new_far, weight_q, momentum_q, weight_o, momentum_o, norm,
    error_q_in, error_o_in, momentum_q_in, weight_q_in,
    error_q, error_o, momentum_q_h, weight_q_h, new_q_h, new_o_h, momentum_o_h, weight_o_h, norm_h,
    stage_q, stage_o, momentum_q_new, weight_q_new, new_q, new_o, momentum_o_new, weight_o_new,
    pieces_q, pieces_o, sems, out_sems
):
    mine = parity()
    me = lax.axis_index("replica")
    wide_q, wide_o = stage_q.shape[1], stage_o.shape[1]
    size_q = mat_q_near.shape[0]
    size_o = mat_o_near.shape[0]
    new_q[:, half_at(mine, wide_q)] = new_near[:, :wide_q]
    new_q[:, half_at(1 - mine, wide_q)] = new_far[:, :wide_q]
    new_o[:, half_at(mine, wide_o)] = new_near[:, wide_q:]
    new_o[:, half_at(1 - mine, wide_o)] = new_far[:, wide_q:]
    copies = [
        load(new_q, new_q_h, out_sems.at[0]),
        load(new_o, new_o_h, out_sems.at[1]),
        load(norm, norm_h, out_sems.at[2]),
    ]
    copies += error_columns(
        1 - mine, hat_near, 0, mine, mat_q_near, mat_o_near, new_far,
        error_q, error_o, stage_q, stage_o, sems, 0
    )
    piece = piece_of(
        new_near.at[:, wide_q:], new_far.at[:, wide_q:], me, count, weight_o.shape[1], pieces_o
    )
    for which, hat in ((mine, hat_near), (1 - mine, hat_far)):
        rows = half_at(which, size_o)
        moved = momentum_decay * momentum_o[rows] + dot(hat[:, size_q:size_q + size_o], piece, 0, 0)
        momentum_o_new[rows] = moved
        weight_o_new[rows] = weight_o[rows] - step_size * moved
    copies.append(load(momentum_o_new, momentum_o_h, out_sems.at[3]))
    copies.append(load(weight_o_new, weight_o_h, out_sems.at[4]))
    copies += error_columns(
        1 - mine, hat_far, 1, 1 - mine, mat_q_far, mat_o_far, new_far,
        error_q, error_o, stage_q, stage_o, sems, 4
    )
    piece = piece_of(hat_near, hat_far, me, count, weight_q.shape[0], pieces_q)
    copies += query_columns(
        1 - mine, piece, new_far, weight_q, momentum_q, momentum_q_new, weight_q_new,
        momentum_q_h, weight_q_h, out_sems.at[5:7]
    )
    for copy in copies:
        copy.wait()


def finish(count, hat_near, hat_far, mats, new_near, weights, norm):
    mat_q, mat_o = mats[0], mats[1]
    weight_q, _, weight_o, _ = weights
    rank = hat_near.shape[0]
    size_q, size_o = mat_q.shape[0], mat_o.shape[0]
    early = (
        shaped((2 * size_q, mat_q.shape[1]), bf16),
        shaped((2 * size_o, mat_o.shape[1]), bf16),
        shaped(weight_q.shape, f32),
        shaped(weight_q.shape, f32),
    )
    late = (
        shaped((rank, mat_q.shape[1]), bf16),
        shaped((rank, mat_o.shape[1]), bf16),
        shaped(weight_o.shape, f32),
        shaped(weight_o.shape, f32),
    )
    piece_q = (weight_q.shape[0], weight_q.shape[1] // 2)
    stages = [
        pltpu.VMEM((2 * size_q, mat_q.shape[1] // 2), bf16),
        pltpu.VMEM((2 * size_o, mat_o.shape[1] // 2), bf16),
        pltpu.VMEM(piece_q, f32),
        pltpu.VMEM(piece_q, f32),
    ]
    pieces_q = pltpu.VMEM((count // 2, rank, weight_q.shape[0]), f32)
    pieces_o = pltpu.VMEM((count // 2, rank, weight_o.shape[1]), f32)
    moved = 4 * (mat_q.size + mat_o.size)
    mats = [in_vmem(mat) for mat in mats]
    weights = [in_vmem(value) for value in weights]
    new_far = swap_halves(new_near)
    parts = pl.pallas_call(
        functools.partial(finish_near_kernel, count),
        out_shape=early,
        in_specs=[whole] * 9,
        out_specs=(in_place,) * 4,
        scratch_shapes=stages + [
            pieces_q, pltpu.SemaphoreType.DMA((8,)), pltpu.SemaphoreType.DMA((2,))
        ],
        compiler_params=params(12),
        cost_estimate=cost(2 * rank * (mat_q.size + mat_o.size), moved),
        name="finish_near",
    )(hat_near, hat_far, *mats, new_near, *weights[:2])
    return pl.pallas_call(
        functools.partial(finish_far_kernel, count),
        out_shape=early + late + (shaped(norm.shape, f32),),
        in_specs=[whole] * 13 + [in_place] * 4,
        out_specs=(in_place,) * 9,
        scratch_shapes=stages + [pltpu.VMEM(out.shape, out.dtype) for out in late] + [
            pieces_q, pieces_o, pltpu.SemaphoreType.DMA((8,)), pltpu.SemaphoreType.DMA((7,))
        ],
        input_output_aliases={13: 0, 14: 1, 15: 2, 16: 3},
        compiler_params=params(16),
        cost_estimate=cost(2 * rank * (mat_q.size + mat_o.size), moved),
        name="finish_far",
    )(hat_near, hat_far, *mats, new_near, new_far, *weights, norm, *parts)


def swap(value, even, odd):
    replicas, tensors = lax.axis_size("replica"), lax.axis_size("tensor")
    pairs = []
    for replica in range(replicas):
        for tensor in range(tensors):
            target = replica ^ (odd if tensor % 2 else even)
            pairs.append((replica * tensors + tensor, target * tensors + tensor))
    return lax.ppermute(value, ("replica", "tensor"), pairs)


def swap_halves(value):
    return swap(value, 1, lax.axis_size("replica") // 2)


def swap_tensor(value, bit):
    count = lax.axis_size("tensor")
    return lax.ppermute(value, "tensor", [(source, source ^ bit) for source in range(count)])


def exchange(states, bits):
    replicas, tensors = lax.axis_size("replica"), lax.axis_size("tensor")
    groups = []
    for tensor in range(tensors):
        offsets = [0]
        for pair in bits:
            offsets += [offset | pair[tensor % 2] for offset in offsets]
        for base in range(replicas):
            if not base & offsets[-1]:
                groups.append([(base | offset) * tensors + tensor for offset in offsets])
    return lax.all_to_all(
        states, ("replica", "tensor"), 0, 0, axis_index_groups=groups, tiled=True
    )


def rounds_of(count):
    places = range(1, count.bit_length() - 1)
    bits = [(1 << place, 1 << (place - 1)) for place in places]
    return [bits[place:place + 2] for place in range(0, len(bits), 2)]


def on_device(
    grad_q,
    error_q,
    qfac_q,
    ginv_q,
    weight_q,
    momentum_q,
    grad_o,
    error_o,
    qfac_o,
    ginv_o,
    weight_o,
    momentum_o,
    norm_grads,
):
    replicas = lax.axis_size("replica")
    tensors = lax.axis_size("tensor")
    rank = qfac_q.shape[1]
    half_q = grad_q.shape[0] // 2
    norm_rows = norm_grads.size // lanes
    mat_q_far, mat_o_far, send, mat_q_near, mat_o_near, part, norm = project(
        grad_q, error_q, grad_o, error_o, qfac_q.T, qfac_o.T, norm_grads
    )
    columns = part.shape[1]
    rounds = rounds_of(replicas)
    sizes = [1 << len(bits) for bits in rounds] + [1]
    states = small(
        first_sum_kernel, "first_sum", shaped((sizes[0], rank, columns + lanes), bf16),
        part, norm, swap_halves(send),
    )
    wide = (rank, columns + 2 * lanes)
    for bits, size in zip(rounds[:-1], sizes[1:]):
        states = small(
            functools.partial(norm_sum_kernel, columns), "norm_sum", shaped((size,) + wide, bf16),
            exchange(states, bits),
        )
    hat_near = small(
        functools.partial(hat_kernel, half_q, columns), "hats", shaped(wide, bf16),
        ginv_q, ginv_o, exchange(states, rounds[-1]),
    )
    hat_far = swap_halves(hat_near)
    part_q, part_o = right_near(hat_near, mat_q_near, mat_o_near)
    send, near, norm = right_far(
        hat_far, mat_q_far, mat_o_far, part_q, part_o, hat_near, norm_rows
    )
    states, norm = small(
        near_sum_kernel, "near_sum",
        (shaped((sizes[0],) + send.shape, bf16), shaped(norm.shape, f32)),
        near, swap_halves(send), norm, swap_tensor(norm, 1),
    )
    for bits, size in zip(rounds[:-1], sizes[1:]):
        states = small(
            plain_sum_kernel, "plain_sum", shaped((size,) + send.shape, bf16), exchange(states, bits)
        )
    new_near, norm = small(
        functools.partial(mean_kernel, replicas, replicas * tensors), "mean",
        (shaped(send.shape, bf16), shaped(norm.shape, f32)),
        norm, swap_tensor(norm, 2), exchange(states, rounds[-1]),
    )
    (
        error_q_new, error_o_new, momentum_q_new, weight_q_new,
        new_q, new_o, momentum_o_new, weight_o_new, norm_mean,
    ) = finish(
        replicas, hat_near, hat_far,
        (mat_q_near, mat_o_near, mat_q_far, mat_o_far), new_near,
        (weight_q, momentum_q, weight_o, momentum_o), norm,
    )
    return (
        error_q_new,
        new_q.T,
        momentum_q_new,
        weight_q_new,
        error_o_new,
        new_o.T,
        momentum_o_new,
        weight_o_new,
        norm_mean.reshape(-1),
    )


def solution(mesh):
    in_specs = (
        P("replica", "tensor"),
        P("replica", "tensor"),
        P("tensor", None),
        P("tensor", None),
        P("replica", "tensor"),
        P("replica", "tensor"),
        P(("replica", "tensor"), None),
        P(("replica", "tensor"), None),
        P("tensor", None),
        P("tensor", None),
        P("tensor", "replica"),
        P("tensor", "replica"),
        P("replica", "tensor", None),
    )
    out_specs = (
        P("replica", "tensor"),
        P("tensor", None),
        P("replica", "tensor"),
        P("replica", "tensor"),
        P(("replica", "tensor"), None),
        P("tensor", None),
        P("tensor", "replica"),
        P("tensor", "replica"),
        P(),
    )
    return jax.shard_map(
        on_device, mesh=mesh, in_specs=in_specs, out_specs=out_specs, check_vma=False
    )
```

```python
import functools

import jax
import jax.numpy as jnp
from jax import lax
from jax.experimental import pallas as pl
from jax.experimental.pallas import tpu as pltpu
from jax.sharding import PartitionSpec as P

momentum_decay = 0.9
step_size = 0.5
lanes = 128
mib = 1024 * 1024
bf16 = jnp.bfloat16
f32 = jnp.float32

whole = pl.BlockSpec(memory_space=pltpu.VMEM)
in_place = pl.BlockSpec(memory_space=pl.ANY)


def dot(left, right, left_dim, right_dim, precision=None):
    return lax.dot_general(
        left,
        right,
        (((left_dim,), (right_dim,)), ((), ())),
        precision=precision,
        preferred_element_type=f32,
    )


def params(limit):
    return pltpu.CompilerParams(vmem_limit_bytes=limit * mib)


def cost(flops, moved):
    return pl.CostEstimate(flops=flops, bytes_accessed=moved, transcendentals=0)


def in_hbm(value):
    return pltpu.with_memory_space_constraint(value, pltpu.HBM)


def in_vmem(value):
    return pltpu.with_memory_space_constraint(value, pltpu.VMEM)


def shaped(shape, dtype):
    return jax.ShapeDtypeStruct(shape, dtype)


def parity():
    replica = lax.axis_index("replica")
    odd = lax.rem(lax.axis_index("tensor"), 2) == 1
    return jnp.where(odd, replica // (lax.axis_size("replica") // 2), lax.rem(replica, 2))


def half_at(which, size):
    return pl.ds(pl.multiple_of(which * size, size), size)


def load(source, target, sem):
    copy = pltpu.make_async_copy(source, target, sem)
    copy.start()
    return copy


def project_half(
    which, fac_q_h, fac_o_h, grad_q, error_q, grad_o, error_o, mat_q, mat_o, store,
    fac_q, fac_o, grad_q_v, error_q_v, grad_o_v, error_o_v, sems,
):
    half_q, half_o = mat_q.shape[0], mat_o.shape[0]
    steps = 4
    rows_q, rows_o = half_q // steps, half_o // steps
    fac_copies = [load(fac_q_h, fac_q, sems.at[0]), load(fac_o_h, fac_o, sems.at[1])]
    jobs = []
    for step in range(steps):
        slot = 2 + 4 * step
        part_q = pl.ds(step * rows_q, rows_q)
        part_o = pl.ds(step * rows_o, rows_o)
        there_q = pl.ds(pl.multiple_of(which * half_q + step * rows_q, rows_q), rows_q)
        there_o = pl.ds(pl.multiple_of(which * half_o + step * rows_o, rows_o), rows_o)
        jobs.append((step, part_q, part_o, (
            load(grad_q.at[there_q], grad_q_v.at[part_q], sems.at[slot]),
            load(error_q.at[there_q], error_q_v.at[part_q], sems.at[slot + 1]),
            load(grad_o.at[there_o], grad_o_v.at[part_o], sems.at[slot + 2]),
            load(error_o.at[there_o], error_o_v.at[part_o], sems.at[slot + 3]),
        )))
    for copy in fac_copies:
        copy.wait()
    columns_o = fac_o[...].T
    for step, part_q, part_o, copies in jobs:
        for copy in copies:
            copy.wait()
        block_q = grad_q_v[part_q] + error_q_v[part_q]
        block_o = grad_o_v[part_o] + error_o_v[part_o]
        mat_q[part_q] = block_q
        mat_o[part_o] = block_o
        store(step * rows_q, dot(fac_q[...], block_q, 1, 1))
        store(half_q + step * rows_o, dot(block_o, columns_o, 1, 0).T)


def far_kernel(
    fac_q_h, fac_o_h, grad_q, error_q, grad_o, error_o, mat_q, mat_o, send, *scratch
):
    def store(column, value):
        send[:, column:column + value.shape[1]] = value.astype(bf16)

    project_half(
        1 - parity(), fac_q_h, fac_o_h, grad_q, error_q, grad_o, error_o,
        mat_q, mat_o, store, *scratch
    )


def near_kernel(
    fac_q_h, fac_o_h, grad_q, error_q, grad_o, error_o, norm_grads,
    mat_q, mat_o, part, norm, *scratch
):
    def store(column, value):
        part[:, column:column + value.shape[1]] = value

    project_half(
        parity(), fac_q_h, fac_o_h, grad_q, error_q, grad_o, error_o,
        mat_q, mat_o, store, *scratch
    )
    values = norm_grads[0].astype(f32)
    for row in range(norm.shape[0]):
        norm[row:row + 1, :] = values[:, row * lanes:(row + 1) * lanes]


def project(grad_q, error_q, grad_o, error_o, fac_q, fac_o, norm_grads):
    rank = fac_q.shape[0]
    half_q = (grad_q.shape[0] // 2, grad_q.shape[1])
    half_o = (grad_o.shape[0] // 2, grad_o.shape[1])
    columns = half_q[0] + half_o[0]
    norm_rows = norm_grads.size // lanes
    mats = (pltpu.VMEM(half_q, bf16), pltpu.VMEM(half_o, bf16))
    scratch = [
        pltpu.VMEM(fac_q.shape, bf16),
        pltpu.VMEM(fac_o.shape, bf16),
        pltpu.VMEM(half_q, bf16),
        pltpu.VMEM(half_q, bf16),
        pltpu.VMEM(half_o, bf16),
        pltpu.VMEM(half_o, bf16),
        pltpu.SemaphoreType.DMA((18,)),
    ]
    operands = [
        in_hbm(value) for value in (fac_q, fac_o, grad_q, error_q, grad_o, error_o)
    ]
    effort = cost(2 * rank * (grad_q.size + grad_o.size) // 2, 4 * grad_q.size)
    mat_q_far, mat_o_far, send = pl.pallas_call(
        far_kernel,
        out_shape=mats + (shaped((rank, columns), bf16),),
        in_specs=[in_place] * 6,
        out_specs=(whole,) * 3,
        scratch_shapes=scratch,
        compiler_params=params(16),
        cost_estimate=effort,
        name="project_far",
    )(*operands)
    mat_q_near, mat_o_near, part, norm = pl.pallas_call(
        near_kernel,
        out_shape=mats + (shaped((rank, columns), f32), shaped((norm_rows, lanes), f32)),
        in_specs=[in_place] * 6 + [whole],
        out_specs=(whole,) * 4,
        scratch_shapes=scratch,
        compiler_params=params(16),
        cost_estimate=effort,
        name="project_near",
    )(*operands, norm_grads)
    return mat_q_far, mat_o_far, send, mat_q_near, mat_o_near, part, norm


def small(kernel, name, outs, *operands):
    return pl.pallas_call(
        kernel,
        out_shape=outs,
        in_specs=[whole] * len(operands),
        out_specs=(whole,) * len(outs) if isinstance(outs, tuple) else whole,
        compiler_params=params(8),
        name=name,
    )(*operands)


def tree(parts):
    while len(parts) > 1:
        parts = [parts[place] + parts[place + 1] for place in range(0, len(parts), 2)]
    return parts[0]


def total_of(states, columns):
    return tree([state[:, :columns].astype(f32) for state in states])


def norm_of(states, columns):
    parts = []
    for state in states:
        part = state[:, columns:columns + lanes].astype(f32)
        if state.shape[1] > columns + lanes:
            part = part + state[:, columns + lanes:columns + 2 * lanes].astype(f32)
        parts.append(part)
    return tree(parts)


def store_norm(state, columns, total):
    high = total.astype(bf16)
    state[:, columns:columns + lanes] = high
    state[:, columns + lanes:columns + 2 * lanes] = (total - high.astype(f32)).astype(bf16)


def first_sum_kernel(part, norm, got, state):
    columns = part.shape[1]
    state[:, :columns] = (part[...] + got[...].astype(f32)).astype(bf16)
    state[:, columns:] = norm[...].astype(bf16)


def norm_sum_kernel(columns, *refs):
    *states, out = refs
    out[:, :columns] = total_of(states, columns).astype(bf16)
    store_norm(out, columns, norm_of(states, columns))


def plain_sum_kernel(*refs):
    *states, out = refs
    out[...] = total_of(states, out.shape[1]).astype(bf16)


def hat_kernel(size_q, columns, ginv_q, ginv_o, *refs):
    *states, out = refs
    total = total_of(states, columns)
    highest = lax.Precision.HIGHEST
    out[:, :size_q] = dot(ginv_q[...].T, total[:, :size_q], 1, 0, highest).astype(bf16)
    out[:, size_q:columns] = dot(ginv_o[...].T, total[:, size_q:], 1, 0, highest).astype(bf16)
    store_norm(out, columns, norm_of(states, columns))


def mean_kernel(count, norm_count, norm, norm_got, *refs):
    *states, new, norm_mean = refs
    new[...] = (total_of(states, new.shape[1]) / count).astype(bf16)
    norm_mean[...] = (norm[...] + norm_got[...]) / norm_count


def right_near_kernel(hat, mat_q, mat_o, part_q, part_o):
    size_q, size_o = mat_q.shape[0], mat_o.shape[0]
    part_q[...] = dot(hat[:, :size_q], mat_q[...], 1, 0)
    part_o[...] = dot(hat[:, size_q:size_q + size_o], mat_o[...], 1, 0)


def right_near(hat, mat_q, mat_o):
    rank = hat.shape[0]
    return pl.pallas_call(
        right_near_kernel,
        out_shape=(shaped((rank, mat_q.shape[1]), f32), shaped((rank, mat_o.shape[1]), f32)),
        in_specs=[whole] * 3,
        out_specs=(whole,) * 2,
        compiler_params=params(8),
        cost_estimate=cost(2 * rank * (mat_q.size + mat_o.size), 2 * (mat_q.size + mat_o.size)),
        name="right_near",
    )(hat, in_vmem(mat_q), in_vmem(mat_o))


def right_half(which, hat, mat_q, mat_o, part_q, part_o, store):
    size_q, size_o = mat_q.shape[0], mat_o.shape[0]
    half_q, half_o = mat_q.shape[1] // 2, mat_o.shape[1] // 2
    columns = half_at(which, half_q)
    store(0, half_q, part_q[:, columns] + dot(hat[:, :size_q], mat_q[:, columns], 1, 0))
    columns = half_at(which, half_o)
    store(half_q, half_o, part_o[:, columns] + dot(
        hat[:, size_q:size_q + size_o], mat_o[:, columns], 1, 0
    ))


def right_send_kernel(hat, mat_q, mat_o, part_q, part_o, send):
    def store(column, width, value):
        send[:, column:column + width] = value.astype(bf16)

    right_half(1 - parity(), hat, mat_q, mat_o, part_q, part_o, store)


def right_keep_kernel(hat, mat_q, mat_o, part_q, part_o, hat_near, near, norm):
    def store(column, width, value):
        near[:, column:column + width] = value

    right_half(parity(), hat, mat_q, mat_o, part_q, part_o, store)
    norm[...] = norm_of([hat_near, hat], mat_q.shape[0] + mat_o.shape[0])


def right_far(hat, mat_q, mat_o, part_q, part_o, hat_near, norm_rows):
    rank = hat.shape[0]
    columns = (mat_q.shape[1] + mat_o.shape[1]) // 2
    operands = (hat, in_vmem(mat_q), in_vmem(mat_o), part_q, part_o)
    effort = cost(rank * (mat_q.size + mat_o.size), mat_q.size + mat_o.size)
    send = pl.pallas_call(
        right_send_kernel,
        out_shape=shaped((rank, columns), bf16),
        in_specs=[whole] * 5,
        out_specs=whole,
        compiler_params=params(8),
        cost_estimate=effort,
        name="right_send",
    )(*operands)
    near, norm = pl.pallas_call(
        right_keep_kernel,
        out_shape=(shaped((rank, columns), f32), shaped((norm_rows, lanes), f32)),
        in_specs=[whole] * 6,
        out_specs=(whole,) * 2,
        compiler_params=params(8),
        cost_estimate=effort,
        name="right_keep",
    )(*operands, hat_near)
    return send, near, norm


def near_sum_kernel(near, got, norm, norm_got, state, norm_sum):
    state[...] = (near[...] + got[...].astype(f32)).astype(bf16)
    norm_sum[...] = norm[...] + norm_got[...]


def error_columns(column, hat, hat_row, half, mat_q, mat_o, new, error_q, error_o, stage_q, stage_o, sems, slot):
    size_q, size_o = mat_q.shape[0], mat_o.shape[0]
    wide_q, wide_o = stage_q.shape[1], stage_o.shape[1]
    copies = []
    chunk_q, chunk_o = size_q // 4, size_o // 4
    cols_q, cols_o = half_at(column, wide_q), half_at(column, wide_o)
    for chunk in range(4):
        part = pl.ds(chunk * chunk_q, chunk_q)
        stage = pl.ds(hat_row * size_q + chunk * chunk_q, chunk_q)
        approx = dot(hat[:, part], new[:, :wide_q], 0, 0)
        stage_q[stage] = (mat_q[part, cols_q].astype(f32) - approx).astype(bf16)
        there = pl.ds(pl.multiple_of(half * size_q + chunk * chunk_q, chunk_q), chunk_q)
        copies.append(load(stage_q.at[stage], error_q.at[there, cols_q], sems.at[slot]))
        part = pl.ds(chunk * chunk_o, chunk_o)
        stage = pl.ds(hat_row * size_o + chunk * chunk_o, chunk_o)
        approx = dot(hat[:, size_q + chunk * chunk_o:size_q + (chunk + 1) * chunk_o], new[:, wide_q:], 0, 0)
        stage_o[stage] = (mat_o[part, cols_o].astype(f32) - approx).astype(bf16)
        there = pl.ds(pl.multiple_of(half * size_o + chunk * chunk_o, chunk_o), chunk_o)
        copies.append(load(stage_o.at[stage], error_o.at[there, cols_o], sems.at[slot + 1]))
        slot += 2
    return copies


def piece_of(near, far, index, count, size, pieces):
    half = count // 2
    here = index // half == parity()
    slot = lax.rem(index, half)
    if size % lanes == 0:
        part = half_at(slot, size)
        return jnp.where(here, near[:, part].astype(f32), far[:, part].astype(f32)).astype(bf16)
    width = half * size
    chosen = jnp.where(here, near[:, :width].astype(f32), far[:, :width].astype(f32))
    for place in range(half):
        pieces[place] = chosen[:, place * size:(place + 1) * size]
    return pieces[slot].astype(bf16)


def finish_near_kernel(
    count, hat_near, hat_far, mat_q_near, mat_o_near, mat_q_far, mat_o_far, new, weight_q, momentum_q,
    error_q, error_o, momentum_q_h, weight_q_h,
    stage_q, stage_o, momentum_q_new, weight_q_new, pieces, sems, out_sems
):
    mine = parity()
    me = lax.axis_index("replica")
    copies = error_columns(
        mine, hat_near, 0, mine, mat_q_near, mat_o_near, new, error_q, error_o, stage_q, stage_o, sems, 0
    ) + error_columns(
        mine, hat_far, 1, 1 - mine, mat_q_far, mat_o_far, new, error_q, error_o, stage_q, stage_o, sems, 8
    )
    piece = piece_of(hat_near, hat_far, me, count, weight_q.shape[0], pieces)
    copies += query_columns(
        mine, piece, new, weight_q, momentum_q, momentum_q_new, weight_q_new,
        momentum_q_h, weight_q_h, out_sems
    )
    for copy in copies:
        copy.wait()


def query_columns(
    which, piece, new, weight, momentum, momentum_new, weight_new, momentum_h, weight_h, sems
):
    wide = momentum_new.shape[1]
    columns = half_at(which, wide)
    moved = momentum_decay * momentum[:, columns] + dot(piece, new[:, :wide], 0, 0)
    momentum_new[...] = moved
    weight_new[...] = weight[:, columns] - step_size * moved
    return [
        load(momentum_new, momentum_h.at[:, columns], sems.at[0]),
        load(weight_new, weight_h.at[:, columns], sems.at[1]),
    ]


def finish_far_kernel(
    count, hat_near, hat_far, mat_q_near, mat_o_near, mat_q_far, mat_o_far,
    new_near, new_far, weight_q, momentum_q, weight_o, momentum_o, norm,
    error_q_in, error_o_in, momentum_q_in, weight_q_in,
    error_q, error_o, momentum_q_h, weight_q_h, new_q_h, new_o_h, momentum_o_h, weight_o_h, norm_h,
    stage_q, stage_o, momentum_q_new, weight_q_new, new_q, new_o, momentum_o_new, weight_o_new,
    pieces_q, pieces_o, sems, out_sems
):
    mine = parity()
    me = lax.axis_index("replica")
    wide_q, wide_o = stage_q.shape[1], stage_o.shape[1]
    size_q = mat_q_near.shape[0]
    size_o = mat_o_near.shape[0]
    new_q[:, half_at(mine, wide_q)] = new_near[:, :wide_q]
    new_q[:, half_at(1 - mine, wide_q)] = new_far[:, :wide_q]
    new_o[:, half_at(mine, wide_o)] = new_near[:, wide_q:]
    new_o[:, half_at(1 - mine, wide_o)] = new_far[:, wide_q:]
    copies = [
        load(new_q, new_q_h, out_sems.at[0]),
        load(new_o, new_o_h, out_sems.at[1]),
        load(norm, norm_h, out_sems.at[2]),
    ]
    copies += error_columns(
        1 - mine, hat_near, 0, mine, mat_q_near, mat_o_near, new_far,
        error_q, error_o, stage_q, stage_o, sems, 0
    )
    piece = piece_of(
        new_near.at[:, wide_q:], new_far.at[:, wide_q:], me, count, weight_o.shape[1], pieces_o
    )
    for which, hat in ((mine, hat_near), (1 - mine, hat_far)):
        rows = half_at(which, size_o)
        moved = momentum_decay * momentum_o[rows] + dot(hat[:, size_q:size_q + size_o], piece, 0, 0)
        momentum_o_new[rows] = moved
        weight_o_new[rows] = weight_o[rows] - step_size * moved
    copies.append(load(momentum_o_new, momentum_o_h, out_sems.at[3]))
    copies.append(load(weight_o_new, weight_o_h, out_sems.at[4]))
    copies += error_columns(
        1 - mine, hat_far, 1, 1 - mine, mat_q_far, mat_o_far, new_far,
        error_q, error_o, stage_q, stage_o, sems, 8
    )
    piece = piece_of(hat_near, hat_far, me, count, weight_q.shape[0], pieces_q)
    copies += query_columns(
        1 - mine, piece, new_far, weight_q, momentum_q, momentum_q_new, weight_q_new,
        momentum_q_h, weight_q_h, out_sems.at[5:7]
    )
    for copy in copies:
        copy.wait()


def finish(count, hat_near, hat_far, mats, new_near, weights, norm):
    mat_q, mat_o = mats[0], mats[1]
    weight_q, _, weight_o, _ = weights
    rank = hat_near.shape[0]
    size_q, size_o = mat_q.shape[0], mat_o.shape[0]
    early = (
        shaped((2 * size_q, mat_q.shape[1]), bf16),
        shaped((2 * size_o, mat_o.shape[1]), bf16),
        shaped(weight_q.shape, f32),
        shaped(weight_q.shape, f32),
    )
    late = (
        shaped((rank, mat_q.shape[1]), bf16),
        shaped((rank, mat_o.shape[1]), bf16),
        shaped(weight_o.shape, f32),
        shaped(weight_o.shape, f32),
    )
    piece_q = (weight_q.shape[0], weight_q.shape[1] // 2)
    stages = [
        pltpu.VMEM((2 * size_q, mat_q.shape[1] // 2), bf16),
        pltpu.VMEM((2 * size_o, mat_o.shape[1] // 2), bf16),
        pltpu.VMEM(piece_q, f32),
        pltpu.VMEM(piece_q, f32),
    ]
    pieces_q = pltpu.VMEM((count // 2, rank, weight_q.shape[0]), f32)
    pieces_o = pltpu.VMEM((count // 2, rank, weight_o.shape[1]), f32)
    moved = 4 * (mat_q.size + mat_o.size)
    mats = [in_vmem(mat) for mat in mats]
    weights = [in_vmem(value) for value in weights]
    new_far = swap_halves(new_near)
    parts = pl.pallas_call(
        functools.partial(finish_near_kernel, count),
        out_shape=early,
        in_specs=[whole] * 9,
        out_specs=(in_place,) * 4,
        scratch_shapes=stages + [
            pieces_q, pltpu.SemaphoreType.DMA((16,)), pltpu.SemaphoreType.DMA((2,))
        ],
        compiler_params=params(12),
        cost_estimate=cost(2 * rank * (mat_q.size + mat_o.size), moved),
        name="finish_near",
    )(hat_near, hat_far, *mats, new_near, *weights[:2])
    return pl.pallas_call(
        functools.partial(finish_far_kernel, count),
        out_shape=early + late + (shaped(norm.shape, f32),),
        in_specs=[whole] * 13 + [in_place] * 4,
        out_specs=(in_place,) * 9,
        scratch_shapes=stages + [pltpu.VMEM(out.shape, out.dtype) for out in late] + [
            pieces_q, pieces_o, pltpu.SemaphoreType.DMA((16,)), pltpu.SemaphoreType.DMA((7,))
        ],
        input_output_aliases={13: 0, 14: 1, 15: 2, 16: 3},
        compiler_params=params(16),
        cost_estimate=cost(2 * rank * (mat_q.size + mat_o.size), moved),
        name="finish_far",
    )(hat_near, hat_far, *mats, new_near, new_far, *weights, norm, *parts)


def swap(value, even, odd):
    replicas, tensors = lax.axis_size("replica"), lax.axis_size("tensor")
    pairs = []
    for replica in range(replicas):
        for tensor in range(tensors):
            target = replica ^ (odd if tensor % 2 else even)
            pairs.append((replica * tensors + tensor, target * tensors + tensor))
    return lax.ppermute(value, ("replica", "tensor"), pairs)


def swap_halves(value):
    return swap(value, 1, lax.axis_size("replica") // 2)


def swap_tensor(value, bit):
    count = lax.axis_size("tensor")
    return lax.ppermute(value, "tensor", [(source, source ^ bit) for source in range(count)])


def exchange(state, bits):
    offsets = [(0, 0)]
    for even, odd in bits:
        offsets += [(first | even, second | odd) for first, second in offsets]
    if len(offsets) == 4:
        offsets = [offsets[place] for place in (0, 1, 3, 2)]
    return [state] + [swap(state, *offset) for offset in offsets[1:]]


def rounds_of(count):
    places = range(1, count.bit_length() - 1)
    bits = [(1 << place, 1 << (place - 1)) for place in places]
    return [bits[place:place + 2] for place in range(0, len(bits), 2)]


def on_device(
    grad_q,
    error_q,
    qfac_q,
    ginv_q,
    weight_q,
    momentum_q,
    grad_o,
    error_o,
    qfac_o,
    ginv_o,
    weight_o,
    momentum_o,
    norm_grads,
):
    replicas = lax.axis_size("replica")
    tensors = lax.axis_size("tensor")
    rank = qfac_q.shape[1]
    half_q = grad_q.shape[0] // 2
    norm_rows = norm_grads.size // lanes
    mat_q_far, mat_o_far, send, mat_q_near, mat_o_near, part, norm = project(
        grad_q, error_q, grad_o, error_o, qfac_q.T, qfac_o.T, norm_grads
    )
    columns = part.shape[1]
    rounds = rounds_of(replicas)
    state = small(
        first_sum_kernel, "first_sum", shaped((rank, columns + lanes), bf16), part, norm, swap_halves(send)
    )
    wide = shaped((rank, columns + 2 * lanes), bf16)
    for bits in rounds[:-1]:
        state = small(
            functools.partial(norm_sum_kernel, columns), "norm_sum", wide, *exchange(state, bits)
        )
    hat_near = small(
        functools.partial(hat_kernel, half_q, columns), "hats", wide,
        ginv_q, ginv_o, *exchange(state, rounds[-1]),
    )
    hat_far = swap_halves(hat_near)
    part_q, part_o = right_near(hat_near, mat_q_near, mat_o_near)
    send, near, norm = right_far(
        hat_far, mat_q_far, mat_o_far, part_q, part_o, hat_near, norm_rows
    )
    state, norm = small(
        near_sum_kernel, "near_sum", (shaped(send.shape, bf16), shaped(norm.shape, f32)),
        near, swap_halves(send), norm, swap_tensor(norm, 1),
    )
    for bits in rounds[:-1]:
        state = small(
            plain_sum_kernel, "plain_sum", shaped(state.shape, bf16), *exchange(state, bits)
        )
    states = exchange(state, rounds[-1])
    new_near, norm = small(
        functools.partial(mean_kernel, replicas, replicas * tensors), "mean",
        (shaped(state.shape, bf16), shaped(norm.shape, f32)),
        norm, swap_tensor(norm, 2), *states,
    )
    (
        error_q_new, error_o_new, momentum_q_new, weight_q_new,
        new_q, new_o, momentum_o_new, weight_o_new, norm_mean,
    ) = finish(
        replicas, hat_near, hat_far,
        (mat_q_near, mat_o_near, mat_q_far, mat_o_far), new_near,
        (weight_q, momentum_q, weight_o, momentum_o), norm,
    )
    return (
        error_q_new,
        new_q.T,
        momentum_q_new,
        weight_q_new,
        error_o_new,
        new_o.T,
        momentum_o_new,
        weight_o_new,
        norm_mean.reshape(-1),
    )


def solution(mesh):
    in_specs = (
        P("replica", "tensor"),
        P("replica", "tensor"),
        P("tensor", None),
        P("tensor", None),
        P("replica", "tensor"),
        P("replica", "tensor"),
        P(("replica", "tensor"), None),
        P(("replica", "tensor"), None),
        P("tensor", None),
        P("tensor", None),
        P("tensor", "replica"),
        P("tensor", "replica"),
        P("replica", "tensor", None),
    )
    out_specs = (
        P("replica", "tensor"),
        P("tensor", None),
        P("replica", "tensor"),
        P("replica", "tensor"),
        P(("replica", "tensor"), None),
        P("tensor", None),
        P("tensor", "replica"),
        P("tensor", "replica"),
        P(),
    )
    return jax.shard_map(
        on_device, mesh=mesh, in_specs=in_specs, out_specs=out_specs, check_vma=False
    )
```

```python
import functools

import jax
import jax.numpy as jnp
from jax import lax
from jax.experimental import pallas as pl
from jax.experimental.pallas import tpu as pltpu
from jax.sharding import PartitionSpec as P

momentum_decay = 0.9
step_size = 0.5
lanes = 128
mib = 1024 * 1024
bf16 = jnp.bfloat16
f32 = jnp.float32

whole = pl.BlockSpec(memory_space=pltpu.VMEM)
in_place = pl.BlockSpec(memory_space=pl.ANY)


def dot(left, right, left_dim, right_dim, precision=None):
    return lax.dot_general(
        left,
        right,
        (((left_dim,), (right_dim,)), ((), ())),
        precision=precision,
        preferred_element_type=f32,
    )


def params(limit):
    return pltpu.CompilerParams(vmem_limit_bytes=limit * mib)


def cost(flops, moved):
    return pl.CostEstimate(flops=flops, bytes_accessed=moved, transcendentals=0)


def in_hbm(value):
    return pltpu.with_memory_space_constraint(value, pltpu.HBM)


def in_vmem(value):
    return pltpu.with_memory_space_constraint(value, pltpu.VMEM)


def shaped(shape, dtype):
    return jax.ShapeDtypeStruct(shape, dtype)


def parity():
    replica = lax.axis_index("replica")
    odd = lax.rem(lax.axis_index("tensor"), 2) == 1
    return jnp.where(odd, replica // (lax.axis_size("replica") // 2), lax.rem(replica, 2))


def half_at(which, size):
    return pl.ds(pl.multiple_of(which * size, size), size)


def load(source, target, sem):
    copy = pltpu.make_async_copy(source, target, sem)
    copy.start()
    return copy


def project_half(
    which, fac_q_h, fac_o_h, grad_q, error_q, grad_o, error_o, mat_q, mat_o, store,
    fac_q, fac_o, grad_q_v, error_q_v, grad_o_v, error_o_v, sems,
):
    half_q, half_o = mat_q.shape[0], mat_o.shape[0]
    steps = 4
    rows_q, rows_o = half_q // steps, half_o // steps
    fac_copies = [load(fac_q_h, fac_q, sems.at[0]), load(fac_o_h, fac_o, sems.at[1])]
    jobs = []
    for step in range(steps):
        slot = 2 + 4 * step
        part_q = pl.ds(step * rows_q, rows_q)
        part_o = pl.ds(step * rows_o, rows_o)
        there_q = pl.ds(pl.multiple_of(which * half_q + step * rows_q, rows_q), rows_q)
        there_o = pl.ds(pl.multiple_of(which * half_o + step * rows_o, rows_o), rows_o)
        jobs.append((step, part_q, part_o, (
            load(grad_q.at[there_q], grad_q_v.at[part_q], sems.at[slot]),
            load(error_q.at[there_q], error_q_v.at[part_q], sems.at[slot + 1]),
            load(grad_o.at[there_o], grad_o_v.at[part_o], sems.at[slot + 2]),
            load(error_o.at[there_o], error_o_v.at[part_o], sems.at[slot + 3]),
        )))
    for copy in fac_copies:
        copy.wait()
    columns_o = fac_o[...].T
    for step, part_q, part_o, copies in jobs:
        early = 2 if step == 0 else 4
        for copy in copies[:early]:
            copy.wait()
        block_q = grad_q_v[part_q] + error_q_v[part_q]
        mat_q[part_q] = block_q
        store(step * rows_q, dot(fac_q[...], block_q, 1, 1))
        for copy in copies[early:]:
            copy.wait()
        block_o = grad_o_v[part_o] + error_o_v[part_o]
        mat_o[part_o] = block_o
        store(half_q + step * rows_o, dot(block_o, columns_o, 1, 0).T)


def far_kernel(
    fac_q_h, fac_o_h, grad_q, error_q, grad_o, error_o, mat_q, mat_o, send, *scratch
):
    def store(column, value):
        send[:, column:column + value.shape[1]] = value.astype(bf16)

    project_half(
        1 - parity(), fac_q_h, fac_o_h, grad_q, error_q, grad_o, error_o,
        mat_q, mat_o, store, *scratch
    )


def near_kernel(
    fac_q_h, fac_o_h, grad_q, error_q, grad_o, error_o, norm_grads,
    mat_q, mat_o, part, norm, *scratch
):
    def store(column, value):
        part[:, column:column + value.shape[1]] = value

    project_half(
        parity(), fac_q_h, fac_o_h, grad_q, error_q, grad_o, error_o,
        mat_q, mat_o, store, *scratch
    )
    values = norm_grads[0].astype(f32)
    for row in range(norm.shape[0]):
        norm[row:row + 1, :] = values[:, row * lanes:(row + 1) * lanes]


def project(grad_q, error_q, grad_o, error_o, fac_q, fac_o, norm_grads):
    rank = fac_q.shape[0]
    half_q = (grad_q.shape[0] // 2, grad_q.shape[1])
    half_o = (grad_o.shape[0] // 2, grad_o.shape[1])
    columns = half_q[0] + half_o[0]
    norm_rows = norm_grads.size // lanes
    mats = (pltpu.VMEM(half_q, bf16), pltpu.VMEM(half_o, bf16))
    scratch = [
        pltpu.VMEM(fac_q.shape, bf16),
        pltpu.VMEM(fac_o.shape, bf16),
        pltpu.VMEM(half_q, bf16),
        pltpu.VMEM(half_q, bf16),
        pltpu.VMEM(half_o, bf16),
        pltpu.VMEM(half_o, bf16),
        pltpu.SemaphoreType.DMA((18,)),
    ]
    operands = [
        in_hbm(value) for value in (fac_q, fac_o, grad_q, error_q, grad_o, error_o)
    ]
    effort = cost(2 * rank * (grad_q.size + grad_o.size) // 2, 4 * grad_q.size)
    mat_q_far, mat_o_far, send = pl.pallas_call(
        far_kernel,
        out_shape=mats + (shaped((rank, columns), bf16),),
        in_specs=[in_place] * 6,
        out_specs=(whole,) * 3,
        scratch_shapes=scratch,
        compiler_params=params(16),
        cost_estimate=effort,
        name="project_far",
    )(*operands)
    mat_q_near, mat_o_near, part, norm = pl.pallas_call(
        near_kernel,
        out_shape=mats + (shaped((rank, columns), f32), shaped((norm_rows, lanes), f32)),
        in_specs=[in_place] * 6 + [whole],
        out_specs=(whole,) * 4,
        scratch_shapes=scratch,
        compiler_params=params(16),
        cost_estimate=effort,
        name="project_near",
    )(*operands, norm_grads)
    return mat_q_far, mat_o_far, send, mat_q_near, mat_o_near, part, norm


def small(kernel, name, outs, *operands):
    return pl.pallas_call(
        kernel,
        out_shape=outs,
        in_specs=[whole] * len(operands),
        out_specs=(whole,) * len(outs) if isinstance(outs, tuple) else whole,
        compiler_params=params(8),
        name=name,
    )(*operands)


def tree(parts):
    while len(parts) > 1:
        parts = [parts[place] + parts[place + 1] for place in range(0, len(parts), 2)]
    return parts[0]


def total_of(states, columns):
    return tree([state[:, :columns].astype(f32) for state in states])


def norm_of(states, columns):
    parts = []
    for state in states:
        part = state[:, columns:columns + lanes].astype(f32)
        if state.shape[1] > columns + lanes:
            part = part + state[:, columns + lanes:columns + 2 * lanes].astype(f32)
        parts.append(part)
    return tree(parts)


def store_norm(state, columns, total):
    high = total.astype(bf16)
    state[:, columns:columns + lanes] = high
    state[:, columns + lanes:columns + 2 * lanes] = (total - high.astype(f32)).astype(bf16)


def first_sum_kernel(part, norm, got, state):
    columns = part.shape[1]
    state[:, :columns] = (part[...] + got[...].astype(f32)).astype(bf16)
    state[:, columns:] = norm[...].astype(bf16)


def norm_sum_kernel(columns, *refs):
    *states, out = refs
    out[:, :columns] = total_of(states, columns).astype(bf16)
    store_norm(out, columns, norm_of(states, columns))


def plain_sum_kernel(*refs):
    *states, out = refs
    out[...] = total_of(states, out.shape[1]).astype(bf16)


def hat_kernel(size_q, columns, ginv_q, ginv_o, *refs):
    *states, out = refs
    total = total_of(states, columns)
    highest = lax.Precision.HIGHEST
    out[:, :size_q] = dot(ginv_q[...].T, total[:, :size_q], 1, 0, highest).astype(bf16)
    out[:, size_q:columns] = dot(ginv_o[...].T, total[:, size_q:], 1, 0, highest).astype(bf16)
    store_norm(out, columns, norm_of(states, columns))


def mean_kernel(count, norm_count, norm, norm_got, *refs):
    *states, new, norm_mean = refs
    new[...] = (total_of(states, new.shape[1]) / count).astype(bf16)
    norm_mean[...] = (norm[...] + norm_got[...]) / norm_count


def right_near_kernel(hat, mat_q, mat_o, part_q, part_o):
    size_q, size_o = mat_q.shape[0], mat_o.shape[0]
    part_q[...] = dot(hat[:, :size_q], mat_q[...], 1, 0)
    part_o[...] = dot(hat[:, size_q:size_q + size_o], mat_o[...], 1, 0)


def right_near(hat, mat_q, mat_o):
    rank = hat.shape[0]
    return pl.pallas_call(
        right_near_kernel,
        out_shape=(shaped((rank, mat_q.shape[1]), f32), shaped((rank, mat_o.shape[1]), f32)),
        in_specs=[whole] * 3,
        out_specs=(whole,) * 2,
        compiler_params=params(8),
        cost_estimate=cost(2 * rank * (mat_q.size + mat_o.size), 2 * (mat_q.size + mat_o.size)),
        name="right_near",
    )(hat, in_vmem(mat_q), in_vmem(mat_o))


def right_half(which, hat, mat_q, mat_o, part_q, part_o, store):
    size_q, size_o = mat_q.shape[0], mat_o.shape[0]
    half_q, half_o = mat_q.shape[1] // 2, mat_o.shape[1] // 2
    columns = half_at(which, half_q)
    store(0, half_q, part_q[:, columns] + dot(hat[:, :size_q], mat_q[:, columns], 1, 0))
    columns = half_at(which, half_o)
    store(half_q, half_o, part_o[:, columns] + dot(
        hat[:, size_q:size_q + size_o], mat_o[:, columns], 1, 0
    ))


def right_send_kernel(hat, mat_q, mat_o, part_q, part_o, send):
    def store(column, width, value):
        send[:, column:column + width] = value.astype(bf16)

    right_half(1 - parity(), hat, mat_q, mat_o, part_q, part_o, store)


def right_keep_kernel(hat, mat_q, mat_o, part_q, part_o, hat_near, near, norm):
    def store(column, width, value):
        near[:, column:column + width] = value

    right_half(parity(), hat, mat_q, mat_o, part_q, part_o, store)
    norm[...] = norm_of([hat_near, hat], mat_q.shape[0] + mat_o.shape[0])


def right_far(hat, mat_q, mat_o, part_q, part_o, hat_near, norm_rows):
    rank = hat.shape[0]
    columns = (mat_q.shape[1] + mat_o.shape[1]) // 2
    operands = (hat, in_vmem(mat_q), in_vmem(mat_o), part_q, part_o)
    effort = cost(rank * (mat_q.size + mat_o.size), mat_q.size + mat_o.size)
    send = pl.pallas_call(
        right_send_kernel,
        out_shape=shaped((rank, columns), bf16),
        in_specs=[whole] * 5,
        out_specs=whole,
        compiler_params=params(8),
        cost_estimate=effort,
        name="right_send",
    )(*operands)
    near, norm = pl.pallas_call(
        right_keep_kernel,
        out_shape=(shaped((rank, columns), f32), shaped((norm_rows, lanes), f32)),
        in_specs=[whole] * 6,
        out_specs=(whole,) * 2,
        compiler_params=params(8),
        cost_estimate=effort,
        name="right_keep",
    )(*operands, hat_near)
    return send, near, norm


def near_sum_kernel(near, got, norm, norm_got, state, norm_sum):
    state[...] = (near[...] + got[...].astype(f32)).astype(bf16)
    norm_sum[...] = norm[...] + norm_got[...]


def error_columns(column, hat, hat_row, half, mat_q, mat_o, new, error_q, error_o, stage_q, stage_o, sems, slot):
    size_q, size_o = mat_q.shape[0], mat_o.shape[0]
    wide_q, wide_o = stage_q.shape[1], stage_o.shape[1]
    copies = []
    chunk_q, chunk_o = size_q // 4, size_o // 4
    cols_q, cols_o = half_at(column, wide_q), half_at(column, wide_o)
    for chunk in range(4):
        part = pl.ds(chunk * chunk_q, chunk_q)
        stage = pl.ds(hat_row * size_q + chunk * chunk_q, chunk_q)
        approx = dot(hat[:, part], new[:, :wide_q], 0, 0)
        stage_q[stage] = (mat_q[part, cols_q].astype(f32) - approx).astype(bf16)
        there = pl.ds(pl.multiple_of(half * size_q + chunk * chunk_q, chunk_q), chunk_q)
        copies.append(load(stage_q.at[stage], error_q.at[there, cols_q], sems.at[slot]))
        part = pl.ds(chunk * chunk_o, chunk_o)
        stage = pl.ds(hat_row * size_o + chunk * chunk_o, chunk_o)
        approx = dot(hat[:, size_q + chunk * chunk_o:size_q + (chunk + 1) * chunk_o], new[:, wide_q:], 0, 0)
        stage_o[stage] = (mat_o[part, cols_o].astype(f32) - approx).astype(bf16)
        there = pl.ds(pl.multiple_of(half * size_o + chunk * chunk_o, chunk_o), chunk_o)
        copies.append(load(stage_o.at[stage], error_o.at[there, cols_o], sems.at[slot + 1]))
        slot += 2
    return copies


def piece_of(near, far, index, count, size, pieces):
    half = count // 2
    here = index // half == parity()
    slot = lax.rem(index, half)
    if size % lanes == 0:
        part = half_at(slot, size)
        return jnp.where(here, near[:, part].astype(f32), far[:, part].astype(f32)).astype(bf16)
    width = half * size
    chosen = jnp.where(here, near[:, :width].astype(f32), far[:, :width].astype(f32))
    for place in range(half):
        pieces[place] = chosen[:, place * size:(place + 1) * size]
    return pieces[slot].astype(bf16)


def finish_near_kernel(
    count, hat_near, hat_far, mat_q_near, mat_o_near, mat_q_far, mat_o_far, new, weight_q, momentum_q,
    error_q, error_o, momentum_q_h, weight_q_h,
    stage_q, stage_o, momentum_q_new, weight_q_new, pieces, sems, out_sems
):
    mine = parity()
    me = lax.axis_index("replica")
    copies = error_columns(
        mine, hat_near, 0, mine, mat_q_near, mat_o_near, new, error_q, error_o, stage_q, stage_o, sems, 0
    ) + error_columns(
        mine, hat_far, 1, 1 - mine, mat_q_far, mat_o_far, new, error_q, error_o, stage_q, stage_o, sems, 8
    )
    piece = piece_of(hat_near, hat_far, me, count, weight_q.shape[0], pieces)
    copies += query_columns(
        mine, piece, new, weight_q, momentum_q, momentum_q_new, weight_q_new,
        momentum_q_h, weight_q_h, out_sems
    )
    for copy in copies:
        copy.wait()


def query_columns(
    which, piece, new, weight, momentum, momentum_new, weight_new, momentum_h, weight_h, sems
):
    wide = momentum_new.shape[1]
    columns = half_at(which, wide)
    moved = momentum_decay * momentum[:, columns] + dot(piece, new[:, :wide], 0, 0)
    momentum_new[...] = moved
    weight_new[...] = weight[:, columns] - step_size * moved
    return [
        load(momentum_new, momentum_h.at[:, columns], sems.at[0]),
        load(weight_new, weight_h.at[:, columns], sems.at[1]),
    ]


def finish_far_kernel(
    count, hat_near, hat_far, mat_q_near, mat_o_near, mat_q_far, mat_o_far,
    new_near, new_far, weight_q, momentum_q, weight_o, momentum_o, norm,
    error_q_in, error_o_in, momentum_q_in, weight_q_in,
    error_q, error_o, momentum_q_h, weight_q_h, new_q_h, new_o_h, momentum_o_h, weight_o_h, norm_h,
    stage_q, stage_o, momentum_q_new, weight_q_new, new_q, new_o, momentum_o_new, weight_o_new,
    pieces_q, pieces_o, sems, out_sems
):
    mine = parity()
    me = lax.axis_index("replica")
    wide_q, wide_o = stage_q.shape[1], stage_o.shape[1]
    size_q = mat_q_near.shape[0]
    size_o = mat_o_near.shape[0]
    new_q[:, half_at(mine, wide_q)] = new_near[:, :wide_q]
    new_q[:, half_at(1 - mine, wide_q)] = new_far[:, :wide_q]
    new_o[:, half_at(mine, wide_o)] = new_near[:, wide_q:]
    new_o[:, half_at(1 - mine, wide_o)] = new_far[:, wide_q:]
    copies = [
        load(new_q, new_q_h, out_sems.at[0]),
        load(new_o, new_o_h, out_sems.at[1]),
        load(norm, norm_h, out_sems.at[2]),
    ]
    copies += error_columns(
        1 - mine, hat_near, 0, mine, mat_q_near, mat_o_near, new_far,
        error_q, error_o, stage_q, stage_o, sems, 0
    )
    piece = piece_of(
        new_near.at[:, wide_q:], new_far.at[:, wide_q:], me, count, weight_o.shape[1], pieces_o
    )
    for which, hat in ((mine, hat_near), (1 - mine, hat_far)):
        rows = half_at(which, size_o)
        moved = momentum_decay * momentum_o[rows] + dot(hat[:, size_q:size_q + size_o], piece, 0, 0)
        momentum_o_new[rows] = moved
        weight_o_new[rows] = weight_o[rows] - step_size * moved
    copies.append(load(momentum_o_new, momentum_o_h, out_sems.at[3]))
    copies.append(load(weight_o_new, weight_o_h, out_sems.at[4]))
    copies += error_columns(
        1 - mine, hat_far, 1, 1 - mine, mat_q_far, mat_o_far, new_far,
        error_q, error_o, stage_q, stage_o, sems, 8
    )
    piece = piece_of(hat_near, hat_far, me, count, weight_q.shape[0], pieces_q)
    copies += query_columns(
        1 - mine, piece, new_far, weight_q, momentum_q, momentum_q_new, weight_q_new,
        momentum_q_h, weight_q_h, out_sems.at[5:7]
    )
    for copy in copies:
        copy.wait()


def finish(count, hat_near, hat_far, mats, new_near, weights, norm):
    mat_q, mat_o = mats[0], mats[1]
    weight_q, _, weight_o, _ = weights
    rank = hat_near.shape[0]
    size_q, size_o = mat_q.shape[0], mat_o.shape[0]
    early = (
        shaped((2 * size_q, mat_q.shape[1]), bf16),
        shaped((2 * size_o, mat_o.shape[1]), bf16),
        shaped(weight_q.shape, f32),
        shaped(weight_q.shape, f32),
    )
    late = (
        shaped((rank, mat_q.shape[1]), bf16),
        shaped((rank, mat_o.shape[1]), bf16),
        shaped(weight_o.shape, f32),
        shaped(weight_o.shape, f32),
    )
    piece_q = (weight_q.shape[0], weight_q.shape[1] // 2)
    stages = [
        pltpu.VMEM((2 * size_q, mat_q.shape[1] // 2), bf16),
        pltpu.VMEM((2 * size_o, mat_o.shape[1] // 2), bf16),
        pltpu.VMEM(piece_q, f32),
        pltpu.VMEM(piece_q, f32),
    ]
    pieces_q = pltpu.VMEM((count // 2, rank, weight_q.shape[0]), f32)
    pieces_o = pltpu.VMEM((count // 2, rank, weight_o.shape[1]), f32)
    moved = 4 * (mat_q.size + mat_o.size)
    mats = [in_vmem(mat) for mat in mats]
    weights = [in_vmem(value) for value in weights]
    new_far = swap_halves(new_near)
    parts = pl.pallas_call(
        functools.partial(finish_near_kernel, count),
        out_shape=early,
        in_specs=[whole] * 9,
        out_specs=(in_place,) * 4,
        scratch_shapes=stages + [
            pieces_q, pltpu.SemaphoreType.DMA((16,)), pltpu.SemaphoreType.DMA((2,))
        ],
        compiler_params=params(12),
        cost_estimate=cost(2 * rank * (mat_q.size + mat_o.size), moved),
        name="finish_near",
    )(hat_near, hat_far, *mats, new_near, *weights[:2])
    return pl.pallas_call(
        functools.partial(finish_far_kernel, count),
        out_shape=early + late + (shaped(norm.shape, f32),),
        in_specs=[whole] * 13 + [in_place] * 4,
        out_specs=(in_place,) * 9,
        scratch_shapes=stages + [pltpu.VMEM(out.shape, out.dtype) for out in late] + [
            pieces_q, pieces_o, pltpu.SemaphoreType.DMA((16,)), pltpu.SemaphoreType.DMA((7,))
        ],
        input_output_aliases={13: 0, 14: 1, 15: 2, 16: 3},
        compiler_params=params(16),
        cost_estimate=cost(2 * rank * (mat_q.size + mat_o.size), moved),
        name="finish_far",
    )(hat_near, hat_far, *mats, new_near, new_far, *weights, norm, *parts)


def swap(value, even, odd):
    replicas, tensors = lax.axis_size("replica"), lax.axis_size("tensor")
    pairs = []
    for replica in range(replicas):
        for tensor in range(tensors):
            target = replica ^ (odd if tensor % 2 else even)
            pairs.append((replica * tensors + tensor, target * tensors + tensor))
    return lax.ppermute(value, ("replica", "tensor"), pairs)


def swap_halves(value):
    return swap(value, 1, lax.axis_size("replica") // 2)


def swap_tensor(value, bit):
    count = lax.axis_size("tensor")
    return lax.ppermute(value, "tensor", [(source, source ^ bit) for source in range(count)])


def exchange(state, bits):
    offsets = [(0, 0)]
    for even, odd in bits:
        offsets += [(first | even, second | odd) for first, second in offsets]
    if len(offsets) == 4:
        offsets = [offsets[place] for place in (0, 1, 3, 2)]
    return [state] + [swap(state, *offset) for offset in offsets[1:]]


def rounds_of(count):
    places = range(1, count.bit_length() - 1)
    bits = [(1 << place, 1 << (place - 1)) for place in places]
    return [bits[place:place + 2] for place in range(0, len(bits), 2)]


def on_device(
    grad_q,
    error_q,
    qfac_q,
    ginv_q,
    weight_q,
    momentum_q,
    grad_o,
    error_o,
    qfac_o,
    ginv_o,
    weight_o,
    momentum_o,
    norm_grads,
):
    replicas = lax.axis_size("replica")
    tensors = lax.axis_size("tensor")
    rank = qfac_q.shape[1]
    half_q = grad_q.shape[0] // 2
    norm_rows = norm_grads.size // lanes
    mat_q_far, mat_o_far, send, mat_q_near, mat_o_near, part, norm = project(
        grad_q, error_q, grad_o, error_o, qfac_q.T, qfac_o.T, norm_grads
    )
    columns = part.shape[1]
    rounds = rounds_of(replicas)
    state = small(
        first_sum_kernel, "first_sum", shaped((rank, columns + lanes), bf16), part, norm, swap_halves(send)
    )
    wide = shaped((rank, columns + 2 * lanes), bf16)
    for bits in rounds[:-1]:
        state = small(
            functools.partial(norm_sum_kernel, columns), "norm_sum", wide, *exchange(state, bits)
        )
    hat_near = small(
        functools.partial(hat_kernel, half_q, columns), "hats", wide,
        ginv_q, ginv_o, *exchange(state, rounds[-1]),
    )
    hat_far = swap_halves(hat_near)
    part_q, part_o = right_near(hat_near, mat_q_near, mat_o_near)
    send, near, norm = right_far(
        hat_far, mat_q_far, mat_o_far, part_q, part_o, hat_near, norm_rows
    )
    state, norm = small(
        near_sum_kernel, "near_sum", (shaped(send.shape, bf16), shaped(norm.shape, f32)),
        near, swap_halves(send), norm, swap_tensor(norm, 1),
    )
    for bits in rounds[:-1]:
        state = small(
            plain_sum_kernel, "plain_sum", shaped(state.shape, bf16), *exchange(state, bits)
        )
    states = exchange(state, rounds[-1])
    new_near, norm = small(
        functools.partial(mean_kernel, replicas, replicas * tensors), "mean",
        (shaped(state.shape, bf16), shaped(norm.shape, f32)),
        norm, swap_tensor(norm, 2), *states,
    )
    (
        error_q_new, error_o_new, momentum_q_new, weight_q_new,
        new_q, new_o, momentum_o_new, weight_o_new, norm_mean,
    ) = finish(
        replicas, hat_near, hat_far,
        (mat_q_near, mat_o_near, mat_q_far, mat_o_far), new_near,
        (weight_q, momentum_q, weight_o, momentum_o), norm,
    )
    return (
        error_q_new,
        new_q.T,
        momentum_q_new,
        weight_q_new,
        error_o_new,
        new_o.T,
        momentum_o_new,
        weight_o_new,
        norm_mean.reshape(-1),
    )


def solution(mesh):
    in_specs = (
        P("replica", "tensor"),
        P("replica", "tensor"),
        P("tensor", None),
        P("tensor", None),
        P("replica", "tensor"),
        P("replica", "tensor"),
        P(("replica", "tensor"), None),
        P(("replica", "tensor"), None),
        P("tensor", None),
        P("tensor", None),
        P("tensor", "replica"),
        P("tensor", "replica"),
        P("replica", "tensor", None),
    )
    out_specs = (
        P("replica", "tensor"),
        P("tensor", None),
        P("replica", "tensor"),
        P("replica", "tensor"),
        P(("replica", "tensor"), None),
        P("tensor", None),
        P("tensor", "replica"),
        P("tensor", "replica"),
        P(),
    )
    return jax.shard_map(
        on_device, mesh=mesh, in_specs=in_specs, out_specs=out_specs, check_vma=False
    )
```
